32 devices in a mesh: seq: 16 (over z, y, core), head: 2 (over x).
Axes of the slice: x: 2, y: 2, z: 4, core: 2. Of those that a mesh axis runs over, the one named last changes fastest.
Arguments:
- query_input: bfloat16 [4096, 2048], P('seq', 'head'), may hold values from -6 to 6
- key_input: bfloat16 [4096, 2048], P('seq', 'head'), may hold values from -6 to 6
- value_input: bfloat16 [4096, 4096], P('seq', 'head'), may hold values from -6 to 6
- kernel_taps: float32 [2, 4, 2048], P(None, None, 'head'), may hold values from -3 to 3
- input_gate: float32 [8, 4096], P('head', 'seq'), may hold values from -6 to 300
- forget_gate: float32 [8, 4096], P('head', 'seq'), may hold values from -0.5 to 16
- request_lengths: int32 [4], replicated, may hold values from 1 to 2048, as said below
- output_weight: bfloat16 [4096, 2048], P('head'), may hold values from -0.09375 to 0.09375
Outputs:
- mixed_out: bfloat16 [4096, 2048], P('seq', 'head')
The draws below stay inside these ranges and needn't reach their ends.
Inputs may be any that keep to these rules, and one draw needn't show every extreme that they name: `request_lengths`: the lengths sum to 4096; the longest request has exactly 2048 tokens.
All inputs are finite; a program needn't handle non-finite values.
Results may differ from the reference program's by a relative error of at most 0.012.
Values may be sent and summed in bfloat16 or wider, within the bound.
No kernel may reach another device: no remote copies, remote signals or barrier semaphores. Data moves between devices by JAX's collectives and lax.ppermute only.
A program may use at most 128 MiB of HBM per device.

```python
import math
import jax
import jax.numpy as jnp
from jax import lax

HEADS = 8
DQK = 256
DV = 512
OUT_COLS = 2048
KCONV = 4
REQS = 4
TOK_DEV = 256
PACKED_TOKENS = 4096


def request_sizes(key):
    base_key = jax.random.fold_in(key, 7001)
    cut_key, order_key = jax.random.split(base_key)
    remaining = PACKED_TOKENS - PACKED_TOKENS // 2
    cut_points = jnp.sort(jax.random.permutation(cut_key, remaining - 1)[:REQS - 2].astype(jnp.int32) + 1)
    edges = jnp.concatenate([jnp.zeros((1,), jnp.int32), cut_points, jnp.full((1,), remaining, jnp.int32)])
    smaller = edges[1:] - edges[:-1]
    sizes_all = jnp.concatenate([jnp.full((1,), PACKED_TOKENS // 2, jnp.int32), smaller])
    return sizes_all[jax.random.permutation(order_key, REQS)].astype(jnp.int32)


def draw_request_lengths(key, part):
    return request_sizes(key)


def draw_input_gate(key, part):
    gate_key = jax.random.fold_in(key, 7002)
    random_keys = jax.random.split(gate_key, 1)
    return 1.5 * jax.random.truncated_normal(random_keys[0], -4.0, 4.0, (HEADS, PACKED_TOKENS), jnp.float32)


def draw_forget_gate(key, part):
    gate_key = jax.random.fold_in(key, 7003)
    random_keys = jax.random.split(gate_key, 7)
    head_order = jax.random.permutation(random_keys[0], HEADS)
    fast_count = jax.random.randint(random_keys[1], (), 2, HEADS - 1)
    token_factor = jnp.exp(jax.random.uniform(random_keys[2], (HEADS, PACKED_TOKENS), jnp.float32, math.log(0.5), math.log(2.0)))
    quick_heads = (head_order < fast_count)[:, None]
    fast_length = jnp.exp(jax.random.uniform(random_keys[3], (HEADS, 1), jnp.float32, math.log(30.0), math.log(50.0)))
    shard_factor = jnp.exp(jax.random.uniform(random_keys[4], (HEADS, PACKED_TOKENS // TOK_DEV), jnp.float32, math.log(0.5), math.log(2.0)))
    shard_factor = jnp.repeat(shard_factor, TOK_DEV, axis=1)
    gradual_decay_rate = 0.2 / (PACKED_TOKENS // 2) * token_factor * shard_factor
    quick_decay_rate = token_factor / fast_length
    spike_position = jax.random.randint(random_keys[5], (2,), 0, PACKED_TOKENS)
    spike_penalty = jax.random.uniform(random_keys[6], (2,), jnp.float32, 0.2, 0.5)
    spike_count = jnp.arange(PACKED_TOKENS)[None, :] == spike_position[:, None]
    spike_probability = jnp.sum(jnp.where(spike_count, -jnp.log1p(-spike_penalty)[:, None], 0.0), axis=0)
    forget_decay_rate = jnp.where(quick_heads, quick_decay_rate, gradual_decay_rate + spike_probability[None, :])
    return -jnp.log(jnp.expm1(forget_decay_rate))


def block_scale(own_key, extent, cuts, low, largest):
    def one(axis_at, parts):
        heights = jax.random.uniform(jax.random.fold_in(jax.random.fold_in(own_key, 6), axis_at), (parts,), jnp.float32, low / len(cuts), largest / len(cuts))
        return jnp.repeat(jnp.exp(heights), extent[axis_at] // parts).reshape((-1,) + (1,) * (len(extent) - axis_at - 1))

    loudness = one(*cuts[0])
    for cut in cuts[1:]:
        loudness = loudness * one(*cut)
    return loudness


def centred(rng, extent, scale, bound, shards=(), kind=jnp.bfloat16):
    drawn = scale * jax.random.normal(rng, extent, jnp.float32)
    if shards:
        drawn = drawn * block_scale(rng, extent, shards, -0.22, 0.18)
    return jnp.clip(drawn, -bound, bound).astype(kind)


def setup_inputs(seed: int = 0) -> dict:
    splits = jax.random.split(jax.random.key(seed), 9)
    query_input = centred(splits[0], (PACKED_TOKENS, HEADS * DQK), 1.0, 6.0, ((0, 16), (1, 2)))
    key_input = centred(splits[1], (PACKED_TOKENS, HEADS * DQK), 1.0, 6.0, ((0, 16), (1, 2)))
    value_input = centred(splits[2], (PACKED_TOKENS, HEADS * DV), 1.0, 6.0, ((0, 16), (1, 2)))
    kernel_taps = centred(splits[3], (2, KCONV, HEADS * DQK), KCONV ** -0.5, 3.0, ((2, 2),), jnp.float32)
    input_gate = draw_input_gate(jax.random.fold_in(splits[8], 71), 0)
    forget_gate = draw_forget_gate(jax.random.fold_in(splits[8], 71), 0)
    request_lengths = draw_request_lengths(jax.random.fold_in(splits[8], 71), 0)
    output_weight = centred(splits[7], (HEADS * DV, OUT_COLS), (HEADS * DV) ** -0.5, 0.09375, ((0, 2),))
    return {"query_input": query_input, "key_input": key_input, "value_input": value_input, "kernel_taps": kernel_taps, "input_gate": input_gate, "forget_gate": forget_gate, "request_lengths": request_lengths, "output_weight": output_weight}


very_negative = -1e+30

def conv_silu(features, kernel_part, segments):
    length = features.shape[0]
    taps = kernel_part.shape[0]
    padded = jnp.concatenate([jnp.zeros((taps - 1, features.shape[1]), features.dtype), features])
    padded_seg = jnp.concatenate([jnp.full((taps - 1,), -1, jnp.int32), segments])
    running = jnp.zeros(features.shape, jnp.float32)
    for shift_by in range(taps):
        piece_rows = padded[taps - 1 - shift_by:taps - 1 - shift_by + length].astype(jnp.float32)
        same_req = (padded_seg[taps - 1 - shift_by:taps - 1 - shift_by + length] == segments)[:, None]
        running = running + jnp.where(same_req, kernel_part[shift_by][None, :] * piece_rows, 0.0)
    return jax.nn.silu(running).astype(jnp.bfloat16)

def block_pass(state, block):
    memory, normal, stabilizer, segment_prev = state
    query_block, key_block, value_block, forget_block, input_block, segment_block = block
    block_len = query_block.shape[0]
    key_scale = 1.0 / math.sqrt(query_block.shape[2])
    cumulative = jnp.cumsum(forget_block, axis=1)
    positions = jnp.arange(block_len, dtype=jnp.int32)
    allowed = (positions[None, :] <= positions[:, None]) & (segment_block[None, :] == segment_block[:, None])
    log_weight = jnp.where(allowed[None], input_block[:, None, :] + cumulative[:, :, None] - cumulative[:, None, :], very_negative)
    linked = segment_block == segment_prev
    carried = jnp.where(linked[None, :], stabilizer[:, None] + cumulative, very_negative)
    row_max = jnp.maximum(lax.optimization_barrier(jnp.max(log_weight, axis=2)), carried)
    query_float = query_block.astype(jnp.float32)
    key_float = key_block.astype(jnp.float32)
    value_float = value_block.astype(jnp.float32)
    scores = jnp.einsum('thd,shd->hts', query_float, key_float, precision=lax.Precision.HIGHEST) * key_scale
    weights = scores * jnp.exp(log_weight - row_max[:, :, None])
    weights_low = lax.optimization_barrier(weights.astype(jnp.bfloat16)).astype(jnp.float32)
    reach_share = jnp.exp(carried - row_max)
    scaled_query = query_float * key_scale
    from_memory = jnp.einsum('thd,hdv->thv', scaled_query, memory, precision=lax.Precision.HIGHEST)
    from_normal = jnp.einsum('thd,hd->ht', scaled_query, normal, precision=lax.Precision.HIGHEST)
    numerator = jnp.einsum('hts,shv->thv', weights_low, value_float, precision=lax.Precision.HIGHEST)
    numerator = numerator + reach_share.T[:, :, None] * from_memory
    denominator = lax.optimization_barrier(jnp.sum(weights, axis=2)) + reach_share * from_normal
    segment_last = segment_block[block_len - 1]
    tail_weight = jnp.where((segment_block == segment_last)[None, :], input_block + cumulative[:, -1:] - cumulative, very_negative)
    tail_carry = jnp.where(segment_prev == segment_last, stabilizer + cumulative[:, -1], very_negative)
    stabilizer_new = jnp.maximum(lax.optimization_barrier(jnp.max(tail_weight, axis=1)), tail_carry)
    factor = jnp.exp(tail_weight - stabilizer_new[:, None])
    weighted_keys = key_float * factor.T[:, :, None]
    keys_low = lax.optimization_barrier(weighted_keys.astype(jnp.bfloat16)).astype(jnp.float32)
    decay_share = jnp.exp(tail_carry - stabilizer_new)
    memory_new = decay_share[:, None, None] * memory + jnp.einsum('shd,shv->hdv', keys_low, value_float, precision=lax.Precision.HIGHEST)
    normal_new = decay_share[:, None] * normal + lax.optimization_barrier(jnp.sum(weighted_keys, axis=0))
    return ((memory_new, normal_new, stabilizer_new, segment_last), (numerator, denominator, row_max))

def reference(query_input, key_input, value_input, kernel_taps, input_gate, forget_gate, request_lengths, output_weight):
    total_rows = query_input.shape[0]
    starts = (jnp.cumsum(request_lengths) - request_lengths).astype(jnp.int32)
    positions = jnp.arange(total_rows, dtype=jnp.int32)
    segments = (lax.optimization_barrier(jnp.sum((starts[None, :] <= positions[:, None]).astype(jnp.int32), axis=1)) - 1).astype(jnp.int32)
    query_conv = conv_silu(query_input, kernel_taps[0], segments)
    key_conv = conv_silu(key_input, kernel_taps[1], segments)
    block_len = min(512, TOK_DEV)
    block_count = total_rows // block_len
    log_forget = jax.nn.log_sigmoid(forget_gate)
    blocks = (query_conv.reshape(block_count, block_len, HEADS, DQK), key_conv.reshape(block_count, block_len, HEADS, DQK), value_input.reshape(block_count, block_len, HEADS, DV), log_forget.reshape(HEADS, block_count, block_len).transpose(1, 0, 2), input_gate.reshape(HEADS, block_count, block_len).transpose(1, 0, 2), segments.reshape(block_count, block_len))
    initial = (jnp.zeros((HEADS, DQK, DV), jnp.float32), jnp.zeros((HEADS, DQK), jnp.float32), jnp.full((HEADS,), very_negative, jnp.float32), jnp.array(-1, jnp.int32))
    _, (numerator, denominator, row_max) = lax.scan(block_pass, initial, blocks)
    floor_value = jnp.maximum(jnp.abs(denominator), 1.0).transpose(0, 2, 1)
    head_out = (numerator / floor_value[..., None]).reshape(total_rows, HEADS * DV).astype(jnp.bfloat16)
    return jnp.dot(head_out, output_weight, preferred_element_type=jnp.float32).astype(jnp.bfloat16)
```

```python
import functools
import math

import jax
import jax.numpy as jnp
from jax import lax
from jax.experimental import pallas as pl
from jax.experimental.pallas import tpu as pltpu
from jax.sharding import PartitionSpec as P

very_negative = -1e30
INFO = 16
TAIL = 16
BF16 = jnp.bfloat16
F32 = jnp.float32


def iota(shape, dim):
    return lax.broadcasted_iota(jnp.int32, shape, dim)


def dot(a, b, contract=((1,), (0,))):
    return lax.dot_general(a, b, (contract, ((), ())), preferred_element_type=F32)


def split3(x):
    high = x.astype(BF16).astype(F32)
    rest = x - high
    mid = rest.astype(BF16).astype(F32)
    return high, mid, (rest - mid).astype(BF16).astype(F32)


def segment_of(lengths_ref, position):
    start = jnp.int32(0)
    count = jnp.zeros_like(position)
    for r in range(lengths_ref.shape[0]):
        count = count + (start <= position).astype(jnp.int32)
        start = start + lengths_ref[r]
    return count - 1


def gate_rows(forget_ref, input_ref, padded):
    heads, length = forget_ref.shape
    padded[...] = jnp.zeros_like(padded)
    padded[0, 0:heads, :] = forget_ref[...]
    padded[1, 0:heads, :] = input_ref[...]
    forget = padded[0]
    log_forget = -(jnp.maximum(-forget, 0.0) + jnp.log1p(jnp.exp(-jnp.abs(forget))))
    upto = jnp.where(iota((length, length), 0) <= iota((length, length), 1), 1.0, 0.0).astype(BF16)
    cumulative = sum(dot(part.astype(BF16), upto) for part in split3(log_forget))
    return padded[1], cumulative


def conv_silu(x_ref, columns, tail, taps_ref, which, same, wide):
    length = x_ref.shape[0]
    taps = taps_ref.shape[1]
    wide[0:8, :] = tail[TAIL - 8 : TAIL]
    wide[8 : 8 + length, :] = x_ref[:, columns].astype(F32)
    total = taps_ref[which, 0:1, columns] * wide[8 : 8 + length, :]
    for lag in range(1, taps):
        total = total + taps_ref[which, lag : lag + 1, columns] * (
            wide[8 - lag : 8 - lag + length, :] * same[lag]
        )
    return (total / (1.0 + jnp.exp(-total))).astype(BF16)


def same_request(lengths_ref, offset, length, taps):
    position = offset + iota((length, 1), 0)
    here = segment_of(lengths_ref, position)
    return here, [
        None if lag == 0 else (segment_of(lengths_ref, position - lag) == here).astype(F32)
        for lag in range(taps)
    ]


def write_info(ref, index, normal, stab, decay):
    n0, n1, n2 = split3(normal)
    s0, s1, s2 = (jnp.broadcast_to(a, (1, 128)) for a in split3(stab))
    d0, d1, d2 = (jnp.broadcast_to(a, (1, 128)) for a in split3(decay))
    row = iota((INFO, 512), 0)
    block = jnp.where(row == 0, jnp.concatenate([n0, n1], axis=1), 0.0)
    block = jnp.where(row == 1, jnp.concatenate([n2, s0, s1], axis=1), block)
    block = jnp.where(row == 2, jnp.concatenate([s2, d0, d1, d2], axis=1), block)
    rows = ref.shape[-2] - INFO
    ref[index + (pl.ds(rows, INFO), slice(None))] = block.astype(BF16)


def read_info(block):
    b = block.astype(F32)
    normal = b[0:1, 0:256] + b[0:1, 256:512] + b[1:2, 0:256]
    stab = b[1:2, 256:257] + b[1:2, 384:385] + b[2:3, 0:1]
    decay = b[2:3, 128:129] + b[2:3, 256:257] + b[2:3, 384:385]
    return normal, stab, decay


def local_kernel(
    lengths_ref, key_ref, tail_ref, taps_ref, value_ref, input_ref, forget_ref,
    conv_ref, keep_ref, send_ref, padded, wide,
):
    length = key_ref.shape[0]
    heads = input_ref.shape[0]
    key_width = key_ref.shape[1] // heads
    value_width = value_ref.shape[1] // heads
    rows = keep_ref.shape[1] - INFO
    place = lax.axis_index("seq")
    core = lax.rem(place, 2)
    offset = place * length
    _, same = same_request(lengths_ref, offset, length, taps_ref.shape[1])
    gate, cumulative = gate_rows(forget_ref, input_ref, padded)
    segment = segment_of(lengths_ref, offset + iota((1, length), 1))
    last = segment_of(lengths_ref, jnp.full((1, 1), offset + length - 1, jnp.int32))
    before = segment_of(lengths_ref, jnp.full((1, 1), offset - 1, jnp.int32))
    total = cumulative[:, length - 1 : length]
    tail_weight = jnp.where(segment == last, gate + total - cumulative, very_negative)
    stab = jnp.max(tail_weight, axis=1, keepdims=True)
    factor = jnp.exp(tail_weight - stab).T
    through = jnp.where(before == last, total, very_negative)
    for h in range(heads):
        columns = slice(h * key_width, (h + 1) * key_width)
        tail = tail_ref[1, :, columns].astype(F32)
        conv = conv_silu(key_ref, columns, tail, taps_ref, 1, same, wide)
        conv_ref[:, columns] = conv
        weighted = conv.astype(F32) * factor[:, h : h + 1]
        normal = jnp.sum(weighted, axis=0, keepdims=True)
        value = value_ref[:, h * value_width : (h + 1) * value_width]
        memory = dot(weighted.astype(BF16), value, ((0,), (0,))).astype(BF16)
        for part in range(key_width // rows):
            piece = h * (key_width // rows) + part
            owner, slot = piece // 4, piece % 4
            content = memory[part * rows : (part + 1) * rows]

            def write(ref, slot=slot, content=content, normal=normal, h=h):
                ref[slot, 0:rows, :] = content
                write_info(ref, (slot,), normal, stab[h : h + 1], through[h : h + 1])

            pl.when(core == owner)(functools.partial(write, keep_ref))
            pl.when(core != owner)(functools.partial(write, send_ref))


def chip_kernel(keep_ref, got_ref, *outs):
    place = lax.axis_index("seq")
    first = lax.rem(place, 2) == 0
    mine = lax.rem(place // 2, 4)
    rows = keep_ref.shape[1] - INFO
    for off, out in enumerate(outs):
        slot = lax.bitwise_xor(mine, off)
        n_a, m_a, d_a = read_info(keep_ref[slot, rows:, :])
        n_b, m_b, d_b = read_info(got_ref[slot, rows:, :])
        m_a = m_a + jnp.where(first, d_b, 0.0)
        m_b = m_b + jnp.where(first, 0.0, d_a)
        m = jnp.maximum(m_a, m_b)
        w_a, w_b = jnp.exp(m_a - m), jnp.exp(m_b - m)
        out[0:rows, :] = (
            w_a * keep_ref[slot, 0:rows, :].astype(F32) + w_b * got_ref[slot, 0:rows, :].astype(F32)
        ).astype(BF16)
        write_info(out, (), w_a * n_a + w_b * n_b, m, d_a + d_b)


def shifted_stab(infos, ranks, upto):
    out = []
    for i, (_, stab, _) in enumerate(infos):
        for j, (_, _, decay) in enumerate(infos):
            if i != j:
                inside = (ranks[j] > ranks[i]) & (ranks[j] < upto)
                stab = stab + jnp.where(inside, decay, 0.0)
        out.append(stab)
    return out


def total_kernel(*refs):
    *states, out = refs
    rows = out.shape[0] - INFO
    mine = lax.rem(lax.axis_index("seq") // 2, 4)
    ranks = [lax.bitwise_xor(mine, off) for off in range(4)]
    infos = [read_info(s[rows:, :]) for s in states]
    stabs = shifted_stab(infos, ranks, 4)
    m = functools.reduce(jnp.maximum, stabs)
    weights = [jnp.exp(s - m) for s in stabs]
    out[0:rows, :] = sum(w * s[0:rows, :].astype(F32) for w, s in zip(weights, states)).astype(BF16)
    write_info(
        out, (), sum(w * i[0] for w, i in zip(weights, infos)), m, sum(i[2] for i in infos)
    )


def round_kernel(bit, first, *refs):
    if first:
        total_ref, got_ref, prefix_out, total_out = refs
    else:
        prefix_ref, total_ref, got_ref, prefix_out, total_out = refs
    rows = total_ref.shape[0] - INFO
    later = lax.rem(lax.shift_right_logical(lax.axis_index("seq"), bit), 2) == 1
    n_t, m_t, d_t = read_info(total_ref[rows:, :])
    n_g, m_g, d_g = read_info(got_ref[rows:, :])
    here, got = total_ref[0:rows, :].astype(F32), got_ref[0:rows, :].astype(F32)
    a_t = m_t + jnp.where(later, 0.0, d_g)
    a_g = m_g + jnp.where(later, d_t, 0.0)
    m = jnp.maximum(a_t, a_g)
    w_t, w_g = jnp.exp(a_t - m), jnp.exp(a_g - m)
    total_out[0:rows, :] = (w_t * here + w_g * got).astype(BF16)
    write_info(total_out, (), w_t * n_t + w_g * n_g, m, d_t + d_g)
    if first:
        n_p, m_p, d_p = jnp.zeros_like(n_g), jnp.full_like(m_g, very_negative), jnp.zeros_like(d_g)
        prefix = jnp.zeros_like(got)
    else:
        n_p, m_p, d_p = read_info(prefix_ref[rows:, :])
        prefix = prefix_ref[0:rows, :].astype(F32)
    a_g = jnp.where(later, m_g + d_p, 2 * very_negative)
    m = jnp.maximum(m_p, a_g)
    w_p = jnp.exp(m_p - m)
    w_g = jnp.where(later, jnp.exp(a_g - m), 0.0)
    prefix_out[0:rows, :] = (w_p * prefix + w_g * got).astype(BF16)
    write_info(prefix_out, (), w_p * n_p + w_g * n_g, m, d_p + jnp.where(later, d_g, 0.0))


def enter_kernel(bit, prefix_ref, *refs):
    states, outs = refs[:4], refs[4:]
    rows = outs[0].shape[0] - INFO
    place = lax.axis_index("seq")
    mine = lax.rem(place // 2, 4)
    ranks = [lax.bitwise_xor(mine, off) for off in range(4)]
    infos = [read_info(s[rows:, :]) for s in states]
    n_p, m_p, _ = read_info(prefix_ref[rows:, :])
    valid = True if bit is None else lax.rem(lax.shift_right_logical(place, bit), 2) == 1
    for off, out in enumerate(outs):
        stabs = shifted_stab(infos, ranks, ranks[off])
        m_in = m_p
        for info, rank in zip(infos, ranks):
            m_in = m_in + jnp.where(rank < ranks[off], info[2], 0.0)
        m_in = jnp.where(valid, m_in, very_negative)
        stabs = [
            jnp.where(rank < ranks[off], s, 2 * very_negative) for s, rank in zip(stabs, ranks)
        ]
        m = functools.reduce(jnp.maximum, stabs, m_in)
        w_in = jnp.where(valid, jnp.exp(m_in - m), 0.0)
        total = w_in * prefix_ref[0:rows, :].astype(F32)
        normal = w_in * n_p
        for i in range(4):
            if i != off:
                w = jnp.where(ranks[i] < ranks[off], jnp.exp(stabs[i] - m), 0.0)
                total = total + w * states[i][0:rows, :].astype(F32)
                normal = normal + w * infos[i][0]
        out[0:rows, :] = total.astype(BF16)
        write_info(out, (), normal, m, jnp.zeros_like(m))


def deliver_kernel(keep_ref, got_ref, *refs):
    enter, (own_ref, other_ref) = refs[:4], refs[4:]
    place = lax.axis_index("seq")
    first = lax.rem(place, 2) == 0
    mine = lax.rem(place // 2, 4)
    rows = keep_ref.shape[1] - INFO

    def fill(same_ref, next_ref, local_ref):
        for off in range(4):
            slot = lax.bitwise_xor(mine, off)
            n_e, m_e, _ = read_info(enter[off][rows:, :])
            n_l, m_l, d_l = read_info(local_ref[slot, rows:, :])
            a_e = m_e + d_l
            m = jnp.maximum(a_e, m_l)
            w_e, w_l = jnp.exp(a_e - m), jnp.exp(m_l - m)
            same_ref[slot] = enter[off][...]
            next_ref[slot, 0:rows, :] = (
                w_e * enter[off][0:rows, :].astype(F32)
                + w_l * local_ref[slot, 0:rows, :].astype(F32)
            ).astype(BF16)
            write_info(next_ref, (slot,), w_e * n_e + w_l * n_l, m, jnp.zeros_like(m))

    pl.when(first)(lambda: fill(own_ref, other_ref, keep_ref))
    pl.when(jnp.logical_not(first))(lambda: fill(other_ref, own_ref, got_ref))


def intra_kernel(
    lengths_ref, query_ref, tail_ref, taps_ref, key_ref, value_ref, input_ref, forget_ref,
    conv_ref, numerator_ref, stats_ref, padded, wide,
):
    length = query_ref.shape[0]
    heads = input_ref.shape[0]
    key_width = query_ref.shape[1] // heads
    value_width = value_ref.shape[1] // heads
    key_scale = 1.0 / math.sqrt(key_width)
    offset = lax.axis_index("seq") * length
    segment, same = same_request(lengths_ref, offset, length, taps_ref.shape[1])
    gate, cumulative = gate_rows(forget_ref, input_ref, padded)
    by_token = cumulative.T
    segment_row = segment_of(lengths_ref, offset + iota((1, length), 1))
    before = segment_of(lengths_ref, jnp.full((1, 1), offset - 1, jnp.int32))
    allowed = (iota((length, length), 1) <= iota((length, length), 0)) & (segment_row == segment)
    lane = iota((length, 128), 1)
    denominators = jnp.ones((length, 128), F32)
    maxima = jnp.zeros((length, 128), F32)
    links = jnp.zeros((length, 128), F32)
    for h in range(heads):
        columns = slice(h * key_width, (h + 1) * key_width)
        tail = tail_ref[0, :, columns].astype(F32)
        conv = conv_silu(query_ref, columns, tail, taps_ref, 0, same, wide)
        conv_ref[:, columns] = conv
        here = by_token[:, h : h + 1]
        log_weight = jnp.where(
            allowed, gate[h : h + 1] - cumulative[h : h + 1] + here, very_negative
        )
        row_max = jnp.max(log_weight, axis=1, keepdims=True)
        scores = dot(conv, key_ref[:, columns], ((1,), (1,))) * key_scale
        weights = scores * jnp.exp(log_weight - row_max)
        value = value_ref[:, h * value_width : (h + 1) * value_width]
        numerator_ref[:, h * value_width : (h + 1) * value_width] = dot(
            weights.astype(BF16), value
        )
        denominators = jnp.where(lane == h, jnp.sum(weights, axis=1, keepdims=True), denominators)
        maxima = jnp.where(lane == h, row_max, maxima)
        links = jnp.where(lane == h, jnp.where(segment == before, here, very_negative), links)
    stats_ref[0] = denominators
    stats_ref[1] = maxima
    stats_ref[2] = links


def weight_copy(weight_ref, held, sem, block, width, chunk):
    start = pl.multiple_of(block * width + chunk * held.shape[1], 128)
    return pltpu.make_async_copy(weight_ref.at[:, pl.ds(start, held.shape[1])], held, sem)


def head_kernel(
    off, chunk, width,
    own_ref, got_ref, query_ref, numerator_ref, stats_ref, weight_ref,
    head_ref, part_ref, memory, info, held, sem,
):
    heads = query_ref.shape[1] // 256
    value_width = numerator_ref.shape[1] // heads
    key_width = query_ref.shape[1] // heads
    key_scale = 1.0 / math.sqrt(key_width)
    rows = own_ref.shape[1] - INFO
    block = lax.bitwise_xor(lax.axis_index("head"), off)
    copy = weight_copy(weight_ref, held, sem, block, width, chunk)
    copy.start()
    core = lax.rem(lax.axis_index("seq"), 2)
    for ref, half in ((own_ref, core), (got_ref, 1 - core)):
        for slot in range(4):
            start = pl.multiple_of((half * 4 + slot) * rows, rows)
            memory[pl.ds(start, rows), :] = ref[slot, 0:rows, :]
            info[half * 4 + slot] = ref[slot, rows:, :]
    for h in range(heads):
        normal, stab, _ = read_info(info[h * key_width // rows])
        query = query_ref[:, h * key_width : (h + 1) * key_width]
        parts = jnp.concatenate([*split3(normal), jnp.zeros((5, key_width), F32)], axis=0)
        from_normal = dot(query, parts.astype(BF16), ((1,), (1,)))
        from_normal = from_normal[:, 0:1] + from_normal[:, 1:2] + from_normal[:, 2:3]
        from_memory = dot(query, memory[h * key_width : (h + 1) * key_width, :])
        denominator = stats_ref[0, :, h : h + 1]
        row_max = stats_ref[1, :, h : h + 1]
        carried = stab + stats_ref[2, :, h : h + 1]
        m = jnp.maximum(row_max, carried)
        w_here = jnp.exp(row_max - m)
        w_in = jnp.exp(carried - m) * key_scale
        denominator = w_here * denominator + w_in * from_normal
        scale = 1.0 / jnp.maximum(jnp.abs(denominator), 1.0)
        columns = slice(h * value_width, (h + 1) * value_width)
        head_ref[:, columns] = (
            (w_here * scale) * numerator_ref[:, columns] + (w_in * scale) * from_memory
        ).astype(BF16)
    copy.wait()
    part_ref[...] = dot(head_ref[...], held[...]).astype(part_ref.dtype)


def project_kernel(off, chunk, width, head_ref, weight_ref, part_ref, held, sem):
    block = lax.bitwise_xor(lax.axis_index("head"), off)
    copy = weight_copy(weight_ref, held, sem, block, width, chunk)
    copy.start()
    copy.wait()
    part_ref[...] = dot(head_ref[...], held[...]).astype(part_ref.dtype)


def call(kernel, out_shape, spaces, scratch, name, flops=0, nbytes=0, limit=24):
    place = {"v": pltpu.VMEM, "s": pltpu.SMEM, "a": pl.ANY}
    outs = jax.tree.map(lambda _: pl.BlockSpec(memory_space=pltpu.VMEM), out_shape)
    return pl.pallas_call(
        kernel,
        out_shape=out_shape,
        in_specs=[pl.BlockSpec(memory_space=place[s]) for s in spaces],
        out_specs=outs,
        scratch_shapes=scratch,
        compiler_params=pltpu.CompilerParams(vmem_limit_bytes=limit << 20),
        cost_estimate=pl.CostEstimate(flops=flops, bytes_accessed=nbytes, transcendentals=0),
        name=name,
    )


def on_device(
    query_input, key_input, value_input, kernel_taps, input_gate, forget_gate, request_lengths,
    output_weight,
):
    seq_count, head_count = lax.axis_size("seq"), lax.axis_size("head")
    length, key_cols = query_input.shape
    heads = input_gate.shape[0]
    value_cols = value_input.shape[1]
    key_width, value_width = key_cols // heads, value_cols // heads
    rows = key_cols // 8
    out_cols = output_weight.shape[1] // head_count
    shape = jax.ShapeDtypeStruct

    def swap(x, off):
        return lax.ppermute(x, "seq", [(i, i ^ off) for i in range(seq_count)])

    tails = jnp.stack([query_input[length - TAIL :], key_input[length - TAIL :]])
    tails = lax.ppermute(tails, "seq", [(i, i + 1) for i in range(seq_count - 1)])

    one = shape((rows + INFO, value_width), BF16)
    four = shape((4, rows + INFO, value_width), BF16)
    gates = [pltpu.VMEM((2, 8, length), F32), pltpu.VMEM((length + 8, key_width), F32)]
    key_conv, keep, send = call(
        local_kernel, (shape(key_input.shape, BF16), four, four), "svvvvvv", gates, "local_state"
    )(request_lengths, key_input, tails, kernel_taps, value_input, input_gate, forget_gate)
    got = swap(send, 1)
    query_conv, numerator, stats = call(
        intra_kernel,
        (
            shape(query_input.shape, BF16),
            shape(value_input.shape, F32),
            shape((3, length, 128), F32),
        ),
        "svvvvvvv", gates, "intra",
    )(
        request_lengths, query_input, tails, kernel_taps, key_conv, value_input, input_gate,
        forget_gate,
    )
    pieces = call(chip_kernel, (one,) * 4, "vv", [], "chip_state")(keep, got)
    states = [pieces[0]] + [swap(pieces[off], 2 * off) for off in (1, 2, 3)]
    total = call(total_kernel, one, "vvvv", [], "group_total")(*states)
    bits = seq_count.bit_length() - 1
    flag = 3
    prefix = swap(total, 8)
    if bits > 4:
        flag = None
        prefix, total = call(
            functools.partial(round_kernel, 3, True), (one, one), "vv", [], "round_state"
        )(total, prefix)
        for bit in range(4, bits):
            prefix, total = call(
                functools.partial(round_kernel, bit, False), (one, one), "vvv", [], "round_state"
            )(prefix, total, swap(total, 1 << bit))
    enter = call(functools.partial(enter_kernel, flag), (one,) * 4, "vvvvv", [], "enter_state")(
        prefix, *states
    )
    enter = [enter[0]] + [swap(enter[off], 2 * off) for off in (1, 2, 3)]
    own, other = call(deliver_kernel, (four, four), "vvvvvv", [], "deliver_state")(
        keep, got, *enter
    )
    other = swap(other, 1)

    chunks = 2 if out_cols % 256 == 0 and head_count == 2 else 1
    piece = out_cols // chunks
    weight_scratch = [
        pltpu.VMEM((value_cols, piece), BF16), pltpu.SemaphoreType.DMA(()),
    ]
    head_out = None
    arrived = []
    for off in range(1, head_count):
        columns = []
        for chunk in range(chunks):
            out = shape((length, piece), BF16)
            if head_out is None:
                head_out, part = call(
                    functools.partial(head_kernel, off, chunk, out_cols),
                    (shape((length, value_cols), BF16), out),
                    "vvvvva",
                    [
                        pltpu.VMEM((key_cols, value_width), BF16),
                        pltpu.VMEM((8, INFO, value_width), BF16),
                    ]
                    + weight_scratch,
                    "head_out",
                )(own, other, query_conv, numerator, stats, output_weight)
            else:
                part = call(
                    functools.partial(project_kernel, off, chunk, out_cols), out, "va",
                    weight_scratch, "project_other",
                )(head_out, output_weight)
            columns.append(
                lax.ppermute(part, "head", [(i, i ^ off) for i in range(head_count)])
            )
        arrived.append(columns)
    mixed = call(
        functools.partial(project_kernel, 0, 0, out_cols), shape((length, out_cols), F32), "va",
        [pltpu.VMEM((value_cols, out_cols), BF16), pltpu.SemaphoreType.DMA(())], "project_own",
    )(head_out, output_weight)
    for columns in arrived:
        mixed = mixed + jnp.concatenate(columns, axis=1).astype(F32)
    return mixed.astype(BF16)


def solution(mesh):
    placed = (
        P("seq", "head"),
        P("seq", "head"),
        P("seq", "head"),
        P(None, None, "head"),
        P("head", "seq"),
        P("head", "seq"),
        P(),
        P("head", None),
    )
    return jax.shard_map(
        on_device, mesh=mesh, in_specs=placed, out_specs=P("seq", "head"), check_vma=False
    )
```

```python
import functools
import math

import jax
import jax.numpy as jnp
from jax import lax
from jax.experimental import pallas as pl
from jax.experimental.pallas import tpu as pltpu
from jax.sharding import PartitionSpec as P

very_negative = -1e30
INFO = 16
TAIL = 16
BF16 = jnp.bfloat16
F32 = jnp.float32


def iota(shape, dim):
    return lax.broadcasted_iota(jnp.int32, shape, dim)


def dot(a, b, contract=((1,), (0,))):
    return lax.dot_general(a, b, (contract, ((), ())), preferred_element_type=F32)


def split3(x):
    high = x.astype(BF16).astype(F32)
    rest = x - high
    mid = rest.astype(BF16).astype(F32)
    return high, mid, (rest - mid).astype(BF16).astype(F32)


def segment_of(lengths_ref, position):
    start = jnp.int32(0)
    count = jnp.zeros_like(position)
    for r in range(lengths_ref.shape[0]):
        count = count + (start <= position).astype(jnp.int32)
        start = start + lengths_ref[r]
    return count - 1


def core_place():
    place = lax.axis_index("seq")
    return lax.rem(place, 2), lax.rem(place // 2, 4)


def start_copies(sems, pairs):
    copies = [pltpu.make_async_copy(a, b, sems.at[i]) for i, (a, b) in enumerate(pairs)]
    for copy in copies:
        copy.start()
    return copies


def by_core(core, own_ref, other_ref, columns, held):
    rows = own_ref.shape[0]
    return [
        (ref.at[:, columns], held.at[pl.ds(pl.multiple_of(half * rows, rows), rows), :])
        for ref, half in ((own_ref, core), (other_ref, 1 - core))
    ]


def gate_rows(core, per_core, gates, raw, picked):
    _, heads, length = gates[0].shape
    for ref, half in ((gates[0], core), (gates[1], 1 - core)):
        for g in range(2):
            raw[g, 0:heads, pl.ds(pl.multiple_of(half * length, length), length)] = ref[g]
    first = core * per_core if heads > 1 else 0
    picked[...] = jnp.zeros_like(picked)
    for g in range(2):
        for i in range(per_core):
            picked[g, i : i + 1, :] = raw[g, pl.ds(first + i, 1), :]
    forget = picked[1]
    log_forget = -(jnp.maximum(-forget, 0.0) + jnp.log1p(jnp.exp(-jnp.abs(forget))))
    upto = jnp.where(iota((length, length), 0) <= iota((length, length), 1), 1.0, 0.0).astype(BF16)
    parts = split3(log_forget)
    sums = [
        sum(dot(part[:, b * length : (b + 1) * length].astype(BF16), upto) for part in parts)
        for b in range(2)
    ]
    cumulative = jnp.concatenate([sums[0], sums[1] + sums[0][:, length - 1 :]], axis=1)
    return picked[0], cumulative


def conv_rows(lengths_ref, offset, start, stop, taps, columns, wide):
    position = offset + start + iota((stop - start, 1), 0)
    here = segment_of(lengths_ref, position)
    total = taps[0:1, columns] * wide[8 + start : 8 + stop, :]
    for lag in range(1, taps.shape[0]):
        same = (segment_of(lengths_ref, position - lag) == here).astype(F32)
        total = total + taps[lag : lag + 1, columns] * (
            wide[8 + start - lag : 8 + stop - lag, :] * same
        )
    return (total / (1.0 + jnp.exp(-total))).astype(BF16)


def write_info(ref, normal, stab, decay):
    lines = [p[:, c : c + 128] for p in split3(normal) for c in range(0, normal.shape[1], 128)]
    lines += [jnp.broadcast_to(p, (1, 128)) for x in (stab, decay) for p in split3(x)]
    row = iota((INFO, 128), 0)
    block = jnp.zeros((INFO, 128), F32)
    for i, line in enumerate(lines):
        block = jnp.where(row == i, line, block)
    ref[ref.shape[0] - INFO :, :] = block.astype(BF16)


def read_info(ref, key_width=256):
    b = ref[ref.shape[0] - INFO :, :].astype(F32)
    k = key_width // 128
    normal = jnp.concatenate(
        [b[i : i + 1] + b[i + k : i + k + 1] + b[i + 2 * k : i + 2 * k + 1] for i in range(k)],
        axis=1,
    )
    sums = [b[i : i + 1] + b[i + 1 : i + 2] + b[i + 2 : i + 3] for i in (3 * k, 3 * k + 3)]
    return normal, sums[0][:, 0:1], sums[1][:, 0:1]


def tail_kernel(query_ref, key_ref, input_ref, forget_ref, out_ref, gate_ref, sems):
    last = query_ref.shape[0] - TAIL
    copies = start_copies(
        sems,
        [
            (ref.at[pl.ds(last, TAIL), :], out_ref.at[i])
            for i, ref in enumerate((query_ref, key_ref))
        ]
        + [(ref, gate_ref.at[i]) for i, ref in enumerate((input_ref, forget_ref))],
    )
    for copy in copies:
        copy.wait()


def local_kernel(
    per_core, lengths_ref, key_ref, key_other, value_ref, value_other,
    gates_ref, gates_other, taps_ref,
    conv_ref, values, gate_ref, taps, key_first, factor_first,
    memory_ref, normal_ref, stab_ref, through_ref,
    keys, raw, picked, wide, sems,
):
    core, _ = core_place()
    length = keys.shape[0]
    key_width = keys.shape[1] // per_core
    value_width = values.shape[1] // per_core
    split = gates_ref.shape[1] > 1
    key_columns = pl.ds(
        pl.multiple_of(core * keys.shape[1], 128) if split else 0, keys.shape[1]
    )
    value_columns = pl.ds(pl.multiple_of(core * values.shape[1], 128), values.shape[1])
    copies = start_copies(
        sems,
        [(taps_ref.at[1, :, key_columns], taps)]
        + by_core(core, key_ref, key_other, key_columns, keys)
        + by_core(core, value_ref, value_other, value_columns, values),
    )
    offset = lax.axis_index("seq") // 2 * length
    for copy in copies[:3]:
        copy.wait()
    gate, cumulative = gate_rows(core, per_core, (gates_ref, gates_other), raw, picked)
    gate_ref[0] = gate
    gate_ref[1] = cumulative
    segment = segment_of(lengths_ref, offset + iota((1, length), 1))
    last = segment_of(lengths_ref, jnp.full((1, 1), offset + length - 1, jnp.int32))
    before = segment_of(lengths_ref, jnp.full((1, 1), offset - 1, jnp.int32))
    total = cumulative[:, length - 1 : length]
    tail_weight = jnp.where(segment == last, gate + total - cumulative, very_negative)
    stab = jnp.max(tail_weight, axis=1, keepdims=True)
    factor = jnp.exp(tail_weight - stab).T
    stab_ref[...] = jnp.broadcast_to(stab, stab_ref.shape)
    through = jnp.where(before == last, total, very_negative)
    through_ref[...] = jnp.broadcast_to(through, through_ref.shape)
    factor_first[...] = factor[0:16]
    key_first[...] = keys[0:16, :]
    normal_ref[...] = jnp.zeros_like(normal_ref)
    weighted_all = []
    step = 128
    for i in range(per_core):
        columns = slice(i * key_width, (i + 1) * key_width)
        wide[0:8, :] = jnp.zeros((8, key_width), F32)
        wide[8:, :] = keys[:, columns].astype(F32)
        normal = jnp.zeros((1, key_width), F32)
        weighted_rows = []
        for start in range(0, length, step):
            conv = conv_rows(lengths_ref, offset, start, start + step, taps, columns, wide)
            conv_ref[start : start + step, columns] = conv
            weight = factor[start : start + step, i : i + 1]
            if start == 0:
                weight = jnp.where(iota((step, 1), 0) >= 8, weight, 0.0)
            weighted = conv.astype(F32) * weight
            normal = normal + jnp.sum(weighted, axis=0, keepdims=True)
            weighted_rows.append(weighted.astype(BF16))
        weighted_all.append(jnp.concatenate(weighted_rows, axis=0))
        normal_ref[i : i + 1, :] = normal
    for copy in copies[3:]:
        copy.wait()
    for i in range(per_core):
        memory_ref[i * key_width : (i + 1) * key_width, :] = dot(
            weighted_all[i], values[:, i * value_width : (i + 1) * value_width], ((0,), (0,))
        )


def pick_tail(core, which, tail_ref, tail_other, columns):
    rows = [ref[which, :, columns].astype(F32) for ref in (tail_ref, tail_other)]
    return jnp.where(core == 0, rows[0], rows[1])[TAIL - 8 :]


def first_kernel(
    per_core, length, lengths_ref, tail_ref, tail_other, taps, key_first, values, factor_first,
    memory_ref, normal_ref, stab_ref, through_ref,
    conv_ref, out0, out1, out2, out3, whole, normals, wide,
):
    core, mine = core_place()
    width = key_first.shape[1]
    key_width = width // per_core
    value_width = values.shape[1] // per_core
    split = tail_ref.shape[2] > width
    tail_columns = pl.ds(pl.multiple_of(core * width, 128) if split else 0, width)
    tail = pick_tail(core, 1, tail_ref, tail_other, tail_columns)
    offset = lax.axis_index("seq") // 2 * length
    normals[...] = jnp.zeros_like(normals)
    for i in range(per_core):
        columns = slice(i * key_width, (i + 1) * key_width)
        wide[0:8, :] = tail[:, columns]
        wide[8:, :] = key_first[:, columns].astype(F32)
        conv = conv_rows(lengths_ref, offset, 0, 16, taps, columns, wide)
        conv_ref[:, columns] = conv
        weight = jnp.where(iota((16, 1), 0) < 8, factor_first[:, i : i + 1], 0.0)
        weighted = conv.astype(F32) * weight
        normals[i : i + 1, :] = normal_ref[i : i + 1, :] + jnp.sum(weighted, axis=0, keepdims=True)
        whole[i * key_width : (i + 1) * key_width, :] = (
            memory_ref[i * key_width : (i + 1) * key_width, :]
            + dot(
                weighted.astype(BF16),
                values[0:16, i * value_width : (i + 1) * value_width],
                ((0,), (0,)),
            )
        ).astype(BF16)
    outs = (out0, out1, out2, out3)
    rows = width // 4
    for off, out in enumerate(outs):
        piece = lax.bitwise_xor(mine, off)
        content = whole[pl.ds(pl.multiple_of(piece * rows, rows), rows), :]
        for j in range(value_width // 128):
            out[j * rows : (j + 1) * rows, :] = content[:, j * 128 : (j + 1) * 128]
        head = piece // (key_width // rows)
        write_info(
            out,
            normals[pl.ds(head, 1), :],
            stab_ref[pl.ds(head, 1), :][:, 0:1],
            through_ref[pl.ds(head, 1), :][:, 0:1],
        )


def shifted_stab(infos, ranks, upto):
    out = []
    for i, (_, stab, _) in enumerate(infos):
        for j, (_, _, decay) in enumerate(infos):
            if i != j:
                inside = (ranks[j] > ranks[i]) & (ranks[j] < upto)
                stab = stab + jnp.where(inside, decay, 0.0)
        out.append(stab)
    return out


def total_kernel(*refs):
    *states, out = refs
    rows = out.shape[0] - INFO
    _, mine = core_place()
    ranks = [lax.bitwise_xor(mine, off) for off in range(4)]
    infos = [read_info(s) for s in states]
    stabs = shifted_stab(infos, ranks, 4)
    m = functools.reduce(jnp.maximum, stabs)
    weights = [jnp.exp(s - m) for s in stabs]
    out[0:rows, :] = sum(w * s[0:rows, :].astype(F32) for w, s in zip(weights, states)).astype(BF16)
    write_info(out, sum(w * i[0] for w, i in zip(weights, infos)), m, sum(i[2] for i in infos))


def is_later(bit):
    return lax.rem(lax.shift_right_logical(lax.axis_index("seq"), bit), 2) == 1


def round_kernel(bit, first, *refs):
    if first:
        total_ref, got_ref, prefix_out, total_out = refs
    else:
        prefix_ref, total_ref, got_ref, prefix_out, total_out = refs
    rows = total_ref.shape[0] - INFO
    later = is_later(bit)
    n_t, m_t, d_t = read_info(total_ref)
    n_g, m_g, d_g = read_info(got_ref)
    here, got = total_ref[0:rows, :].astype(F32), got_ref[0:rows, :].astype(F32)
    a_t = m_t + jnp.where(later, 0.0, d_g)
    a_g = m_g + jnp.where(later, d_t, 0.0)
    m = jnp.maximum(a_t, a_g)
    w_t, w_g = jnp.exp(a_t - m), jnp.exp(a_g - m)
    total_out[0:rows, :] = (w_t * here + w_g * got).astype(BF16)
    write_info(total_out, w_t * n_t + w_g * n_g, m, d_t + d_g)
    if first:
        n_p, m_p, d_p = jnp.zeros_like(n_g), jnp.full_like(m_g, very_negative), jnp.zeros_like(d_g)
        prefix = jnp.zeros_like(got)
    else:
        n_p, m_p, d_p = read_info(prefix_ref)
        prefix = prefix_ref[0:rows, :].astype(F32)
    a_g = jnp.where(later, m_g + d_p, 2 * very_negative)
    m = jnp.maximum(m_p, a_g)
    w_p = jnp.exp(m_p - m)
    w_g = jnp.where(later, jnp.exp(a_g - m), 0.0)
    prefix_out[0:rows, :] = (w_p * prefix + w_g * got).astype(BF16)
    write_info(prefix_out, w_p * n_p + w_g * n_g, m, d_p + jnp.where(later, d_g, 0.0))


def enter_kernel(bit, prefix_ref, *refs):
    states, outs = refs[:4], refs[4:]
    rows = outs[0].shape[0] - INFO
    _, mine = core_place()
    ranks = [lax.bitwise_xor(mine, off) for off in range(4)]
    infos = [read_info(s) for s in states]
    n_p, m_p, _ = read_info(prefix_ref)
    valid = True if bit is None else is_later(bit)
    for off in (1, 2, 3, 0):
        out = outs[off]
        stabs = shifted_stab(infos, ranks, ranks[off])
        m_in = m_p
        for info, rank in zip(infos, ranks):
            m_in = m_in + jnp.where(rank < ranks[off], info[2], 0.0)
        m_in = jnp.where(valid, m_in, very_negative)
        stabs = [
            jnp.where(rank < ranks[off], s, 2 * very_negative) for s, rank in zip(stabs, ranks)
        ]
        m = functools.reduce(jnp.maximum, stabs, m_in)
        w_in = jnp.where(valid, jnp.exp(m_in - m), 0.0)
        total = w_in * prefix_ref[0:rows, :].astype(F32)
        normal = w_in * n_p
        for i in range(4):
            if i != off:
                w = jnp.where(ranks[i] < ranks[off], jnp.exp(stabs[i] - m), 0.0)
                total = total + w * states[i][0:rows, :].astype(F32)
                normal = normal + w * infos[i][0]
        out[0:rows, :] = total.astype(BF16)
        write_info(out, normal, m, jnp.zeros_like(m))


def intra_kernel(
    per_core, lengths_ref, query_ref, query_other, tail_ref, tail_other, taps_ref,
    key_ref, key_first, values, gate_ref,
    conv_ref, numerator_ref, stats_ref, queries, taps, keys, wide, sems,
):
    core, _ = core_place()
    length, width = queries.shape
    key_width = width // per_core
    value_width = values.shape[1] // per_core
    key_scale = 1.0 / math.sqrt(key_width)
    split = tail_ref.shape[2] > width
    columns = pl.ds(pl.multiple_of(core * width, 128) if split else 0, width)
    copies = start_copies(
        sems,
        [(taps_ref.at[0, :, columns], taps)]
        + by_core(core, query_ref, query_other, columns, queries),
    )
    offset = lax.axis_index("seq") // 2 * length
    tail = pick_tail(core, 0, tail_ref, tail_other, columns)
    keys[...] = key_ref[...]
    keys[0:16, :] = key_first[...]
    gate, cumulative = gate_ref[0], gate_ref[1]
    by_token = cumulative.T
    segment = segment_of(lengths_ref, offset + iota((length, 1), 0))
    segment_row = segment_of(lengths_ref, offset + iota((1, length), 1))
    before = segment_of(lengths_ref, jnp.full((1, 1), offset - 1, jnp.int32))
    step = length // 2
    lane = iota((step, 128), 1)
    for copy in copies:
        copy.wait()
    stats = [[jnp.zeros((step, 128), F32)] * 3 for _ in range(2)]
    for i in range(per_core):
        here = slice(i * key_width, (i + 1) * key_width)
        value_columns = slice(i * value_width, (i + 1) * value_width)
        wide[0:8, :] = tail[:, here]
        wide[8:, :] = queries[:, here].astype(F32)
        for start in range(0, length, 128):
            conv_ref[start : start + 128, here] = conv_rows(
                lengths_ref, offset, start, start + 128, taps, here, wide
            )
        for b in range(2):
            rows, stop = slice(b * step, (b + 1) * step), (b + 1) * step
            allowed = segment_row[:, 0:stop] == segment[rows]
            allowed &= iota((step, stop), 1) <= iota((step, stop), 0) + b * step
            total = by_token[rows, i : i + 1]
            log_weight = jnp.where(
                allowed,
                gate[i : i + 1, 0:stop] - cumulative[i : i + 1, 0:stop] + total,
                very_negative,
            )
            row_max = jnp.max(log_weight, axis=1, keepdims=True)
            scores = dot(conv_ref[rows, here], keys[0:stop, here], ((1,), (1,))) * key_scale
            weights = scores * jnp.exp(log_weight - row_max)
            numerator_ref[rows, value_columns] = dot(
                weights.astype(BF16), values[0:stop, value_columns]
            )
            linked = jnp.where(segment[rows] == before, total, very_negative)
            found = (jnp.sum(weights, axis=1, keepdims=True), row_max, linked)
            stats[b] = [jnp.where(lane == i, new, old) for new, old in zip(found, stats[b])]
    for b in range(2):
        for k in range(3):
            stats_ref[k, b * step : (b + 1) * step, :] = stats[b][k]


def head_kernel(
    per_core, own_ref, got1, got2, got3, query_ref, numerator_ref, stats_ref,
    keep_ref, send_ref, memory, info,
):
    core, mine = core_place()
    key_width = query_ref.shape[1] // per_core
    value_width = numerator_ref.shape[1] // per_core
    key_scale = 1.0 / math.sqrt(key_width)
    rows = query_ref.shape[1] // 4
    step = keep_ref.shape[0]
    for off, ref in enumerate((own_ref, got1, got2, got3)):
        piece = lax.bitwise_xor(mine, off)
        start = pl.multiple_of(piece * rows, rows)
        for j in range(value_width // 128):
            memory[pl.ds(start, rows), j * 128 : (j + 1) * 128] = ref[j * rows : (j + 1) * rows, :]
        info[piece] = ref[ref.shape[0] - INFO :, :]
    row, lane = iota((128, key_width), 0), iota((1, 128), 1)
    stabs = jnp.full((1, 128), very_negative, F32)
    parts = []
    for i in range(per_core):
        normal, stab, _ = read_info(info.at[i * key_width // rows], key_width)
        stabs = jnp.where(lane == i, stab, stabs)
        block = jnp.zeros((128, key_width), F32)
        for k, part in enumerate(split3(normal)):
            block = jnp.where(row == 8 * k + i, part, block)
        parts.append(block.astype(BF16))
    for b in range(2):
        span = slice(b * step, (b + 1) * step)
        queries = [
            query_ref[span, i * key_width : (i + 1) * key_width] for i in range(per_core)
        ]
        from_normal = sum(dot(q, p, ((1,), (1,))) for q, p in zip(queries, parts))
        from_normal = (
            from_normal
            + pltpu.roll(from_normal, 128 - 8, 1)
            + pltpu.roll(from_normal, 128 - 16, 1)
        )
        row_max = stats_ref[1, span, :]
        carried = stabs + stats_ref[2, span, :]
        m = jnp.maximum(row_max, carried)
        w_here = jnp.exp(row_max - m)
        w_in = jnp.exp(carried - m) * key_scale
        denominator = w_here * stats_ref[0, span, :] + w_in * from_normal
        scale = 1.0 / jnp.maximum(jnp.abs(denominator), 1.0)
        w_here, w_in = w_here * scale, w_in * scale
        for i in range(per_core):
            columns = slice(i * value_width, (i + 1) * value_width)
            from_memory = dot(queries[i], memory[i * key_width : (i + 1) * key_width, :])
            head_out = (
                w_here[:, i : i + 1] * numerator_ref[span, columns]
                + w_in[:, i : i + 1] * from_memory
            ).astype(BF16)

            def write(ref, columns=columns, head_out=head_out):
                ref[:, columns] = head_out

            pl.when(core == b)(functools.partial(write, keep_ref))
            pl.when(core != b)(functools.partial(write, send_ref))


def weight_part(weight_ref, half, rows, start, width):
    return weight_ref[
        pl.ds(pl.multiple_of(half * rows, 128), rows), pl.ds(pl.multiple_of(start, 128), width)
    ]


def keep_kernel(off, head_ref, weight_ref, part_ref):
    core, _ = core_place()
    rows, width = head_ref.shape[1], part_ref.shape[1]
    start = lax.bitwise_xor(lax.axis_index("head"), off) * width
    part_ref[...] = dot(head_ref[...], weight_part(weight_ref, core, rows, start, width))


def send_kernel(off, chunk, head_ref, weight_ref, kept_ref, part_ref):
    core, _ = core_place()
    rows, piece, width = head_ref.shape[1], part_ref.shape[1], kept_ref.shape[1]
    start = lax.bitwise_xor(lax.axis_index("head"), off) * width + chunk * piece
    part_ref[...] = (
        dot(head_ref[...], weight_part(weight_ref, 1 - core, rows, start, piece))
        + kept_ref[:, chunk * piece : (chunk + 1) * piece]
    ).astype(part_ref.dtype)


def own_kernel(keep_ref, got_ref, weight_ref, part_ref):
    core, _ = core_place()
    rows, width = keep_ref.shape[1], part_ref.shape[1]
    start = lax.axis_index("head") * width
    part_ref[...] = dot(
        keep_ref[...], weight_part(weight_ref, core, rows, start, width)
    ) + dot(got_ref[...], weight_part(weight_ref, 1 - core, rows, start, width))


def sum_kernel(chunks, own_ref, *refs):
    *arrived, out_ref = refs
    width = out_ref.shape[1] // chunks
    for c in range(chunks):
        columns = slice(c * width, (c + 1) * width)
        total = own_ref[:, columns]
        for ref in arrived[c::chunks]:
            total = total + ref[...].astype(F32)
        out_ref[:, columns] = total.astype(out_ref.dtype)


def call(kernel, out_shape, spaces, scratch, name, flops=0, nbytes=0, limit=24):
    place = {"v": pltpu.VMEM, "s": pltpu.SMEM, "a": pl.ANY, "h": pl.ANY}
    outs = jax.tree.map(lambda _: pl.BlockSpec(memory_space=pltpu.VMEM), out_shape)
    inner = pl.pallas_call(
        kernel,
        out_shape=out_shape,
        in_specs=[pl.BlockSpec(memory_space=place[s]) for s in spaces],
        out_specs=outs,
        scratch_shapes=scratch,
        compiler_params=pltpu.CompilerParams(vmem_limit_bytes=limit << 20),
        cost_estimate=pl.CostEstimate(flops=flops, bytes_accessed=nbytes, transcendentals=0),
        name=name,
    )

    def run(*args):
        return inner(
            *(
                pltpu.with_memory_space_constraint(x, pltpu.HBM) if s in "hs" else x
                for s, x in zip(spaces, args, strict=True)
            )
        )

    return run


def on_device(
    query_input, key_input, value_input, kernel_taps, input_gate, forget_gate, request_lengths,
    output_weight,
):
    seq_count, head_count = lax.axis_size("seq"), lax.axis_size("head")
    length, key_cols = query_input.shape
    heads = input_gate.shape[0]
    value_cols = value_input.shape[1]
    out_cols = output_weight.shape[1] // head_count
    chip_length = 2 * length
    key_width = key_cols // heads
    per_core = max(1, heads // 2)
    part_keys, part_values = per_core * key_width, value_cols // 2
    value_width = part_values // per_core
    lags = kernel_taps.shape[1]
    rows = part_keys // 4

    def shape(dims, dtype=F32):
        return jax.ShapeDtypeStruct(dims, dtype)

    def swap(x, off):
        return lax.ppermute(x, "seq", [(i, i ^ off) for i in range(seq_count)])

    key_other, value_other = swap(key_input, 1), swap(value_input, 1)
    tails, gates = call(
        tail_kernel, (shape((2, TAIL, key_cols), BF16), shape((2, heads, length))), "hhhh",
        [pltpu.SemaphoreType.DMA((4,))], "tails",
    )(query_input, key_input, input_gate, forget_gate)
    gates_other = swap(gates, 1)
    tails = lax.ppermute(tails, "seq", [(i, i + 1) for i in range(seq_count - 1)])
    tails_other = swap(tails, 1)
    query_other = swap(lax.optimization_barrier((query_input, tails))[0], 1)

    one = shape((rows * value_width // 128 + INFO, 128), BF16)
    key_conv, values, gate_sums, taps, key_first, factor, memory, normal, stab, through = call(
        functools.partial(local_kernel, per_core),
        (
            shape((chip_length, part_keys), BF16),
            shape((chip_length, part_values), BF16),
            shape((2, 8, chip_length)),
            shape((lags, part_keys)),
            shape((16, part_keys), BF16),
            shape((16, 8)),
            shape((part_keys, value_width)),
            shape((8, key_width)),
            shape((8, 128)),
            shape((8, 128)),
        ),
        "shahavvh",
        [pltpu.VMEM((chip_length, part_keys), BF16)]
        + [
            pltpu.VMEM((2, max(8, heads), chip_length), F32),
            pltpu.VMEM((2, 8, chip_length), F32),
            pltpu.VMEM((chip_length + 8, key_width), F32),
            pltpu.SemaphoreType.DMA((5,)),
        ],
        "local_state",
        flops=1 << 30,
    )(
        request_lengths, key_input, key_other, value_input, value_other, gates, gates_other,
        kernel_taps,
    )
    conv_first, *pieces = call(
        functools.partial(first_kernel, per_core, chip_length),
        (shape((16, part_keys), BF16),) + (one,) * 4,
        "s" + "v" * 10,
        [
            pltpu.VMEM((part_keys, value_width), BF16),
            pltpu.VMEM((8, key_width), F32),
            pltpu.VMEM((24, key_width), F32),
        ],
        "first_tokens",
    )(
        request_lengths, tails, tails_other, taps, key_first, values, factor, memory, normal, stab,
        through,
    )
    states = [pieces[0]] + [swap(pieces[off], 2 * off) for off in (1, 2, 3)]
    inside = call(
        functools.partial(intra_kernel, per_core),
        (
            shape((chip_length, part_keys), BF16),
            shape((chip_length, part_values)),
            shape((3, chip_length, 128)),
        ),
        "shavvhvvvv",
        [
            pltpu.VMEM((chip_length, part_keys), BF16),
            pltpu.VMEM((lags, part_keys), F32),
            pltpu.VMEM((chip_length, part_keys), BF16),
            pltpu.VMEM((chip_length + 8, key_width), F32),
            pltpu.SemaphoreType.DMA((3,)),
        ],
        "intra",
        flops=4 << 30,
    )(
        request_lengths, query_input, query_other, tails, tails_other, kernel_taps, key_conv,
        conv_first, values, gate_sums,
    )
    states, inside = lax.optimization_barrier((states, inside))
    total = call(total_kernel, one, "vvvv", [], "group_total")(*states)
    bits = seq_count.bit_length() - 1
    flag = 3
    prefix = swap(total, 8)
    if bits > 4:
        flag = None
        prefix, total = call(
            functools.partial(round_kernel, 3, True), (one, one), "vv", [], "round_state"
        )(total, prefix)
        for bit in range(4, bits):
            prefix, total = call(
                functools.partial(round_kernel, bit, False), (one, one), "vvv", [], "round_state"
            )(prefix, total, swap(total, 1 << bit))
    enter = call(functools.partial(enter_kernel, flag), (one,) * 4, "vvvvv", [], "enter_state")(
        prefix, *states
    )
    enter = [enter[0]] + [swap(enter[off], 2 * off) for off in (1, 2, 3)]
    half = shape((length, part_values), BF16)
    keep, send = call(
        functools.partial(head_kernel, per_core), (half, half), "v" * 7,
        [
            pltpu.VMEM((part_keys, value_width), BF16),
            pltpu.VMEM((4, INFO, 128), BF16),
        ],
        "head_out",
    )(*enter, *inside)
    got = swap(send, 1)

    chunks = 2 if head_count == 2 and out_cols % 256 == 0 else 1
    piece = out_cols // chunks
    arrived = []
    for off in range(1, head_count):
        kept = call(
            functools.partial(keep_kernel, off), shape((length, out_cols)), "vv", [],
            "project_kept", flops=2 << 30,
        )(keep, output_weight)
        columns = [
            call(
                functools.partial(send_kernel, off, chunk), shape((length, piece), BF16), "vvv",
                [], "project_other",
            )(got, output_weight, kept)
            for chunk in range(chunks)
        ]
        arrived.append(
            [lax.ppermute(c, "head", [(i, i ^ off) for i in range(head_count)]) for c in columns]
        )
    mixed = call(
        own_kernel, shape((length, out_cols)), "vvv", [], "project_own", flops=4 << 30
    )(keep, got, output_weight)
    return call(
        functools.partial(sum_kernel, chunks), shape((length, out_cols), BF16),
        "v" * (1 + chunks * len(arrived)), [], "mixed_out",
    )(mixed, *(c for columns in arrived for c in columns))


def solution(mesh):
    placed = (
        P("seq", "head"),
        P("seq", "head"),
        P("seq", "head"),
        P(None, None, "head"),
        P("head", "seq"),
        P("head", "seq"),
        P(),
        P("head", None),
    )
    return jax.shard_map(
        on_device, mesh=mesh, in_specs=placed, out_specs=P("seq", "head"), check_vma=False
    )
```

```python
import functools
import math

import jax
import jax.numpy as jnp
from jax import lax
from jax.experimental import pallas as pl
from jax.experimental.pallas import tpu as pltpu
from jax.sharding import PartitionSpec as P

very_negative = -1e30
FIRST = 3
INFO = 16
TAIL = 16
BF16 = jnp.bfloat16
F32 = jnp.float32


def iota(shape, dim):
    return lax.broadcasted_iota(jnp.int32, shape, dim)


def dot(a, b, contract=((1,), (0,))):
    return lax.dot_general(a, b, (contract, ((), ())), preferred_element_type=F32)


def split3(x):
    high = x.astype(BF16).astype(F32)
    rest = x - high
    mid = rest.astype(BF16).astype(F32)
    return high, mid, (rest - mid).astype(BF16).astype(F32)


def segment_of(lengths_ref, position):
    start = jnp.int32(0)
    count = jnp.zeros_like(position)
    for r in range(lengths_ref.shape[0]):
        count = count + (start <= position).astype(jnp.int32)
        start = start + lengths_ref[r]
    return count - 1


def core_place():
    place = lax.axis_index("seq")
    return lax.rem(place, 2), lax.rem(place // 2, 4)


def piece_of(mine, off):
    piece = lax.bitwise_xor(mine, off)
    if lax.axis_size("seq") == 16:
        piece = lax.bitwise_xor(piece, lax.axis_index("seq") // 8 * 2)
    return piece


def start_copies(sems, pairs):
    copies = [pltpu.make_async_copy(a, b, sems.at[i]) for i, (a, b) in enumerate(pairs)]
    for copy in copies:
        copy.start()
    return copies


def by_core(core, own_ref, other_ref, columns, held):
    rows = own_ref.shape[0]
    return [
        (ref.at[:, columns], held.at[pl.ds(pl.multiple_of(half * rows, rows), rows), :])
        for ref, half in ((own_ref, core), (other_ref, 1 - core))
    ]


def gate_rows(core, per_core, gates, raw, picked):
    _, heads, length = gates[0].shape
    for ref, half in ((gates[0], core), (gates[1], 1 - core)):
        for g in range(2):
            raw[g, 0:heads, pl.ds(pl.multiple_of(half * length, length), length)] = ref[g]
    first = core * per_core if heads > 1 else 0
    picked[...] = jnp.zeros_like(picked)
    for g in range(2):
        for i in range(per_core):
            picked[g, i : i + 1, :] = raw[g, pl.ds(first + i, 1), :]
    forget = picked[1]
    log_forget = -(jnp.maximum(-forget, 0.0) + jnp.log1p(jnp.exp(-jnp.abs(forget))))
    upto = jnp.where(iota((length, length), 0) <= iota((length, length), 1), 1.0, 0.0).astype(BF16)
    parts = split3(log_forget)
    sums = [
        sum(dot(part[:, b * length : (b + 1) * length].astype(BF16), upto) for part in parts)
        for b in range(2)
    ]
    cumulative = jnp.concatenate([sums[0], sums[1] + sums[0][:, length - 1 :]], axis=1)
    return picked[0], cumulative


def same_request(lengths_ref, offset, length):
    position = offset + iota((length, 128), 0)
    lag = iota((length, 128), 1)
    here = segment_of(lengths_ref, position)
    return (segment_of(lengths_ref, position - lag) == here).astype(F32)


def conv_rows(same, start, stop, taps, columns, wide):
    total = taps[0:1, columns] * wide[8 + start : 8 + stop, :]
    for lag in range(1, taps.shape[0]):
        total = total + taps[lag : lag + 1, columns] * (
            wide[8 + start - lag : 8 + stop - lag, :] * same[start:stop, lag : lag + 1]
        )
    return (0.5 * total * (1.0 + jnp.tanh(0.5 * total))).astype(BF16)


def write_info(ref, normal, stab, decay):
    lines = [p[:, c : c + 128] for p in split3(normal) for c in range(0, normal.shape[1], 128)]
    lines += [jnp.broadcast_to(p, (1, 128)) for x in (stab, decay) for p in split3(x)]
    row = iota((INFO, 128), 0)
    block = jnp.zeros((INFO, 128), F32)
    for i, line in enumerate(lines):
        block = jnp.where(row == i, line, block)
    ref[ref.shape[0] - INFO :, :] = block.astype(BF16)


def read_info(ref, key_width=256):
    b = ref[ref.shape[0] - INFO :, :].astype(F32)
    k = key_width // 128
    normal = jnp.concatenate(
        [b[i : i + 1] + b[i + k : i + k + 1] + b[i + 2 * k : i + 2 * k + 1] for i in range(k)],
        axis=1,
    )
    sums = [b[i : i + 1] + b[i + 1 : i + 2] + b[i + 2 : i + 3] for i in (3 * k, 3 * k + 3)]
    return normal, sums[0][:, 0:1], sums[1][:, 0:1]


def tail_kernel(query_ref, key_ref, input_ref, forget_ref, out_ref, gate_ref, sems):
    last = query_ref.shape[0] - TAIL
    copies = start_copies(
        sems,
        [
            (ref.at[pl.ds(last, TAIL), :], out_ref.at[i])
            for i, ref in enumerate((query_ref, key_ref))
        ]
        + [(ref, gate_ref.at[i]) for i, ref in enumerate((input_ref, forget_ref))],
    )
    for copy in copies:
        copy.wait()


def chip_kernel(
    per_core, lengths_ref, key_ref, key_other, value_ref, value_other, gates_ref, gates_other,
    taps_ref,
    conv_ref, values, gate_ref, taps, key_first, levels_first, out0, out1, out2, out3,
    keys, raw, picked, wide, weighted_ref, whole, normals, levels, sems,
):
    core, mine = core_place()
    length, width = keys.shape
    key_width = width // per_core
    value_width = values.shape[1] // per_core
    split = gates_ref.shape[1] > 1
    key_columns = pl.ds(pl.multiple_of(core * width, 128) if split else 0, width)
    value_columns = pl.ds(pl.multiple_of(core * values.shape[1], 128), values.shape[1])
    copies = start_copies(
        sems,
        [(taps_ref.at[1, :, key_columns], taps)]
        + by_core(core, key_ref, key_other, key_columns, keys)
        + by_core(core, value_ref, value_other, value_columns, values),
    )
    offset = lax.axis_index("seq") // 2 * length
    gate, cumulative = gate_rows(core, per_core, (gates_ref, gates_other), raw, picked)
    gate_ref[0] = gate
    gate_ref[1] = cumulative
    segment = segment_of(lengths_ref, offset + iota((1, length), 1))
    last = segment_of(lengths_ref, jnp.full((1, 1), offset + length - 1, jnp.int32))
    before = segment_of(lengths_ref, jnp.full((1, 1), offset - 1, jnp.int32))
    total = cumulative[:, length - 1 : length]
    tail_weight = jnp.where(segment == last, gate + total - cumulative, very_negative)
    stab = jnp.max(tail_weight, axis=1, keepdims=True)
    factor = jnp.exp(tail_weight - stab).T
    levels[0] = jnp.broadcast_to(stab, (8, 128))
    through = jnp.where(before == last, total, very_negative)
    levels[1] = jnp.broadcast_to(through, (8, 128))
    levels_first[0] = tail_weight[:, 0:128]
    levels_first[1] = levels[1]
    same = same_request(lengths_ref, offset, length)
    normals[...] = jnp.zeros_like(normals)
    for copy in copies[:3]:
        copy.wait()
    key_first[...] = keys[0:16, :]
    step = 128
    for i in range(per_core):
        columns = slice(i * key_width, (i + 1) * key_width)
        wide[0:8, :] = jnp.zeros((8, key_width), F32)
        wide[8:, :] = keys[:, columns].astype(F32)
        normal = jnp.zeros((1, key_width), F32)
        for start in range(0, length, step):
            conv = conv_rows(same, start, start + step, taps, columns, wide)
            conv_ref[start : start + step, columns] = conv
            weight = factor[start : start + step, i : i + 1]
            if start == 0:
                weight = jnp.where(iota((step, 1), 0) >= FIRST, weight, 0.0)
            weighted = conv.astype(F32) * weight
            normal = normal + jnp.sum(weighted, axis=0, keepdims=True)
            weighted_ref[start : start + step, columns] = weighted.astype(BF16)
        normals[i : i + 1, :] = normal
    for copy in copies[3:]:
        copy.wait()
    for i in range(per_core):
        columns = slice(i * key_width, (i + 1) * key_width)
        whole[columns, :] = dot(
            weighted_ref[:, columns],
            values[:, i * value_width : (i + 1) * value_width],
            ((0,), (0,)),
        ).astype(BF16)
    rows = width // 4
    for off, out in enumerate((out0, out1, out2, out3)):
        piece = piece_of(mine, off)
        content = whole[pl.ds(pl.multiple_of(piece * rows, rows), rows), :]
        for j in range(value_width // 128):
            out[j * rows : (j + 1) * rows, :] = content[:, j * 128 : (j + 1) * 128]
        head = piece // (key_width // rows)
        write_info(
            out,
            normals[pl.ds(head, 1), :],
            levels[0, pl.ds(head, 1), :][:, 0:1],
            levels[1, pl.ds(head, 1), :][:, 0:1],
        )


def pick_tail(core, which, tail_ref, tail_other, columns):
    rows = [ref[which, :, columns].astype(F32) for ref in (tail_ref, tail_other)]
    return jnp.where(core == 0, rows[0], rows[1])[TAIL - 8 :]


def first_kernel(
    per_core, length, lengths_ref, tail_ref, tail_other, taps, key_first, values, levels_first,
    conv_ref, out_ref, rows_ref, wide,
):
    core, _ = core_place()
    width = key_first.shape[1]
    key_width = width // per_core
    split = tail_ref.shape[2] > width
    tail_columns = pl.ds(pl.multiple_of(core * width, 128) if split else 0, width)
    tail = pick_tail(core, 1, tail_ref, tail_other, tail_columns)
    offset = lax.axis_index("seq") // 2 * length
    same = same_request(lengths_ref, offset, 16)
    for i in range(per_core):
        columns = slice(i * key_width, (i + 1) * key_width)
        wide[0:8, :] = tail[:, columns]
        wide[8:, :] = key_first[:, columns].astype(F32)
        conv_ref[:, columns] = conv_rows(same, 0, 16, taps, columns, wide)
    rows_ref[...] = jnp.zeros_like(rows_ref)
    keys, first = conv_ref[...].astype(F32), values[0:16, :].astype(F32)
    at = 0
    for block in (keys, first):
        for j in range(block.shape[1] // 128):
            rows_ref[at : at + FIRST, :] = block[0:FIRST, j * 128 : (j + 1) * 128]
            at += FIRST
    for k in range(2):
        for part in split3(levels_first[k]):
            rows_ref[at : at + per_core, :] = part[0:per_core]
            at += per_core
    out_ref[0] = rows_ref[...].astype(BF16)


def join_kernel(first_ref, second_ref, out_ref):
    count = first_ref.shape[0]
    out_ref[0:count] = first_ref[...]
    out_ref[count:] = second_ref[...]


def gathered_kernel(
    per_core, key_width, offsets, near_ref, far_ref, keys_ref, values_ref, levels_ref,
    key_rows, value_rows,
):
    half = near_ref.shape[0]
    me = lax.axis_index("seq") // 2
    value_width = values_ref.shape[1]
    count = 2 * half * FIRST
    key_blocks, value_blocks = key_width // 128, value_width // 128
    base = FIRST * per_core * (key_blocks + value_blocks)
    ends, decays = [], []
    for g in range(2 * half):
        rows = (near_ref[g] if g < half else far_ref[g - half]).astype(F32)
        for i in range(per_core):
            at = i * count + g * FIRST
            for j in range(key_blocks):
                source = FIRST * (i * key_blocks + j)
                key_rows[at : at + FIRST, j * 128 : (j + 1) * 128] = rows[source : source + FIRST]
            for j in range(value_blocks):
                source = FIRST * (per_core * key_blocks + i * value_blocks + j)
                value_rows[at : at + FIRST, j * 128 : (j + 1) * 128] = rows[source : source + FIRST]
        levels = [
            sum(
                rows[base + (3 * k + p) * per_core : base + (3 * k + p + 1) * per_core]
                for p in range(3)
            )
            for k in range(2)
        ]
        ends.append(levels[0])
        decays.append(levels[1][:, 0:1])
    keys_ref[...] = key_rows[...].astype(BF16)
    values_ref[...] = value_rows[...].astype(BF16)
    chips = [lax.bitwise_xor(me, off) for off in offsets]
    square = iota((FIRST, 128), 0) == iota((FIRST, 128), 1)
    for g in range(2 * half):
        since = sum(
            jnp.where((chips[k] > chips[g]) & (chips[k] < me), decays[k], 0.0)
            for k in range(2 * half)
            if k != g
        )
        here = jnp.where(chips[g] < me, ends[g] + since, 2 * very_negative)
        for i in range(per_core):
            column = jnp.sum(jnp.where(square, here[i : i + 1], 0.0), axis=1, keepdims=True)
            at = i * count + g * FIRST
            levels_ref[at : at + FIRST, :] = jnp.broadcast_to(column, (FIRST, 128))


def shifted_stab(infos, ranks, upto):
    out = []
    for i, (_, stab, _) in enumerate(infos):
        for j, (_, _, decay) in enumerate(infos):
            if i != j:
                inside = (ranks[j] > ranks[i]) & (ranks[j] < upto)
                stab = stab + jnp.where(inside, decay, 0.0)
        out.append(stab)
    return out


def total_kernel(*refs):
    *states, out = refs
    rows = out.shape[0] - INFO
    _, mine = core_place()
    ranks = [lax.bitwise_xor(mine, off) for off in range(4)]
    infos = [read_info(s) for s in states]
    stabs = shifted_stab(infos, ranks, 4)
    m = functools.reduce(jnp.maximum, stabs)
    weights = [jnp.exp(s - m) for s in stabs]
    out[0:rows, :] = sum(w * s[0:rows, :].astype(F32) for w, s in zip(weights, states)).astype(BF16)
    write_info(out, sum(w * i[0] for w, i in zip(weights, infos)), m, sum(i[2] for i in infos))


def is_later(bit):
    return lax.rem(lax.shift_right_logical(lax.axis_index("seq"), bit), 2) == 1


def round_kernel(bit, first, *refs):
    if first:
        total_ref, got_ref, prefix_out, total_out = refs
    else:
        prefix_ref, total_ref, got_ref, prefix_out, total_out = refs
    rows = total_ref.shape[0] - INFO
    later = is_later(bit)
    n_t, m_t, d_t = read_info(total_ref)
    n_g, m_g, d_g = read_info(got_ref)
    here, got = total_ref[0:rows, :].astype(F32), got_ref[0:rows, :].astype(F32)
    a_t = m_t + jnp.where(later, 0.0, d_g)
    a_g = m_g + jnp.where(later, d_t, 0.0)
    m = jnp.maximum(a_t, a_g)
    w_t, w_g = jnp.exp(a_t - m), jnp.exp(a_g - m)
    total_out[0:rows, :] = (w_t * here + w_g * got).astype(BF16)
    write_info(total_out, w_t * n_t + w_g * n_g, m, d_t + d_g)
    if first:
        n_p, m_p, d_p = jnp.zeros_like(n_g), jnp.full_like(m_g, very_negative), jnp.zeros_like(d_g)
        prefix = jnp.zeros_like(got)
    else:
        n_p, m_p, d_p = read_info(prefix_ref)
        prefix = prefix_ref[0:rows, :].astype(F32)
    a_g = jnp.where(later, m_g + d_p, 2 * very_negative)
    m = jnp.maximum(m_p, a_g)
    w_p = jnp.exp(m_p - m)
    w_g = jnp.where(later, jnp.exp(a_g - m), 0.0)
    prefix_out[0:rows, :] = (w_p * prefix + w_g * got).astype(BF16)
    write_info(prefix_out, w_p * n_p + w_g * n_g, m, d_p + jnp.where(later, d_g, 0.0))


def enter_kernel(bit, prefix_ref, *refs):
    states, outs = refs[:4], refs[4:]
    rows = outs[0].shape[0] - INFO
    _, mine = core_place()
    ranks = [lax.bitwise_xor(mine, off) for off in range(4)]
    infos = [read_info(s) for s in states]
    n_p, m_p, _ = read_info(prefix_ref)
    valid = True if bit is None else is_later(bit)
    for off in (1, 2, 3, 0):
        out = outs[off]
        stabs = shifted_stab(infos, ranks, ranks[off])
        m_in = m_p
        for info, rank in zip(infos, ranks):
            m_in = m_in + jnp.where(rank < ranks[off], info[2], 0.0)
        m_in = jnp.where(valid, m_in, very_negative)
        stabs = [
            jnp.where(rank < ranks[off], s, 2 * very_negative) for s, rank in zip(stabs, ranks)
        ]
        m = functools.reduce(jnp.maximum, stabs, m_in)
        w_in = jnp.where(valid, jnp.exp(m_in - m), 0.0)
        total = w_in * prefix_ref[0:rows, :].astype(F32)
        normal = w_in * n_p
        for i in range(4):
            if i != off:
                w = jnp.where(ranks[i] < ranks[off], jnp.exp(stabs[i] - m), 0.0)
                total = total + w * states[i][0:rows, :].astype(F32)
                normal = normal + w * infos[i][0]
        out[0:rows, :] = total.astype(BF16)
        write_info(out, normal, m, jnp.zeros_like(m))


def query_kernel(
    per_core, lengths_ref, query_ref, query_other, tail_ref, tail_other, taps_ref,
    conv_ref, queries, taps, wide, sems,
):
    core, _ = core_place()
    length, width = queries.shape
    key_width = width // per_core
    split = tail_ref.shape[2] > width
    columns = pl.ds(pl.multiple_of(core * width, 128) if split else 0, width)
    copies = start_copies(
        sems,
        [(taps_ref.at[0, :, columns], taps)]
        + by_core(core, query_ref, query_other, columns, queries),
    )
    offset = lax.axis_index("seq") // 2 * length
    tail = pick_tail(core, 0, tail_ref, tail_other, columns)
    same = same_request(lengths_ref, offset, length)
    for copy in copies:
        copy.wait()
    for i in range(per_core):
        here = slice(i * key_width, (i + 1) * key_width)
        wide[0:8, :] = tail[:, here]
        wide[8:, :] = queries[:, here].astype(F32)
        for start in range(0, length, 128):
            conv_ref[start : start + 128, here] = conv_rows(
                same, start, start + 128, taps, here, wide
            )


def intra_kernel(
    per_core, lengths_ref, query_ref, key_ref, key_first, values, gate_ref,
    numerator_ref, stats_ref, keys,
):
    length, width = query_ref.shape
    key_width = width // per_core
    value_width = values.shape[1] // per_core
    key_scale = 1.0 / math.sqrt(key_width)
    offset = lax.axis_index("seq") // 2 * length
    keys[...] = key_ref[...]
    keys[0:16, :] = key_first[...]
    gate, cumulative = gate_ref[0], gate_ref[1]
    by_token = cumulative.T
    segment = segment_of(lengths_ref, offset + iota((length, 1), 0))
    segment_row = segment_of(lengths_ref, offset + iota((1, length), 1))
    before = segment_of(lengths_ref, jnp.full((1, 1), offset - 1, jnp.int32))
    step = length // 2
    lane = iota((step, 128), 1)
    stats = [[jnp.zeros((step, 128), F32)] * 3 for _ in range(2)]
    for i in range(per_core):
        here = slice(i * key_width, (i + 1) * key_width)
        value_columns = slice(i * value_width, (i + 1) * value_width)
        for b in range(2):
            rows, stop = slice(b * step, (b + 1) * step), (b + 1) * step
            allowed = segment_row[:, 0:stop] == segment[rows]
            allowed &= iota((step, stop), 1) <= iota((step, stop), 0) + b * step
            total = by_token[rows, i : i + 1]
            log_weight = jnp.where(
                allowed,
                gate[i : i + 1, 0:stop] - cumulative[i : i + 1, 0:stop] + total,
                very_negative,
            )
            row_max = jnp.max(log_weight, axis=1, keepdims=True)
            scores = dot(query_ref[rows, here], keys[0:stop, here], ((1,), (1,))) * key_scale
            weights = scores * jnp.exp(log_weight - row_max)
            numerator_ref[rows, value_columns] = dot(
                weights.astype(BF16), values[0:stop, value_columns]
            )
            linked = jnp.where(segment[rows] == before, total, very_negative)
            found = (jnp.sum(weights, axis=1, keepdims=True), row_max, linked)
            stats[b] = [jnp.where(lane == i, new, old) for new, old in zip(found, stats[b])]
    for b in range(2):
        for k in range(3):
            stats_ref[k, b * step : (b + 1) * step, :] = stats[b][k]


def head_kernel(
    per_core, own_ref, got1, got2, got3, keys_ref, values_ref, levels_ref,
    query_ref, numerator_ref, stats_ref, keep_ref, send_ref, memory, info,
):
    core, mine = core_place()
    key_width = query_ref.shape[1] // per_core
    value_width = numerator_ref.shape[1] // per_core
    key_scale = 1.0 / math.sqrt(key_width)
    rows = query_ref.shape[1] // 4
    step = keep_ref.shape[0]
    for off, ref in enumerate((own_ref, got1, got2, got3)):
        piece = piece_of(mine, off)
        start = pl.multiple_of(piece * rows, rows)
        for j in range(value_width // 128):
            memory[pl.ds(start, rows), j * 128 : (j + 1) * 128] = ref[j * rows : (j + 1) * rows, :]
        info[piece] = ref[ref.shape[0] - INFO :, :]
    count = keys_ref.shape[0] // per_core
    row, lane = iota((128, key_width), 0), iota((1, 128), 1)
    stabs = jnp.full((1, 128), very_negative, F32)
    parts = []
    for i in range(per_core):
        normal, stab, _ = read_info(info.at[i * key_width // rows], key_width)
        here = slice(i * key_width, (i + 1) * key_width)
        extra = slice(i * count, (i + 1) * count)
        weighted = keys_ref[extra, :].astype(F32) * jnp.exp(levels_ref[extra, 0:1] - stab)
        normal = normal + jnp.sum(weighted, axis=0, keepdims=True)
        memory[here, :] = (
            memory[here, :].astype(F32)
            + dot(weighted.astype(BF16), values_ref[extra, :], ((0,), (0,)))
        ).astype(BF16)
        stabs = jnp.where(lane == i, stab, stabs)
        block = jnp.zeros((128, key_width), F32)
        for k, part in enumerate(split3(normal)):
            block = jnp.where(row == 8 * k + i, part, block)
        parts.append(block.astype(BF16))
    for b in range(2):
        span = slice(b * step, (b + 1) * step)
        queries = [
            query_ref[span, i * key_width : (i + 1) * key_width] for i in range(per_core)
        ]
        from_normal = sum(dot(q, p, ((1,), (1,))) for q, p in zip(queries, parts))
        from_normal = (
            from_normal
            + pltpu.roll(from_normal, 128 - 8, 1)
            + pltpu.roll(from_normal, 128 - 16, 1)
        )
        row_max = stats_ref[1, span, :]
        carried = stabs + stats_ref[2, span, :]
        m = jnp.maximum(row_max, carried)
        w_here = jnp.exp(row_max - m)
        w_in = jnp.exp(carried - m) * key_scale
        denominator = w_here * stats_ref[0, span, :] + w_in * from_normal
        scale = 1.0 / jnp.maximum(jnp.abs(denominator), 1.0)
        w_here, w_in = w_here * scale, w_in * scale
        for i in range(per_core):
            columns = slice(i * value_width, (i + 1) * value_width)
            from_memory = dot(queries[i], memory[i * key_width : (i + 1) * key_width, :])
            head_out = (
                w_here[:, i : i + 1] * numerator_ref[span, columns]
                + w_in[:, i : i + 1] * from_memory
            ).astype(BF16)

            def write(ref, columns=columns, head_out=head_out):
                ref[:, columns] = head_out

            pl.when(core == b)(functools.partial(write, keep_ref))
            pl.when(core != b)(functools.partial(write, send_ref))


def weight_part(weight_ref, half, rows, start, width):
    return weight_ref[
        pl.ds(pl.multiple_of(half * rows, 128), rows), pl.ds(pl.multiple_of(start, 128), width)
    ]


def keep_kernel(off, head_ref, weight_ref, part_ref):
    core, _ = core_place()
    rows, width = head_ref.shape[1], part_ref.shape[1]
    start = lax.bitwise_xor(lax.axis_index("head"), off) * width
    part_ref[...] = dot(head_ref[...], weight_part(weight_ref, core, rows, start, width))


def send_kernel(off, chunk, head_ref, weight_ref, kept_ref, part_ref):
    core, _ = core_place()
    rows, piece, width = head_ref.shape[1], part_ref.shape[1], kept_ref.shape[1]
    start = lax.bitwise_xor(lax.axis_index("head"), off) * width + chunk * piece
    part_ref[...] = (
        dot(head_ref[...], weight_part(weight_ref, 1 - core, rows, start, piece))
        + kept_ref[:, chunk * piece : (chunk + 1) * piece]
    ).astype(part_ref.dtype)


def own_kernel(keep_ref, got_ref, weight_ref, part_ref):
    core, _ = core_place()
    rows, width = keep_ref.shape[1], part_ref.shape[1]
    start = lax.axis_index("head") * width
    part_ref[...] = dot(
        keep_ref[...], weight_part(weight_ref, core, rows, start, width)
    ) + dot(got_ref[...], weight_part(weight_ref, 1 - core, rows, start, width))


def sum_kernel(chunks, own_ref, *refs):
    *arrived, out_ref, held, sems = refs
    width = own_ref.shape[1] // chunks
    parts = sems.shape[0]
    step = own_ref.shape[0] // parts
    copies = []
    for part in range(parts):
        rows = slice(part * step, (part + 1) * step)
        for c in range(chunks):
            columns = slice(c * width, (c + 1) * width)
            total = own_ref[rows, columns]
            for ref in arrived[c::chunks]:
                total = total + ref[rows, :].astype(F32)
            held[rows, columns] = total.astype(held.dtype)
        copies.append(
            pltpu.make_async_copy(
                held.at[pl.ds(part * step, step), :],
                out_ref.at[pl.ds(part * step, step), :],
                sems.at[part],
            )
        )
        copies[-1].start()
    for copy in copies:
        copy.wait()


def call(kernel, out_shape, spaces, scratch, name, flops=0, nbytes=0, limit=24, out=pltpu.VMEM):
    place = {"v": pltpu.VMEM, "s": pltpu.SMEM, "a": pl.ANY, "h": pl.ANY}
    outs = jax.tree.map(lambda _: pl.BlockSpec(memory_space=out), out_shape)
    inner = pl.pallas_call(
        kernel,
        out_shape=out_shape,
        in_specs=[pl.BlockSpec(memory_space=place[s]) for s in spaces],
        out_specs=outs,
        scratch_shapes=scratch,
        compiler_params=pltpu.CompilerParams(vmem_limit_bytes=limit << 20),
        cost_estimate=pl.CostEstimate(flops=flops, bytes_accessed=nbytes, transcendentals=0),
        name=name,
    )

    def run(*args):
        return inner(
            *(
                pltpu.with_memory_space_constraint(x, pltpu.HBM) if s in "hs" else x
                for s, x in zip(spaces, args, strict=True)
            )
        )

    return run


def on_device(
    query_input, key_input, value_input, kernel_taps, input_gate, forget_gate, request_lengths,
    output_weight,
):
    seq_count, head_count = lax.axis_size("seq"), lax.axis_size("head")
    length, key_cols = query_input.shape
    heads = input_gate.shape[0]
    value_cols = value_input.shape[1]
    out_cols = output_weight.shape[1] // head_count
    chip_length = 2 * length
    key_width = key_cols // heads
    per_core = max(1, heads // 2)
    part_keys, part_values = per_core * key_width, value_cols // 2
    value_width = part_values // per_core
    lags = kernel_taps.shape[1]
    rows = part_keys // 4

    def shape(dims, dtype=F32):
        return jax.ShapeDtypeStruct(dims, dtype)

    def swap(x, off):
        return lax.ppermute(x, "seq", [(i, i ^ off) for i in range(seq_count)])

    key_other, value_other = swap(key_input, 1), swap(value_input, 1)
    tails, gates = call(
        tail_kernel, (shape((2, TAIL, key_cols), BF16), shape((2, heads, length))), "hhhh",
        [pltpu.SemaphoreType.DMA((4,))], "tails",
    )(query_input, key_input, input_gate, forget_gate)
    gates_other = swap(gates, 1)
    query_after, gates = lax.optimization_barrier((query_input, gates))
    query_other = swap(query_after, 1)
    tails = lax.ppermute(tails, "seq", [(i, i + 1) for i in range(seq_count - 1)])

    one = shape((rows * value_width // 128 + INFO, 128), BF16)
    key_conv, values, gate_sums, taps, key_first, levels, *pieces = call(
        functools.partial(chip_kernel, per_core),
        (
            shape((chip_length, part_keys), BF16),
            shape((chip_length, part_values), BF16),
            shape((2, 8, chip_length)),
            shape((lags, part_keys)),
            shape((16, part_keys), BF16),
            shape((2, 8, 128)),
        )
        + (one,) * 4,
        "shahavvh",
        [
            pltpu.VMEM((chip_length, part_keys), BF16),
            pltpu.VMEM((2, max(8, heads), chip_length), F32),
            pltpu.VMEM((2, 8, chip_length), F32),
            pltpu.VMEM((chip_length + 8, key_width), F32),
            pltpu.VMEM((chip_length, part_keys), BF16),
            pltpu.VMEM((part_keys, value_width), BF16),
            pltpu.VMEM((8, key_width), F32),
            pltpu.VMEM((2, 8, 128), F32),
            pltpu.SemaphoreType.DMA((5,)),
        ],
        "chip_state",
        flops=1 << 30,
    )(
        request_lengths, key_input, key_other, value_input, value_other, gates, gates_other,
        kernel_taps,
    )
    states = [pieces[0]] + [swap(pieces[off], 2 * off) for off in (1, 2, 3)]

    tails, key_first = lax.optimization_barrier((tails, key_first))
    tails_other = swap(tails, 1)
    count = FIRST * seq_count // 2
    lines = per_core * (FIRST * (key_width + value_width) // 128 + 6)
    lines = -(-lines // 16) * 16
    conv_first, message = call(
        functools.partial(first_kernel, per_core, chip_length),
        (shape((16, part_keys), BF16), shape((1, lines, 128), BF16)),
        "s" + "v" * 6,
        [pltpu.VMEM((lines, 128), F32), pltpu.VMEM((24, key_width), F32)],
        "first_tokens",
    )(request_lengths, tails, tails_other, taps, key_first, values, levels)
    bits = seq_count.bit_length() - 1
    steps = [4, 2, 8] if bits == 4 else [1 << b for b in range(1, bits)]
    near, far, offsets = message, swap(message, steps[0]), [0, steps[0] // 2]
    query_conv = call(
        functools.partial(query_kernel, per_core), shape((chip_length, part_keys), BF16),
        "shavvh",
        [
            pltpu.VMEM((chip_length, part_keys), BF16),
            pltpu.VMEM((lags, part_keys), F32),
            pltpu.VMEM((chip_length + 8, key_width), F32),
            pltpu.SemaphoreType.DMA((3,)),
        ],
        "query_conv",
        flops=1 << 30,
    )(request_lengths, query_after, query_other, tails, tails_other, kernel_taps)
    states, query_conv, far = lax.optimization_barrier((states, query_conv, far))
    total = call(total_kernel, one, "vvvv", [], "group_total")(*states)
    flag = 3
    prefix = swap(total, 12 if bits == 4 else 8)
    near, far, total = lax.optimization_barrier((near, far, total))
    for step in steps[1:]:
        near = call(
            join_kernel, shape((2 * near.shape[0], lines, 128), BF16), "vv", [], "join"
        )(near, far)
        far = swap(near, step)
        offsets = offsets + [off ^ (step // 2) for off in offsets]
    if bits > 4:
        flag = None
        prefix, total = call(
            functools.partial(round_kernel, 3, True), (one, one), "vv", [], "round_state"
        )(total, prefix)
        for bit in range(4, bits):
            prefix, total = call(
                functools.partial(round_kernel, bit, False), (one, one), "vvv", [], "round_state"
            )(prefix, total, swap(total, 1 << bit))
    enter = call(functools.partial(enter_kernel, flag), (one,) * 4, "vvvvv", [], "enter_state")(
        prefix, *states
    )
    gate_sums, near, *enter = lax.optimization_barrier((gate_sums, near, *enter))
    enter = [enter[0]] + [swap(enter[off], 2 * off) for off in (1, 2, 3)]
    extras = call(
        functools.partial(gathered_kernel, per_core, key_width, tuple(offsets)),
        (
            shape((per_core * count, key_width), BF16),
            shape((per_core * count, value_width), BF16),
            shape((per_core * count, 128)),
        ),
        "vv",
        [
            pltpu.VMEM((per_core * count, key_width), F32),
            pltpu.VMEM((per_core * count, value_width), F32),
        ],
        "gathered_first",
    )(near, far)
    inside = call(
        functools.partial(intra_kernel, per_core),
        (shape((chip_length, part_values)), shape((3, chip_length, 128))),
        "svvvvv",
        [pltpu.VMEM((chip_length, part_keys), BF16)],
        "intra",
        flops=4 << 30,
    )(request_lengths, query_conv, key_conv, conv_first, values, gate_sums)
    half = shape((length, part_values), BF16)
    keep, send = call(
        functools.partial(head_kernel, per_core), (half, half), "v" * 10,
        [
            pltpu.VMEM((part_keys, value_width), BF16),
            pltpu.VMEM((4, INFO, 128), BF16),
        ],
        "head_out",
    )(*enter, *extras, query_conv, *inside)
    got = swap(send, 1)

    chunks = 2 if head_count == 2 and out_cols % 256 == 0 else 1
    piece = out_cols // chunks
    arrived = []
    for off in range(1, head_count):
        kept = call(
            functools.partial(keep_kernel, off), shape((length, out_cols)), "vv", [],
            "project_kept", flops=2 << 30,
        )(keep, output_weight)
        columns = [
            call(
                functools.partial(send_kernel, off, chunk), shape((length, piece), BF16), "vvv",
                [], "project_other",
            )(got, output_weight, kept)
            for chunk in range(chunks)
        ]
        arrived.append(
            [lax.ppermute(c, "head", [(i, i ^ off) for i in range(head_count)]) for c in columns]
        )
    mixed = call(
        own_kernel, shape((length, out_cols)), "vvv", [], "project_own", flops=4 << 30
    )(keep, got, output_weight)
    return call(
        functools.partial(sum_kernel, chunks), shape((length, out_cols), BF16),
        "v" * (1 + chunks * len(arrived)),
        [pltpu.VMEM((length, out_cols), BF16), pltpu.SemaphoreType.DMA((4,))],
        "mixed_out", out=pl.ANY,
    )(mixed, *(c for columns in arrived for c in columns))


def solution(mesh):
    placed = (
        P("seq", "head"),
        P("seq", "head"),
        P("seq", "head"),
        P(None, None, "head"),
        P("head", "seq"),
        P("head", "seq"),
        P(),
        P("head", None),
    )
    return jax.shard_map(
        on_device, mesh=mesh, in_specs=placed, out_specs=P("seq", "head"), check_vma=False
    )
```

```python
import functools
import math

import jax
import jax.numpy as jnp
from jax import lax
from jax.experimental import pallas as pl
from jax.experimental.pallas import tpu as pltpu
from jax.sharding import PartitionSpec as P

very_negative = -1e30
FIRST = 3
INFO = 16
TAIL = 16
BF16 = jnp.bfloat16
F32 = jnp.float32


def iota(shape, dim):
    return lax.broadcasted_iota(jnp.int32, shape, dim)


def dot(a, b, contract=((1,), (0,))):
    return lax.dot_general(a, b, (contract, ((), ())), preferred_element_type=F32)


def split3(x):
    high = x.astype(BF16).astype(F32)
    rest = x - high
    mid = rest.astype(BF16).astype(F32)
    return high, mid, (rest - mid).astype(BF16).astype(F32)


def segment_of(lengths_ref, position):
    start = jnp.int32(0)
    count = jnp.zeros_like(position)
    for r in range(lengths_ref.shape[0]):
        count = count + (start <= position).astype(jnp.int32)
        start = start + lengths_ref[r]
    return count - 1


def core_place():
    place = lax.axis_index("seq")
    return lax.rem(place, 2), lax.rem(place // 2, 4)


def piece_of(mine, off):
    piece = lax.bitwise_xor(mine, off)
    if lax.axis_size("seq") == 16:
        piece = lax.bitwise_xor(piece, lax.axis_index("seq") // 8 * 2)
    return piece


def start_copies(sems, pairs):
    copies = [pltpu.make_async_copy(a, b, sems.at[i]) for i, (a, b) in enumerate(pairs)]
    for copy in copies:
        copy.start()
    return copies


def by_core(core, own_ref, other_ref, columns, held):
    rows = own_ref.shape[0]
    return [
        (ref.at[:, columns], held.at[pl.ds(pl.multiple_of(half * rows, rows), rows), :])
        for ref, half in ((own_ref, core), (other_ref, 1 - core))
    ]


def gate_rows(core, per_core, gates, raw, picked):
    _, heads, length = gates[0].shape
    for ref, half in ((gates[0], core), (gates[1], 1 - core)):
        for g in range(2):
            raw[g, 0:heads, pl.ds(pl.multiple_of(half * length, length), length)] = ref[g]
    first = core * per_core if heads > 1 else 0
    picked[...] = jnp.zeros_like(picked)
    for g in range(2):
        for i in range(per_core):
            picked[g, i : i + 1, :] = raw[g, pl.ds(first + i, 1), :]
    forget = picked[1]
    log_forget = -(jnp.maximum(-forget, 0.0) + jnp.log1p(jnp.exp(-jnp.abs(forget))))
    upto = jnp.where(iota((length, length), 0) <= iota((length, length), 1), 1.0, 0.0).astype(BF16)
    parts = split3(log_forget)
    sums = [
        sum(dot(part[:, b * length : (b + 1) * length].astype(BF16), upto) for part in parts)
        for b in range(2)
    ]
    cumulative = jnp.concatenate([sums[0], sums[1] + sums[0][:, length - 1 :]], axis=1)
    return picked[0], cumulative


def same_request(lengths_ref, position):
    lag = iota((position.shape[0], 128), 1)
    here = segment_of(lengths_ref, position)
    return (segment_of(lengths_ref, position - lag) == here).astype(F32)


def conv_rows(same, start, stop, taps, columns, wide):
    total = taps[0:1, columns] * wide[8 + start : 8 + stop, :]
    for lag in range(1, taps.shape[0]):
        total = total + taps[lag : lag + 1, columns] * (
            wide[8 + start - lag : 8 + stop - lag, :] * same[start:stop, lag : lag + 1]
        )
    return (0.5 * total * (1.0 + jnp.tanh(0.5 * total))).astype(BF16)


def write_info(ref, normal, stab, decay):
    lines = [p[:, c : c + 128] for p in split3(normal) for c in range(0, normal.shape[1], 128)]
    lines += [jnp.broadcast_to(p, (1, 128)) for x in (stab, decay) for p in split3(x)]
    row = iota((INFO, 128), 0)
    block = jnp.zeros((INFO, 128), F32)
    for i, line in enumerate(lines):
        block = jnp.where(row == i, line, block)
    ref[ref.shape[0] - INFO :, :] = block.astype(BF16)


def read_info(ref, key_width=256):
    b = ref[ref.shape[0] - INFO :, :].astype(F32)
    k = key_width // 128
    normal = jnp.concatenate(
        [b[i : i + 1] + b[i + k : i + k + 1] + b[i + 2 * k : i + 2 * k + 1] for i in range(k)],
        axis=1,
    )
    sums = [b[i : i + 1] + b[i + 1 : i + 2] + b[i + 2 : i + 3] for i in (3 * k, 3 * k + 3)]
    return normal, sums[0][:, 0:1], sums[1][:, 0:1]


def gates_kernel(input_ref, forget_ref, gate_ref, sems):
    copies = start_copies(
        sems, [(ref, gate_ref.at[i]) for i, ref in enumerate((input_ref, forget_ref))]
    )
    for copy in copies:
        copy.wait()


def chip_kernel(
    per_core, lengths_ref, key_ref, key_other, value_ref, value_other, gates_ref, gates_other,
    taps_ref,
    conv_ref, values, gate_ref, taps, key_edge, levels_first, out0, out1, out2, out3,
    keys, raw, picked, wide, weighted_ref, whole, normals, levels, sems,
):
    core, mine = core_place()
    length, width = keys.shape
    key_width = width // per_core
    value_width = values.shape[1] // per_core
    split = gates_ref.shape[1] > 1
    key_columns = pl.ds(pl.multiple_of(core * width, 128) if split else 0, width)
    value_columns = pl.ds(pl.multiple_of(core * values.shape[1], 128), values.shape[1])
    copies = start_copies(
        sems,
        [(taps_ref.at[1, :, key_columns], taps)]
        + by_core(core, key_ref, key_other, key_columns, keys)
        + by_core(core, value_ref, value_other, value_columns, values),
    )
    offset = lax.axis_index("seq") // 2 * length
    gate, cumulative = gate_rows(core, per_core, (gates_ref, gates_other), raw, picked)
    gate_ref[0] = gate
    gate_ref[1] = cumulative
    segment = segment_of(lengths_ref, offset + iota((1, length), 1))
    last = segment_of(lengths_ref, jnp.full((1, 1), offset + length - 1, jnp.int32))
    before = segment_of(lengths_ref, jnp.full((1, 1), offset - 1, jnp.int32))
    total = cumulative[:, length - 1 : length]
    tail_weight = jnp.where(segment == last, gate + total - cumulative, very_negative)
    stab = jnp.max(tail_weight, axis=1, keepdims=True)
    factor = jnp.exp(tail_weight - stab).T
    levels[0] = jnp.broadcast_to(stab, (8, 128))
    through = jnp.where(before == last, total, very_negative)
    levels[1] = jnp.broadcast_to(through, (8, 128))
    levels_first[0] = tail_weight[:, 0:128]
    levels_first[1] = levels[1]
    same = same_request(lengths_ref, offset + iota((length, 128), 0))
    normals[...] = jnp.zeros_like(normals)
    for copy in copies[:3]:
        copy.wait()
    key_edge[0] = keys[0:16, :]
    key_edge[1] = keys[length - 16 :, :]
    step = 128
    for i in range(per_core):
        columns = slice(i * key_width, (i + 1) * key_width)
        wide[0:8, :] = jnp.zeros((8, key_width), F32)
        wide[8:, :] = keys[:, columns].astype(F32)
        normal = jnp.zeros((1, key_width), F32)
        for start in range(0, length, step):
            conv = conv_rows(same, start, start + step, taps, columns, wide)
            conv_ref[start : start + step, columns] = conv
            weight = factor[start : start + step, i : i + 1]
            if start == 0:
                weight = jnp.where(iota((step, 1), 0) >= FIRST, weight, 0.0)
            weighted = conv.astype(F32) * weight
            normal = normal + jnp.sum(weighted, axis=0, keepdims=True)
            weighted_ref[start : start + step, columns] = weighted.astype(BF16)
        normals[i : i + 1, :] = normal
    for copy in copies[3:]:
        copy.wait()
    for i in range(per_core):
        columns = slice(i * key_width, (i + 1) * key_width)
        whole[columns, :] = dot(
            weighted_ref[:, columns],
            values[:, i * value_width : (i + 1) * value_width],
            ((0,), (0,)),
        ).astype(BF16)
    rows = width // 4
    for off, out in enumerate((out0, out1, out2, out3)):
        piece = piece_of(mine, off)
        content = whole[pl.ds(pl.multiple_of(piece * rows, rows), rows), :]
        for j in range(value_width // 128):
            out[j * rows : (j + 1) * rows, :] = content[:, j * 128 : (j + 1) * 128]
        head = piece // (key_width // rows)
        write_info(
            out,
            normals[pl.ds(head, 1), :],
            levels[0, pl.ds(head, 1), :][:, 0:1],
            levels[1, pl.ds(head, 1), :][:, 0:1],
        )


def message_kernel(
    per_core, query_ref, query_other, key_edge, values, levels_first, out_ref, rows_ref, tail, sems
):
    core, _ = core_place()
    width = key_edge.shape[2]
    split = query_ref.shape[1] > width
    columns = pl.ds(pl.multiple_of(core * width, 128) if split else 0, width)
    last = pl.ds(query_ref.shape[0] - 16, 16)
    for ref, here in ((query_ref, core == 1), (query_other, core == 0)):

        def fetch(ref=ref):
            copy = pltpu.make_async_copy(ref.at[last, columns], tail, sems.at[0])
            copy.start()
            copy.wait()

        pl.when(here)(fetch)
    rows_ref[...] = jnp.zeros_like(rows_ref)
    at = 0
    for block in (
        key_edge[0].astype(F32)[0:FIRST],
        values[0:16, :].astype(F32)[0:FIRST],
        key_edge[1].astype(F32)[16 - FIRST :],
        tail[...].astype(F32)[16 - FIRST :],
    ):
        for j in range(block.shape[1] // 128):
            rows_ref[at : at + FIRST, :] = block[:, j * 128 : (j + 1) * 128]
            at += FIRST
    lane, span = iota((1, 128), 1), 64 // per_core
    line = jnp.zeros((1, 128), F32)
    for i in range(per_core):
        ends, decay = levels_first[0, i : i + 1, :], levels_first[1, i : i + 1, :]
        if i > 0:
            ends = pltpu.roll(ends, i * span, 1)
        line = jnp.where((lane >= i * span) & (lane < (i + 1) * span), ends, line)
        line = jnp.where((lane >= 64 + i * span) & (lane < 64 + (i + 1) * span), decay, line)
    for p, part in enumerate(split3(line)):
        rows_ref[at + p : at + p + 1, :] = part
    out_ref[0] = rows_ref[...].astype(BF16)


def join_kernel(first_ref, second_ref, out_ref):
    count = first_ref.shape[0]
    out_ref[0:count] = first_ref[...]
    out_ref[count:] = second_ref[...]


def gathered_kernel(
    per_core, length, offsets, lengths_ref, near_ref, far_ref, taps, key_edge,
    query_taps, query_edge,
    keys_ref, values_ref, levels_ref, conv_ref, by_chip, wide, value_rows, level_rows, narrow,
):
    half = near_ref.shape[0]
    chips = 2 * half
    me = lax.axis_index("seq") // 2
    width = key_edge.shape[2]
    key_width = width // per_core
    value_width = values_ref.shape[1]
    key_blocks, value_blocks = key_width // 128, value_width // 128
    for k, off in enumerate(offsets):
        message = near_ref[k] if k < half else far_ref[k - half]
        by_chip[lax.bitwise_xor(me, off)] = message.astype(F32)
    row = iota((16 * chips, 128), 0)
    position = length * lax.shift_right_logical(row, 4) + lax.bitwise_and(row, 15) - 8
    same = same_request(lengths_ref, position)
    value_rows[...] = jnp.zeros_like(value_rows)
    level_rows[...] = jnp.full_like(level_rows, 2 * very_negative)
    values_at = FIRST * per_core * key_blocks
    tails_at = values_at + FIRST * per_core * value_blocks
    levels_at = tails_at + 2 * FIRST * per_core * key_blocks
    span = 64 // per_core
    lines = [
        sum(by_chip[g, levels_at + p : levels_at + p + 1, :] for p in range(3))
        for g in range(chips)
    ]
    square = iota((FIRST, 128), 0) == iota((FIRST, 128), 1)
    for i in range(per_core):
        wide[...] = jnp.zeros_like(wide)
        since = jnp.zeros((1, 1), F32)
        for g in reversed(range(chips)):
            at = 16 * g + 8
            for j in range(key_blocks):
                columns = slice(j * 128, (j + 1) * 128)
                source = FIRST * (i * key_blocks + j)
                wide[8 + at : 8 + at + FIRST, columns] = by_chip[g, source : source + FIRST, :]
                if g > 0:
                    source += tails_at
                    wide[8 + at - FIRST : 8 + at, columns] = by_chip[
                        g - 1, source : source + FIRST, :
                    ]
            for j in range(value_blocks):
                source = values_at + FIRST * (i * value_blocks + j)
                value_rows[i * 16 * chips + at : i * 16 * chips + at + FIRST, j * 128 : (j + 1) * 128] = (
                    by_chip[g, source : source + FIRST, :]
                )
            ends = lines[g]
            if i > 0:
                ends = pltpu.roll(ends, 128 - i * span, 1)
            ends = jnp.where(g < me, ends + since, 2 * very_negative)
            decay = lines[g][:, 64 + i * span : 64 + i * span + 1]
            since = since + jnp.where(g < me, decay, 0.0)
            column = jnp.sum(jnp.where(square, ends, 0.0), axis=1, keepdims=True)
            level_rows[i * 16 * chips + at : i * 16 * chips + at + FIRST, :] = jnp.broadcast_to(
                column, (FIRST, 128)
            )
        keys_ref[i * 16 * chips : (i + 1) * 16 * chips, :] = conv_rows(
            same, 0, 16 * chips, taps, slice(i * key_width, (i + 1) * key_width), wide
        )
    values_ref[...] = value_rows[...].astype(BF16)
    levels_ref[...] = level_rows[...]
    same = same_request(lengths_ref, me * length + iota((16, 128), 0))
    previous = jnp.maximum(me - 1, 0)
    for which, (weights, edge) in enumerate(((query_taps, query_edge), (taps, key_edge))):
        for i in range(per_core):
            columns = slice(i * key_width, (i + 1) * key_width)
            for j in range(key_blocks):
                source = tails_at + FIRST * ((1 - which) * per_core + i) * key_blocks + FIRST * j
                narrow[8 - FIRST : 8, j * 128 : (j + 1) * 128] = by_chip[
                    previous, source : source + FIRST, :
                ]
            narrow[8:, :] = edge[0, :, columns].astype(F32)
            conv_ref[which, :, columns] = conv_rows(same, 0, 16, weights, columns, narrow)


def shifted_stab(infos, ranks, upto):
    out = []
    for i, (_, stab, _) in enumerate(infos):
        for j, (_, _, decay) in enumerate(infos):
            if i != j:
                inside = (ranks[j] > ranks[i]) & (ranks[j] < upto)
                stab = stab + jnp.where(inside, decay, 0.0)
        out.append(stab)
    return out


def total_kernel(*refs):
    *states, out = refs
    rows = out.shape[0] - INFO
    _, mine = core_place()
    ranks = [lax.bitwise_xor(mine, off) for off in range(4)]
    infos = [read_info(s) for s in states]
    stabs = shifted_stab(infos, ranks, 4)
    m = functools.reduce(jnp.maximum, stabs)
    weights = [jnp.exp(s - m) for s in stabs]
    out[0:rows, :] = sum(w * s[0:rows, :].astype(F32) for w, s in zip(weights, states)).astype(BF16)
    write_info(out, sum(w * i[0] for w, i in zip(weights, infos)), m, sum(i[2] for i in infos))


def is_later(bit):
    return lax.rem(lax.shift_right_logical(lax.axis_index("seq"), bit), 2) == 1


def round_kernel(bit, first, *refs):
    if first:
        total_ref, got_ref, prefix_out, total_out = refs
    else:
        prefix_ref, total_ref, got_ref, prefix_out, total_out = refs
    rows = total_ref.shape[0] - INFO
    later = is_later(bit)
    n_t, m_t, d_t = read_info(total_ref)
    n_g, m_g, d_g = read_info(got_ref)
    here, got = total_ref[0:rows, :].astype(F32), got_ref[0:rows, :].astype(F32)
    a_t = m_t + jnp.where(later, 0.0, d_g)
    a_g = m_g + jnp.where(later, d_t, 0.0)
    m = jnp.maximum(a_t, a_g)
    w_t, w_g = jnp.exp(a_t - m), jnp.exp(a_g - m)
    total_out[0:rows, :] = (w_t * here + w_g * got).astype(BF16)
    write_info(total_out, w_t * n_t + w_g * n_g, m, d_t + d_g)
    if first:
        n_p, m_p, d_p = jnp.zeros_like(n_g), jnp.full_like(m_g, very_negative), jnp.zeros_like(d_g)
        prefix = jnp.zeros_like(got)
    else:
        n_p, m_p, d_p = read_info(prefix_ref)
        prefix = prefix_ref[0:rows, :].astype(F32)
    a_g = jnp.where(later, m_g + d_p, 2 * very_negative)
    m = jnp.maximum(m_p, a_g)
    w_p = jnp.exp(m_p - m)
    w_g = jnp.where(later, jnp.exp(a_g - m), 0.0)
    prefix_out[0:rows, :] = (w_p * prefix + w_g * got).astype(BF16)
    write_info(prefix_out, w_p * n_p + w_g * n_g, m, d_p + jnp.where(later, d_g, 0.0))


def enter_kernel(bit, prefix_ref, *refs):
    states, outs = refs[:4], refs[4:]
    rows = outs[0].shape[0] - INFO
    _, mine = core_place()
    ranks = [lax.bitwise_xor(mine, off) for off in range(4)]
    infos = [read_info(s) for s in states]
    n_p, m_p, _ = read_info(prefix_ref)
    valid = True if bit is None else is_later(bit)
    for off in (1, 2, 3, 0):
        out = outs[off]
        stabs = shifted_stab(infos, ranks, ranks[off])
        m_in = m_p
        for info, rank in zip(infos, ranks):
            m_in = m_in + jnp.where(rank < ranks[off], info[2], 0.0)
        m_in = jnp.where(valid, m_in, very_negative)
        stabs = [
            jnp.where(rank < ranks[off], s, 2 * very_negative) for s, rank in zip(stabs, ranks)
        ]
        m = functools.reduce(jnp.maximum, stabs, m_in)
        w_in = jnp.where(valid, jnp.exp(m_in - m), 0.0)
        total = w_in * prefix_ref[0:rows, :].astype(F32)
        normal = w_in * n_p
        for i in range(4):
            if i != off:
                w = jnp.where(ranks[i] < ranks[off], jnp.exp(stabs[i] - m), 0.0)
                total = total + w * states[i][0:rows, :].astype(F32)
                normal = normal + w * infos[i][0]
        out[0:rows, :] = total.astype(BF16)
        write_info(out, normal, m, jnp.zeros_like(m))


def query_kernel(
    per_core, lengths_ref, query_ref, query_other, taps_ref,
    conv_ref, taps, edge_ref, queries, wide, sems,
):
    core, _ = core_place()
    length, width = queries.shape
    key_width = width // per_core
    split = query_ref.shape[1] > width
    columns = pl.ds(pl.multiple_of(core * width, 128) if split else 0, width)
    copies = start_copies(
        sems,
        [(taps_ref.at[0, :, columns], taps)]
        + by_core(core, query_ref, query_other, columns, queries),
    )
    offset = lax.axis_index("seq") // 2 * length
    same = same_request(lengths_ref, offset + iota((length, 128), 0))
    for copy in copies:
        copy.wait()
    edge_ref[0] = queries[0:16, :]
    edge_ref[1] = queries[length - 16 :, :]
    for i in range(per_core):
        here = slice(i * key_width, (i + 1) * key_width)
        wide[0:8, :] = jnp.zeros((8, key_width), F32)
        wide[8:, :] = queries[:, here].astype(F32)
        for start in range(0, length, 128):
            conv_ref[start : start + 128, here] = conv_rows(
                same, start, start + 128, taps, here, wide
            )


def intra_kernel(
    per_core, lengths_ref, query_conv, key_ref, conv_first, values, gate_ref,
    query_ref, numerator_ref, stats_ref, keys,
):
    length, width = query_ref.shape
    key_width = width // per_core
    value_width = values.shape[1] // per_core
    key_scale = 1.0 / math.sqrt(key_width)
    offset = lax.axis_index("seq") // 2 * length
    query_ref[...] = query_conv[...]
    query_ref[0:16, :] = conv_first[0]
    keys[...] = key_ref[...]
    keys[0:16, :] = conv_first[1]
    gate, cumulative = gate_ref[0], gate_ref[1]
    by_token = cumulative.T
    segment = segment_of(lengths_ref, offset + iota((length, 1), 0))
    segment_row = segment_of(lengths_ref, offset + iota((1, length), 1))
    before = segment_of(lengths_ref, jnp.full((1, 1), offset - 1, jnp.int32))
    step = length // 2
    lane = iota((step, 128), 1)
    stats = [[jnp.zeros((step, 128), F32)] * 3 for _ in range(2)]
    for i in range(per_core):
        here = slice(i * key_width, (i + 1) * key_width)
        value_columns = slice(i * value_width, (i + 1) * value_width)
        for b in range(2):
            rows, stop = slice(b * step, (b + 1) * step), (b + 1) * step
            allowed = segment_row[:, 0:stop] == segment[rows]
            allowed &= iota((step, stop), 1) <= iota((step, stop), 0) + b * step
            total = by_token[rows, i : i + 1]
            log_weight = jnp.where(
                allowed,
                gate[i : i + 1, 0:stop] - cumulative[i : i + 1, 0:stop] + total,
                very_negative,
            )
            row_max = jnp.max(log_weight, axis=1, keepdims=True)
            scores = dot(query_ref[rows, here], keys[0:stop, here], ((1,), (1,))) * key_scale
            weights = scores * jnp.exp(log_weight - row_max)
            numerator_ref[rows, value_columns] = dot(
                weights.astype(BF16), values[0:stop, value_columns]
            )
            linked = jnp.where(segment[rows] == before, total, very_negative)
            found = (jnp.sum(weights, axis=1, keepdims=True), row_max, linked)
            stats[b] = [jnp.where(lane == i, new, old) for new, old in zip(found, stats[b])]
    for b in range(2):
        for k in range(3):
            stats_ref[k, b * step : (b + 1) * step, :] = stats[b][k]


def head_kernel(
    per_core, own_ref, got1, got2, got3, keys_ref, values_ref, levels_ref,
    query_ref, numerator_ref, stats_ref, keep_ref, send_ref, memory, info,
):
    core, mine = core_place()
    key_width = query_ref.shape[1] // per_core
    value_width = numerator_ref.shape[1] // per_core
    key_scale = 1.0 / math.sqrt(key_width)
    rows = query_ref.shape[1] // 4
    step = keep_ref.shape[0]
    for off, ref in enumerate((own_ref, got1, got2, got3)):
        piece = piece_of(mine, off)
        start = pl.multiple_of(piece * rows, rows)
        for j in range(value_width // 128):
            memory[pl.ds(start, rows), j * 128 : (j + 1) * 128] = ref[j * rows : (j + 1) * rows, :]
        info[piece] = ref[ref.shape[0] - INFO :, :]
    count = keys_ref.shape[0] // per_core
    row, lane = iota((128, key_width), 0), iota((1, 128), 1)
    stabs = jnp.full((1, 128), very_negative, F32)
    parts = []
    for i in range(per_core):
        normal, stab, _ = read_info(info.at[i * key_width // rows], key_width)
        here = slice(i * key_width, (i + 1) * key_width)
        extra = slice(i * count, (i + 1) * count)
        weighted = keys_ref[extra, :].astype(F32) * jnp.exp(levels_ref[extra, 0:1] - stab)
        normal = normal + jnp.sum(weighted, axis=0, keepdims=True)
        memory[here, :] = (
            memory[here, :].astype(F32)
            + dot(weighted.astype(BF16), values_ref[extra, :], ((0,), (0,)))
        ).astype(BF16)
        stabs = jnp.where(lane == i, stab, stabs)
        block = jnp.zeros((128, key_width), F32)
        for k, part in enumerate(split3(normal)):
            block = jnp.where(row == 8 * k + i, part, block)
        parts.append(block.astype(BF16))
    for b in range(2):
        span = slice(b * step, (b + 1) * step)
        queries = [
            query_ref[span, i * key_width : (i + 1) * key_width] for i in range(per_core)
        ]
        from_normal = sum(dot(q, p, ((1,), (1,))) for q, p in zip(queries, parts))
        from_normal = (
            from_normal
            + pltpu.roll(from_normal, 128 - 8, 1)
            + pltpu.roll(from_normal, 128 - 16, 1)
        )
        row_max = stats_ref[1, span, :]
        carried = stabs + stats_ref[2, span, :]
        m = jnp.maximum(row_max, carried)
        w_here = jnp.exp(row_max - m)
        w_in = jnp.exp(carried - m) * key_scale
        denominator = w_here * stats_ref[0, span, :] + w_in * from_normal
        scale = 1.0 / jnp.maximum(jnp.abs(denominator), 1.0)
        w_here, w_in = w_here * scale, w_in * scale
        for i in range(per_core):
            columns = slice(i * value_width, (i + 1) * value_width)
            from_memory = dot(queries[i], memory[i * key_width : (i + 1) * key_width, :])
            head_out = (
                w_here[:, i : i + 1] * numerator_ref[span, columns]
                + w_in[:, i : i + 1] * from_memory
            ).astype(BF16)

            def write(ref, columns=columns, head_out=head_out):
                ref[:, columns] = head_out

            pl.when(core == b)(functools.partial(write, keep_ref))
            pl.when(core != b)(functools.partial(write, send_ref))


def weight_part(weight_ref, half, rows, start, width):
    return weight_ref[
        pl.ds(pl.multiple_of(half * rows, 128), rows), pl.ds(pl.multiple_of(start, 128), width)
    ]


def keep_kernel(off, head_ref, weight_ref, part_ref):
    core, _ = core_place()
    rows, width = head_ref.shape[1], part_ref.shape[1]
    start = lax.bitwise_xor(lax.axis_index("head"), off) * width
    part_ref[...] = dot(head_ref[...], weight_part(weight_ref, core, rows, start, width))


def send_kernel(off, chunk, head_ref, weight_ref, kept_ref, part_ref):
    core, _ = core_place()
    rows, piece, width = head_ref.shape[1], part_ref.shape[1], kept_ref.shape[1]
    start = lax.bitwise_xor(lax.axis_index("head"), off) * width + chunk * piece
    part_ref[...] = (
        dot(head_ref[...], weight_part(weight_ref, 1 - core, rows, start, piece))
        + kept_ref[:, chunk * piece : (chunk + 1) * piece]
    ).astype(part_ref.dtype)


def own_kernel(keep_ref, got_ref, weight_ref, part_ref):
    core, _ = core_place()
    rows, width = keep_ref.shape[1], part_ref.shape[1]
    start = lax.axis_index("head") * width
    part_ref[...] = dot(
        keep_ref[...], weight_part(weight_ref, core, rows, start, width)
    ) + dot(got_ref[...], weight_part(weight_ref, 1 - core, rows, start, width))


def sum_kernel(chunks, own_ref, *refs):
    *arrived, out_ref, held, sems = refs
    width = own_ref.shape[1] // chunks
    parts = sems.shape[0]
    step = own_ref.shape[0] // parts
    copies = []
    for part in range(parts):
        rows = slice(part * step, (part + 1) * step)
        for c in range(chunks):
            columns = slice(c * width, (c + 1) * width)
            total = own_ref[rows, columns]
            for ref in arrived[c::chunks]:
                total = total + ref[rows, :].astype(F32)
            held[rows, columns] = total.astype(held.dtype)
        copies.append(
            pltpu.make_async_copy(
                held.at[pl.ds(part * step, step), :],
                out_ref.at[pl.ds(part * step, step), :],
                sems.at[part],
            )
        )
        copies[-1].start()
    for copy in copies:
        copy.wait()


def call(kernel, out_shape, spaces, scratch, name, flops=0, nbytes=0, limit=24, out=pltpu.VMEM):
    place = {"v": pltpu.VMEM, "s": pltpu.SMEM, "a": pl.ANY, "h": pl.ANY}
    outs = jax.tree.map(lambda _: pl.BlockSpec(memory_space=out), out_shape)
    inner = pl.pallas_call(
        kernel,
        out_shape=out_shape,
        in_specs=[pl.BlockSpec(memory_space=place[s]) for s in spaces],
        out_specs=outs,
        scratch_shapes=scratch,
        compiler_params=pltpu.CompilerParams(vmem_limit_bytes=limit << 20),
        cost_estimate=pl.CostEstimate(flops=flops, bytes_accessed=nbytes, transcendentals=0),
        name=name,
    )

    def run(*args):
        return inner(
            *(
                pltpu.with_memory_space_constraint(x, pltpu.HBM) if s in "hs" else x
                for s, x in zip(spaces, args, strict=True)
            )
        )

    return run


def on_device(
    query_input, key_input, value_input, kernel_taps, input_gate, forget_gate, request_lengths,
    output_weight,
):
    seq_count, head_count = lax.axis_size("seq"), lax.axis_size("head")
    length, key_cols = query_input.shape
    heads = input_gate.shape[0]
    value_cols = value_input.shape[1]
    out_cols = output_weight.shape[1] // head_count
    chip_length = 2 * length
    key_width = key_cols // heads
    per_core = max(1, heads // 2)
    part_keys, part_values = per_core * key_width, value_cols // 2
    value_width = part_values // per_core
    lags = kernel_taps.shape[1]
    rows = part_keys // 4

    def shape(dims, dtype=F32):
        return jax.ShapeDtypeStruct(dims, dtype)

    def swap(x, off):
        return lax.ppermute(x, "seq", [(i, i ^ off) for i in range(seq_count)])

    key_other, value_other = swap(key_input, 1), swap(value_input, 1)
    query_other = swap(query_input, 1)
    gates = call(
        gates_kernel, shape((2, heads, length)), "hh", [pltpu.SemaphoreType.DMA((2,))], "gates"
    )(input_gate, forget_gate)
    gates_other = swap(gates, 1)

    one = shape((rows * value_width // 128 + INFO, 128), BF16)
    key_conv, values, gate_sums, taps, key_edge, levels, *pieces = call(
        functools.partial(chip_kernel, per_core),
        (
            shape((chip_length, part_keys), BF16),
            shape((chip_length, part_values), BF16),
            shape((2, 8, chip_length)),
            shape((lags, part_keys)),
            shape((2, 16, part_keys), BF16),
            shape((2, 8, 128)),
        )
        + (one,) * 4,
        "shahavvh",
        [
            pltpu.VMEM((chip_length, part_keys), BF16),
            pltpu.VMEM((2, max(8, heads), chip_length), F32),
            pltpu.VMEM((2, 8, chip_length), F32),
            pltpu.VMEM((chip_length + 8, key_width), F32),
            pltpu.VMEM((chip_length, part_keys), BF16),
            pltpu.VMEM((part_keys, value_width), BF16),
            pltpu.VMEM((8, key_width), F32),
            pltpu.VMEM((2, 8, 128), F32),
            pltpu.SemaphoreType.DMA((5,)),
        ],
        "chip_state",
        flops=1 << 30,
    )(
        request_lengths, key_input, key_other, value_input, value_other, gates, gates_other,
        kernel_taps,
    )
    states = [pieces[0]] + [swap(pieces[off], 2 * off) for off in (1, 2, 3)]

    count = 16 * seq_count // 2
    lines = FIRST * per_core * (3 * key_width + value_width) // 128 + 3
    lines = -(-lines // 16) * 16
    message = call(
        functools.partial(message_kernel, per_core), shape((1, lines, 128), BF16), "havvv",
        [
            pltpu.VMEM((lines, 128), F32),
            pltpu.VMEM((16, part_keys), BF16),
            pltpu.SemaphoreType.DMA((1,)),
        ],
        "message",
    )(query_input, query_other, key_edge, values, levels)
    bits = seq_count.bit_length() - 1
    steps = [4, 2, 8] if bits == 4 else [1 << b for b in range(1, bits)]
    near, far, offsets = message, swap(message, steps[0]), [0, steps[0] // 2]
    query_conv, query_taps, query_edge = call(
        functools.partial(query_kernel, per_core),
        (
            shape((chip_length, part_keys), BF16),
            shape((lags, part_keys)),
            shape((2, 16, part_keys), BF16),
        ),
        "shah",
        [
            pltpu.VMEM((chip_length, part_keys), BF16),
            pltpu.VMEM((chip_length + 8, key_width), F32),
            pltpu.SemaphoreType.DMA((3,)),
        ],
        "query_conv",
        flops=1 << 30,
    )(request_lengths, query_input, query_other, kernel_taps)
    states, query_conv, far = lax.optimization_barrier((states, query_conv, far))
    total = call(total_kernel, one, "vvvv", [], "group_total")(*states)
    flag = 3
    prefix = swap(total, 12 if bits == 4 else 8)
    near, far, total = lax.optimization_barrier((near, far, total))
    for step in steps[1:]:
        near = call(
            join_kernel, shape((2 * near.shape[0], lines, 128), BF16), "vv", [], "join"
        )(near, far)
        far = swap(near, step)
        offsets = offsets + [off ^ (step // 2) for off in offsets]
    if bits > 4:
        flag = None
        prefix, total = call(
            functools.partial(round_kernel, 3, True), (one, one), "vv", [], "round_state"
        )(total, prefix)
        for bit in range(4, bits):
            prefix, total = call(
                functools.partial(round_kernel, bit, False), (one, one), "vvv", [], "round_state"
            )(prefix, total, swap(total, 1 << bit))
    enter = call(functools.partial(enter_kernel, flag), (one,) * 4, "vvvvv", [], "enter_state")(
        prefix, *states
    )
    gate_sums, near, *enter = lax.optimization_barrier((gate_sums, near, *enter))
    enter = [enter[0]] + [swap(enter[off], 2 * off) for off in (1, 2, 3)]
    *extras, conv_first = call(
        functools.partial(gathered_kernel, per_core, chip_length, tuple(offsets)),
        (
            shape((per_core * count, key_width), BF16),
            shape((per_core * count, value_width), BF16),
            shape((per_core * count, 128)),
            shape((2, 16, part_keys), BF16),
        ),
        "svvvvvv",
        [
            pltpu.VMEM((seq_count // 2, lines, 128), F32),
            pltpu.VMEM((count + 8, key_width), F32),
            pltpu.VMEM((per_core * count, value_width), F32),
            pltpu.VMEM((per_core * count, 128), F32),
            pltpu.VMEM((24, key_width), F32),
        ],
        "gathered_first",
    )(request_lengths, near, far, taps, key_edge, query_taps, query_edge)
    inside = call(
        functools.partial(intra_kernel, per_core),
        (
            shape((chip_length, part_keys), BF16),
            shape((chip_length, part_values)),
            shape((3, chip_length, 128)),
        ),
        "svvvvv",
        [pltpu.VMEM((chip_length, part_keys), BF16)],
        "intra",
        flops=4 << 30,
    )(request_lengths, query_conv, key_conv, conv_first, values, gate_sums)
    half = shape((length, part_values), BF16)
    keep, send = call(
        functools.partial(head_kernel, per_core), (half, half), "v" * 10,
        [
            pltpu.VMEM((part_keys, value_width), BF16),
            pltpu.VMEM((4, INFO, 128), BF16),
        ],
        "head_out",
    )(*enter, *extras, *inside)
    got = swap(send, 1)

    chunks = 2 if head_count == 2 and out_cols % 256 == 0 else 1
    piece = out_cols // chunks
    arrived = []
    for off in range(1, head_count):
        kept = call(
            functools.partial(keep_kernel, off), shape((length, out_cols)), "vv", [],
            "project_kept", flops=2 << 30,
        )(keep, output_weight)
        columns = [
            call(
                functools.partial(send_kernel, off, chunk), shape((length, piece), BF16), "vvv",
                [], "project_other",
            )(got, output_weight, kept)
            for chunk in range(chunks)
        ]
        arrived.append(
            [lax.ppermute(c, "head", [(i, i ^ off) for i in range(head_count)]) for c in columns]
        )
    mixed = call(
        own_kernel, shape((length, out_cols)), "vvv", [], "project_own", flops=4 << 30
    )(keep, got, output_weight)
    return call(
        functools.partial(sum_kernel, chunks), shape((length, out_cols), BF16),
        "v" * (1 + chunks * len(arrived)),
        [pltpu.VMEM((length, out_cols), BF16), pltpu.SemaphoreType.DMA((4,))],
        "mixed_out", out=pl.ANY,
    )(mixed, *(c for columns in arrived for c in columns))


def solution(mesh):
    placed = (
        P("seq", "head"),
        P("seq", "head"),
        P("seq", "head"),
        P(None, None, "head"),
        P("head", "seq"),
        P("head", "seq"),
        P(),
        P("head", None),
    )
    return jax.shard_map(
        on_device, mesh=mesh, in_specs=placed, out_specs=P("seq", "head"), check_vma=False
    )
```

```python
import functools
import math

import jax
import jax.numpy as jnp
from jax import lax
from jax.experimental import pallas as pl
from jax.experimental.pallas import tpu as pltpu
from jax.sharding import PartitionSpec as P

very_negative = -1e30
FIRST = 3
INFO = 16
TAIL = 16
BF16 = jnp.bfloat16
F32 = jnp.float32


def iota(shape, dim):
    return lax.broadcasted_iota(jnp.int32, shape, dim)


def dot(a, b, contract=((1,), (0,))):
    return lax.dot_general(a, b, (contract, ((), ())), preferred_element_type=F32)


def split3(x):
    high = x.astype(BF16).astype(F32)
    rest = x - high
    mid = rest.astype(BF16).astype(F32)
    return high, mid, (rest - mid).astype(BF16).astype(F32)


def segment_of(lengths_ref, position):
    start = jnp.int32(0)
    count = jnp.zeros_like(position)
    for r in range(lengths_ref.shape[0]):
        count = count + (start <= position).astype(jnp.int32)
        start = start + lengths_ref[r]
    return count - 1


def core_place():
    place = lax.axis_index("seq")
    return lax.rem(place, 2), lax.rem(place // 2, 4)


def piece_of(mine, off):
    piece = lax.bitwise_xor(mine, off)
    if lax.axis_size("seq") == 16:
        piece = lax.bitwise_xor(piece, lax.axis_index("seq") // 8 * 2)
    return piece


def start_copies(sems, pairs):
    copies = [pltpu.make_async_copy(a, b, sems.at[i]) for i, (a, b) in enumerate(pairs)]
    for copy in copies:
        copy.start()
    return copies


def by_core(core, own_ref, other_ref, columns, held):
    rows = own_ref.shape[0]
    return [
        (ref.at[:, columns], held.at[pl.ds(pl.multiple_of(half * rows, rows), rows), :])
        for ref, half in ((own_ref, core), (other_ref, 1 - core))
    ]


def gate_rows(core, per_core, gates, raw, picked):
    _, heads, length = gates[0].shape
    for ref, half in ((gates[0], core), (gates[1], 1 - core)):
        for g in range(2):
            raw[g, 0:heads, pl.ds(pl.multiple_of(half * length, length), length)] = ref[g]
    first = core * per_core if heads > 1 else 0
    picked[...] = jnp.zeros_like(picked)
    for g in range(2):
        for i in range(per_core):
            picked[g, i : i + 1, :] = raw[g, pl.ds(first + i, 1), :]
    forget = picked[1]
    log_forget = -(jnp.maximum(-forget, 0.0) + jnp.log1p(jnp.exp(-jnp.abs(forget))))
    upto = jnp.where(iota((length, length), 0) <= iota((length, length), 1), 1.0, 0.0).astype(BF16)
    parts = split3(log_forget)
    sums = [
        sum(dot(part[:, b * length : (b + 1) * length].astype(BF16), upto) for part in parts)
        for b in range(2)
    ]
    cumulative = jnp.concatenate([sums[0], sums[1] + sums[0][:, length - 1 :]], axis=1)
    return picked[0], cumulative


def same_request(lengths_ref, position):
    lag = iota((position.shape[0], 128), 1)
    here = segment_of(lengths_ref, position)
    return (segment_of(lengths_ref, position - lag) == here).astype(F32)


def conv_rows(same, start, stop, taps, columns, wide):
    total = taps[0:1, columns] * wide[8 + start : 8 + stop, :]
    for lag in range(1, taps.shape[0]):
        total = total + taps[lag : lag + 1, columns] * (
            wide[8 + start - lag : 8 + stop - lag, :] * same[start:stop, lag : lag + 1]
        )
    return (0.5 * total * (1.0 + jnp.tanh(0.5 * total))).astype(BF16)


def write_info(ref, normal, stab, decay):
    lines = [p[:, c : c + 128] for p in split3(normal) for c in range(0, normal.shape[1], 128)]
    lines += [jnp.broadcast_to(p, (1, 128)) for x in (stab, decay) for p in split3(x)]
    row = iota((INFO, 128), 0)
    block = jnp.zeros((INFO, 128), F32)
    for i, line in enumerate(lines):
        block = jnp.where(row == i, line, block)
    ref[ref.shape[0] - INFO :, :] = block.astype(BF16)


def read_info(ref, key_width=256):
    b = ref[ref.shape[0] - INFO :, :].astype(F32)
    k = key_width // 128
    normal = jnp.concatenate(
        [b[i : i + 1] + b[i + k : i + k + 1] + b[i + 2 * k : i + 2 * k + 1] for i in range(k)],
        axis=1,
    )
    sums = [b[i : i + 1] + b[i + 1 : i + 2] + b[i + 2 : i + 3] for i in (3 * k, 3 * k + 3)]
    return normal, sums[0][:, 0:1], sums[1][:, 0:1]


def gates_kernel(input_ref, forget_ref, gate_ref, sems):
    copies = start_copies(
        sems, [(ref, gate_ref.at[i]) for i, ref in enumerate((input_ref, forget_ref))]
    )
    for copy in copies:
        copy.wait()


def chip_kernel(
    per_core, lengths_ref, key_ref, key_other, value_ref, value_other, gates_ref, gates_other,
    taps_ref,
    conv_ref, values, gate_ref, taps, key_edge, levels_first, out0, out1, out2, out3,
    keys, raw, picked, wide, weighted_ref, whole, normals, levels, sems,
):
    core, mine = core_place()
    length, width = keys.shape
    key_width = width // per_core
    value_width = values.shape[1] // per_core
    split = gates_ref.shape[1] > 1
    key_columns = pl.ds(pl.multiple_of(core * width, 128) if split else 0, width)
    value_columns = pl.ds(pl.multiple_of(core * values.shape[1], 128), values.shape[1])
    copies = start_copies(
        sems,
        [(taps_ref.at[1, :, key_columns], taps)]
        + by_core(core, key_ref, key_other, key_columns, keys)
        + by_core(core, value_ref, value_other, value_columns, values),
    )
    offset = lax.axis_index("seq") // 2 * length
    gate, cumulative = gate_rows(core, per_core, (gates_ref, gates_other), raw, picked)
    gate_ref[0] = gate
    gate_ref[1] = cumulative
    segment = segment_of(lengths_ref, offset + iota((1, length), 1))
    last = segment_of(lengths_ref, jnp.full((1, 1), offset + length - 1, jnp.int32))
    before = segment_of(lengths_ref, jnp.full((1, 1), offset - 1, jnp.int32))
    total = cumulative[:, length - 1 : length]
    tail_weight = jnp.where(segment == last, gate + total - cumulative, very_negative)
    stab = jnp.max(tail_weight, axis=1, keepdims=True)
    factor = jnp.exp(tail_weight - stab).T
    levels[0] = jnp.broadcast_to(stab, (8, 128))
    through = jnp.where(before == last, total, very_negative)
    levels[1] = jnp.broadcast_to(through, (8, 128))
    levels_first[0] = tail_weight[:, 0:128]
    levels_first[1] = levels[1]
    same = same_request(lengths_ref, offset + iota((length, 128), 0))
    normals[...] = jnp.zeros_like(normals)
    for copy in copies[:3]:
        copy.wait()
    key_edge[0] = keys[0:16, :]
    key_edge[1] = keys[length - 16 :, :]
    step = 128
    for i in range(per_core):
        columns = slice(i * key_width, (i + 1) * key_width)
        wide[0:8, :] = jnp.zeros((8, key_width), F32)
        wide[8:, :] = keys[:, columns].astype(F32)
        normal = jnp.zeros((1, key_width), F32)
        for start in range(0, length, step):
            conv = conv_rows(same, start, start + step, taps, columns, wide)
            conv_ref[start : start + step, columns] = conv
            weight = factor[start : start + step, i : i + 1]
            if start == 0:
                weight = jnp.where(iota((step, 1), 0) >= FIRST, weight, 0.0)
            weighted = conv.astype(F32) * weight
            normal = normal + jnp.sum(weighted, axis=0, keepdims=True)
            weighted_ref[start : start + step, columns] = weighted.astype(BF16)
        normals[i : i + 1, :] = normal
    for copy in copies[3:]:
        copy.wait()
    for i in range(per_core):
        columns = slice(i * key_width, (i + 1) * key_width)
        whole[columns, :] = dot(
            weighted_ref[:, columns],
            values[:, i * value_width : (i + 1) * value_width],
            ((0,), (0,)),
        ).astype(BF16)
    rows = width // 4
    for off, out in enumerate((out0, out1, out2, out3)):
        piece = piece_of(mine, off)
        content = whole[pl.ds(pl.multiple_of(piece * rows, rows), rows), :]
        for j in range(value_width // 128):
            out[j * rows : (j + 1) * rows, :] = content[:, j * 128 : (j + 1) * 128]
        head = piece // (key_width // rows)
        write_info(
            out,
            normals[pl.ds(head, 1), :],
            levels[0, pl.ds(head, 1), :][:, 0:1],
            levels[1, pl.ds(head, 1), :][:, 0:1],
        )


def message_kernel(
    per_core, query_ref, query_other, key_edge, values, levels_first, out_ref, rows_ref, tail, sems
):
    core, _ = core_place()
    width = key_edge.shape[2]
    split = query_ref.shape[1] > width
    columns = pl.ds(pl.multiple_of(core * width, 128) if split else 0, width)
    last = pl.ds(query_ref.shape[0] - 16, 16)
    for ref, here in ((query_ref, core == 1), (query_other, core == 0)):

        def fetch(ref=ref):
            copy = pltpu.make_async_copy(ref.at[last, columns], tail, sems.at[0])
            copy.start()
            copy.wait()

        pl.when(here)(fetch)
    rows_ref[...] = jnp.zeros_like(rows_ref)
    at = 0
    for block in (
        key_edge[0].astype(F32)[0:FIRST],
        values[0:16, :].astype(F32)[0:FIRST],
        key_edge[1].astype(F32)[16 - FIRST :],
        tail[...].astype(F32)[16 - FIRST :],
    ):
        for j in range(block.shape[1] // 128):
            rows_ref[at : at + FIRST, :] = block[:, j * 128 : (j + 1) * 128]
            at += FIRST
    lane, span = iota((1, 128), 1), 64 // per_core
    line = jnp.zeros((1, 128), F32)
    for i in range(per_core):
        ends, decay = levels_first[0, i : i + 1, :], levels_first[1, i : i + 1, :]
        if i > 0:
            ends = pltpu.roll(ends, i * span, 1)
        line = jnp.where((lane >= i * span) & (lane < (i + 1) * span), ends, line)
        line = jnp.where((lane >= 64 + i * span) & (lane < 64 + (i + 1) * span), decay, line)
    for p, part in enumerate(split3(line)):
        rows_ref[at + p : at + p + 1, :] = part
    out_ref[0] = rows_ref[...].astype(BF16)


def join_kernel(first_ref, second_ref, out_ref):
    count = first_ref.shape[0]
    out_ref[0:count] = first_ref[...]
    out_ref[count:] = second_ref[...]


def gathered_kernel(
    per_core, length, offsets, lengths_ref, near_ref, far_ref, taps, key_edge,
    query_taps, query_edge,
    keys_ref, values_ref, levels_ref, conv_ref, by_chip, wide, value_rows, level_rows, narrow,
):
    half = near_ref.shape[0]
    chips = 2 * half
    me = lax.axis_index("seq") // 2
    width = key_edge.shape[2]
    key_width = width // per_core
    value_width = values_ref.shape[1]
    key_blocks, value_blocks = key_width // 128, value_width // 128
    for k, off in enumerate(offsets):
        message = near_ref[k] if k < half else far_ref[k - half]
        by_chip[lax.bitwise_xor(me, off)] = message.astype(F32)
    row = iota((16 * chips, 128), 0)
    position = length * lax.shift_right_logical(row, 4) + lax.bitwise_and(row, 15) - 8
    same = same_request(lengths_ref, position)
    value_rows[...] = jnp.zeros_like(value_rows)
    level_rows[...] = jnp.full_like(level_rows, 2 * very_negative)
    values_at = FIRST * per_core * key_blocks
    tails_at = values_at + FIRST * per_core * value_blocks
    levels_at = tails_at + 2 * FIRST * per_core * key_blocks
    span = 64 // per_core
    lines = [
        sum(by_chip[g, levels_at + p : levels_at + p + 1, :] for p in range(3))
        for g in range(chips)
    ]
    square = iota((FIRST, 128), 0) == iota((FIRST, 128), 1)
    for i in range(per_core):
        wide[...] = jnp.zeros_like(wide)
        since = jnp.zeros((1, 1), F32)
        for g in reversed(range(chips)):
            at = 16 * g + 8
            for j in range(key_blocks):
                columns = slice(j * 128, (j + 1) * 128)
                source = FIRST * (i * key_blocks + j)
                wide[8 + at : 8 + at + FIRST, columns] = by_chip[g, source : source + FIRST, :]
                if g > 0:
                    source += tails_at
                    wide[8 + at - FIRST : 8 + at, columns] = by_chip[
                        g - 1, source : source + FIRST, :
                    ]
            for j in range(value_blocks):
                source = values_at + FIRST * (i * value_blocks + j)
                value_rows[i * 16 * chips + at : i * 16 * chips + at + FIRST, j * 128 : (j + 1) * 128] = (
                    by_chip[g, source : source + FIRST, :]
                )
            ends = lines[g]
            if i > 0:
                ends = pltpu.roll(ends, 128 - i * span, 1)
            ends = jnp.where(g < me, ends + since, 2 * very_negative)
            decay = lines[g][:, 64 + i * span : 64 + i * span + 1]
            since = since + jnp.where(g < me, decay, 0.0)
            column = jnp.sum(jnp.where(square, ends, 0.0), axis=1, keepdims=True)
            level_rows[i * 16 * chips + at : i * 16 * chips + at + FIRST, :] = jnp.broadcast_to(
                column, (FIRST, 128)
            )
        keys_ref[i * 16 * chips : (i + 1) * 16 * chips, :] = conv_rows(
            same, 0, 16 * chips, taps, slice(i * key_width, (i + 1) * key_width), wide
        )
    values_ref[...] = value_rows[...].astype(BF16)
    levels_ref[...] = level_rows[...]
    same = same_request(lengths_ref, me * length + iota((16, 128), 0))
    previous = jnp.maximum(me - 1, 0)
    for which, (weights, edge) in enumerate(((query_taps, query_edge), (taps, key_edge))):
        for i in range(per_core):
            columns = slice(i * key_width, (i + 1) * key_width)
            for j in range(key_blocks):
                source = tails_at + FIRST * ((1 - which) * per_core + i) * key_blocks + FIRST * j
                narrow[8 - FIRST : 8, j * 128 : (j + 1) * 128] = by_chip[
                    previous, source : source + FIRST, :
                ]
            narrow[8:, :] = edge[0, :, columns].astype(F32)
            conv_ref[which, :, columns] = conv_rows(same, 0, 16, weights, columns, narrow)


def shifted_stab(infos, ranks, upto):
    out = []
    for i, (_, stab, _) in enumerate(infos):
        for j, (_, _, decay) in enumerate(infos):
            if i != j:
                inside = (ranks[j] > ranks[i]) & (ranks[j] < upto)
                stab = stab + jnp.where(inside, decay, 0.0)
        out.append(stab)
    return out


def total_kernel(*refs):
    *states, out = refs
    rows = out.shape[0] - INFO
    _, mine = core_place()
    ranks = [lax.bitwise_xor(mine, off) for off in range(4)]
    infos = [read_info(s) for s in states]
    stabs = shifted_stab(infos, ranks, 4)
    m = functools.reduce(jnp.maximum, stabs)
    weights = [jnp.exp(s - m) for s in stabs]
    out[0:rows, :] = sum(w * s[0:rows, :].astype(F32) for w, s in zip(weights, states)).astype(BF16)
    write_info(out, sum(w * i[0] for w, i in zip(weights, infos)), m, sum(i[2] for i in infos))


def is_later(bit):
    return lax.rem(lax.shift_right_logical(lax.axis_index("seq"), bit), 2) == 1


def round_kernel(bit, first, *refs):
    if first:
        total_ref, got_ref, prefix_out, total_out = refs
    else:
        prefix_ref, total_ref, got_ref, prefix_out, total_out = refs
    rows = total_ref.shape[0] - INFO
    later = is_later(bit)
    n_t, m_t, d_t = read_info(total_ref)
    n_g, m_g, d_g = read_info(got_ref)
    here, got = total_ref[0:rows, :].astype(F32), got_ref[0:rows, :].astype(F32)
    a_t = m_t + jnp.where(later, 0.0, d_g)
    a_g = m_g + jnp.where(later, d_t, 0.0)
    m = jnp.maximum(a_t, a_g)
    w_t, w_g = jnp.exp(a_t - m), jnp.exp(a_g - m)
    total_out[0:rows, :] = (w_t * here + w_g * got).astype(BF16)
    write_info(total_out, w_t * n_t + w_g * n_g, m, d_t + d_g)
    if first:
        n_p, m_p, d_p = jnp.zeros_like(n_g), jnp.full_like(m_g, very_negative), jnp.zeros_like(d_g)
        prefix = jnp.zeros_like(got)
    else:
        n_p, m_p, d_p = read_info(prefix_ref)
        prefix = prefix_ref[0:rows, :].astype(F32)
    a_g = jnp.where(later, m_g + d_p, 2 * very_negative)
    m = jnp.maximum(m_p, a_g)
    w_p = jnp.exp(m_p - m)
    w_g = jnp.where(later, jnp.exp(a_g - m), 0.0)
    prefix_out[0:rows, :] = (w_p * prefix + w_g * got).astype(BF16)
    write_info(prefix_out, w_p * n_p + w_g * n_g, m, d_p + jnp.where(later, d_g, 0.0))


def enter_kernel(bit, prefix_ref, *refs):
    states, outs = refs[:4], refs[4:]
    rows = outs[0].shape[0] - INFO
    _, mine = core_place()
    ranks = [lax.bitwise_xor(mine, off) for off in range(4)]
    infos = [read_info(s) for s in states]
    n_p, m_p, _ = read_info(prefix_ref)
    valid = True if bit is None else is_later(bit)
    for off in (1, 2, 3, 0):
        out = outs[off]
        stabs = shifted_stab(infos, ranks, ranks[off])
        m_in = m_p
        for info, rank in zip(infos, ranks):
            m_in = m_in + jnp.where(rank < ranks[off], info[2], 0.0)
        m_in = jnp.where(valid, m_in, very_negative)
        stabs = [
            jnp.where(rank < ranks[off], s, 2 * very_negative) for s, rank in zip(stabs, ranks)
        ]
        m = functools.reduce(jnp.maximum, stabs, m_in)
        w_in = jnp.where(valid, jnp.exp(m_in - m), 0.0)
        total = w_in * prefix_ref[0:rows, :].astype(F32)
        normal = w_in * n_p
        for i in range(4):
            if i != off:
                w = jnp.where(ranks[i] < ranks[off], jnp.exp(stabs[i] - m), 0.0)
                total = total + w * states[i][0:rows, :].astype(F32)
                normal = normal + w * infos[i][0]
        out[0:rows, :] = total.astype(BF16)
        write_info(out, normal, m, jnp.zeros_like(m))


def query_kernel(
    per_core, lengths_ref, query_ref, query_other, taps_ref,
    conv_ref, taps, edge_ref, queries, wide, sems,
):
    core, _ = core_place()
    length, width = queries.shape
    key_width = width // per_core
    split = query_ref.shape[1] > width
    columns = pl.ds(pl.multiple_of(core * width, 128) if split else 0, width)
    copies = start_copies(
        sems,
        [(taps_ref.at[0, :, columns], taps)]
        + by_core(core, query_ref, query_other, columns, queries),
    )
    offset = lax.axis_index("seq") // 2 * length
    same = same_request(lengths_ref, offset + iota((length, 128), 0))
    for copy in copies:
        copy.wait()
    edge_ref[0] = queries[0:16, :]
    edge_ref[1] = queries[length - 16 :, :]
    for i in range(per_core):
        here = slice(i * key_width, (i + 1) * key_width)
        wide[0:8, :] = jnp.zeros((8, key_width), F32)
        wide[8:, :] = queries[:, here].astype(F32)
        for start in range(0, length, 128):
            conv_ref[start : start + 128, here] = conv_rows(
                same, start, start + 128, taps, here, wide
            )


def intra_kernel(
    per_core, lengths_ref, query_conv, key_ref, conv_first, values, gate_ref,
    query_ref, numerator_ref, stats_ref, keys,
):
    length, width = query_ref.shape
    key_width = width // per_core
    value_width = values.shape[1] // per_core
    key_scale = 1.0 / math.sqrt(key_width)
    offset = lax.axis_index("seq") // 2 * length
    query_ref[...] = query_conv[...]
    query_ref[0:16, :] = conv_first[0]
    keys[...] = key_ref[...]
    keys[0:16, :] = conv_first[1]
    gate, cumulative = gate_ref[0], gate_ref[1]
    by_token = cumulative.T
    segment = segment_of(lengths_ref, offset + iota((length, 1), 0))
    segment_row = segment_of(lengths_ref, offset + iota((1, length), 1))
    before = segment_of(lengths_ref, jnp.full((1, 1), offset - 1, jnp.int32))
    step = length // 2
    lane = iota((step, 128), 1)
    stats = [[jnp.zeros((step, 128), F32)] * 3 for _ in range(2)]
    for i in range(per_core):
        here = slice(i * key_width, (i + 1) * key_width)
        value_columns = slice(i * value_width, (i + 1) * value_width)
        for b in range(2):
            rows, stop = slice(b * step, (b + 1) * step), (b + 1) * step
            allowed = segment_row[:, 0:stop] == segment[rows]
            allowed &= iota((step, stop), 1) <= iota((step, stop), 0) + b * step
            total = by_token[rows, i : i + 1]
            log_weight = jnp.where(
                allowed,
                gate[i : i + 1, 0:stop] - cumulative[i : i + 1, 0:stop] + total,
                very_negative,
            )
            row_max = jnp.max(log_weight, axis=1, keepdims=True)
            scores = dot(query_ref[rows, here], keys[0:stop, here], ((1,), (1,))) * key_scale
            weights = scores * jnp.exp(log_weight - row_max)
            numerator_ref[rows, value_columns] = dot(
                weights.astype(BF16), values[0:stop, value_columns]
            )
            linked = jnp.where(segment[rows] == before, total, very_negative)
            found = (jnp.sum(weights, axis=1, keepdims=True), row_max, linked)
            stats[b] = [jnp.where(lane == i, new, old) for new, old in zip(found, stats[b])]
    for b in range(2):
        for k in range(3):
            stats_ref[k, b * step : (b + 1) * step, :] = stats[b][k]


def head_rows(
    per_core, start, memory, parts, stabs, query_ref, numerator_ref, stats_ref, out_ref
):
    step = out_ref.shape[0]
    key_width = query_ref.shape[1] // per_core
    value_width = memory.shape[1]
    key_scale = 1.0 / math.sqrt(key_width)
    span = pl.ds(pl.multiple_of(start, step), step)
    queries = [query_ref[span, i * key_width : (i + 1) * key_width] for i in range(per_core)]
    from_normal = sum(
        dot(q, parts[i * 128 : (i + 1) * 128, :], ((1,), (1,))) for i, q in enumerate(queries)
    )
    from_normal = (
        from_normal
        + pltpu.roll(from_normal, 128 - 8, 1)
        + pltpu.roll(from_normal, 128 - 16, 1)
    )
    row_max = stats_ref[1, span, :]
    carried = stabs[0:1, :] + stats_ref[2, span, :]
    m = jnp.maximum(row_max, carried)
    w_here = jnp.exp(row_max - m)
    w_in = jnp.exp(carried - m) * key_scale
    denominator = w_here * stats_ref[0, span, :] + w_in * from_normal
    scale = 1.0 / jnp.maximum(jnp.abs(denominator), 1.0)
    w_here, w_in = w_here * scale, w_in * scale
    for i in range(per_core):
        columns = slice(i * value_width, (i + 1) * value_width)
        from_memory = dot(queries[i], memory[i * key_width : (i + 1) * key_width, :])
        out_ref[:, columns] = (
            w_here[:, i : i + 1] * numerator_ref[span, columns] + w_in[:, i : i + 1] * from_memory
        ).astype(BF16)


def head_send_kernel(
    per_core, own_ref, got1, got2, got3, keys_ref, values_ref, levels_ref,
    query_ref, numerator_ref, stats_ref, send_ref, memory, parts, stabs, info,
):
    core, mine = core_place()
    key_width = query_ref.shape[1] // per_core
    value_width = memory.shape[1]
    rows = query_ref.shape[1] // 4
    for off, ref in enumerate((own_ref, got1, got2, got3)):
        piece = piece_of(mine, off)
        start = pl.multiple_of(piece * rows, rows)
        for j in range(value_width // 128):
            memory[pl.ds(start, rows), j * 128 : (j + 1) * 128] = ref[j * rows : (j + 1) * rows, :]
        info[piece] = ref[ref.shape[0] - INFO :, :]
    count = keys_ref.shape[0] // per_core
    row, lane = iota((128, key_width), 0), iota((1, 128), 1)
    levels = jnp.full((1, 128), very_negative, F32)
    for i in range(per_core):
        normal, stab, _ = read_info(info.at[i * key_width // rows], key_width)
        here = slice(i * key_width, (i + 1) * key_width)
        extra = slice(i * count, (i + 1) * count)
        weighted = keys_ref[extra, :].astype(F32) * jnp.exp(levels_ref[extra, 0:1] - stab)
        normal = normal + jnp.sum(weighted, axis=0, keepdims=True)
        memory[here, :] = (
            memory[here, :].astype(F32)
            + dot(weighted.astype(BF16), values_ref[extra, :], ((0,), (0,)))
        ).astype(BF16)
        levels = jnp.where(lane == i, stab, levels)
        block = jnp.zeros((128, key_width), F32)
        for k, part in enumerate(split3(normal)):
            block = jnp.where(row == 8 * k + i, part, block)
        parts[i * 128 : (i + 1) * 128, :] = block.astype(BF16)
    stabs[...] = jnp.broadcast_to(levels, stabs.shape)
    start = (1 - core) * send_ref.shape[0]
    head_rows(
        per_core, start, memory, parts, stabs, query_ref, numerator_ref, stats_ref, send_ref
    )


def head_keep_kernel(
    per_core, memory, parts, stabs, query_ref, numerator_ref, stats_ref, keep_ref
):
    core, _ = core_place()
    start = core * keep_ref.shape[0]
    head_rows(
        per_core, start, memory, parts, stabs, query_ref, numerator_ref, stats_ref, keep_ref
    )


def weight_part(weight_ref, half, rows, start, width):
    return weight_ref[
        pl.ds(pl.multiple_of(half * rows, 128), rows), pl.ds(pl.multiple_of(start, 128), width)
    ]


def keep_kernel(off, head_ref, weight_ref, part_ref):
    core, _ = core_place()
    rows, width = head_ref.shape[1], part_ref.shape[1]
    start = lax.bitwise_xor(lax.axis_index("head"), off) * width
    part_ref[...] = dot(head_ref[...], weight_part(weight_ref, core, rows, start, width))


def send_kernel(off, chunk, head_ref, weight_ref, kept_ref, part_ref):
    core, _ = core_place()
    rows, piece, width = head_ref.shape[1], part_ref.shape[1], kept_ref.shape[1]
    start = lax.bitwise_xor(lax.axis_index("head"), off) * width + chunk * piece
    part_ref[...] = (
        dot(head_ref[...], weight_part(weight_ref, 1 - core, rows, start, piece))
        + kept_ref[:, chunk * piece : (chunk + 1) * piece]
    ).astype(part_ref.dtype)


def own_kernel(keep_ref, got_ref, weight_ref, part_ref):
    core, _ = core_place()
    rows, width = keep_ref.shape[1], part_ref.shape[1]
    start = lax.axis_index("head") * width
    part_ref[...] = dot(
        keep_ref[...], weight_part(weight_ref, core, rows, start, width)
    ) + dot(got_ref[...], weight_part(weight_ref, 1 - core, rows, start, width))


def sum_kernel(chunk, count, own_ref, *refs):
    arrived, (out_ref, held, sems) = refs[:count], refs[-3:]
    width = held.shape[1]
    columns = pl.ds(chunk * width, width)
    parts = sems.shape[0]
    step = own_ref.shape[0] // parts
    copies = []
    for part in range(parts):
        rows = slice(part * step, (part + 1) * step)
        total = own_ref[rows, chunk * width : (chunk + 1) * width]
        for ref in arrived:
            total = total + ref[rows, :].astype(F32)
        held[rows, :] = total.astype(held.dtype)
        span = pl.ds(part * step, step)
        copies.append(
            pltpu.make_async_copy(held.at[span, :], out_ref.at[span, columns], sems.at[part])
        )
        copies[-1].start()
    for copy in copies:
        copy.wait()


def call(kernel, out_shape, spaces, scratch, name, flops=0, nbytes=0, limit=24, out=pltpu.VMEM,
         aliases=None):
    place = {"v": pltpu.VMEM, "s": pltpu.SMEM, "a": pl.ANY, "h": pl.ANY}
    outs = jax.tree.map(lambda _: pl.BlockSpec(memory_space=out), out_shape)
    inner = pl.pallas_call(
        kernel,
        out_shape=out_shape,
        in_specs=[pl.BlockSpec(memory_space=place[s]) for s in spaces],
        out_specs=outs,
        scratch_shapes=scratch,
        compiler_params=pltpu.CompilerParams(vmem_limit_bytes=limit << 20),
        cost_estimate=pl.CostEstimate(flops=flops, bytes_accessed=nbytes, transcendentals=0),
        name=name,
        input_output_aliases=aliases or {},
    )

    def run(*args):
        return inner(
            *(
                pltpu.with_memory_space_constraint(x, pltpu.HBM) if s in "hs" else x
                for s, x in zip(spaces, args, strict=True)
            )
        )

    return run


def on_device(
    query_input, key_input, value_input, kernel_taps, input_gate, forget_gate, request_lengths,
    output_weight,
):
    seq_count, head_count = lax.axis_size("seq"), lax.axis_size("head")
    length, key_cols = query_input.shape
    heads = input_gate.shape[0]
    value_cols = value_input.shape[1]
    out_cols = output_weight.shape[1] // head_count
    chip_length = 2 * length
    key_width = key_cols // heads
    per_core = max(1, heads // 2)
    part_keys, part_values = per_core * key_width, value_cols // 2
    value_width = part_values // per_core
    lags = kernel_taps.shape[1]
    rows = part_keys // 4

    def shape(dims, dtype=F32):
        return jax.ShapeDtypeStruct(dims, dtype)

    def swap(x, off):
        return lax.ppermute(x, "seq", [(i, i ^ off) for i in range(seq_count)])

    key_other, value_other = swap(key_input, 1), swap(value_input, 1)
    query_other = swap(query_input, 1)
    gates = call(
        gates_kernel, shape((2, heads, length)), "hh", [pltpu.SemaphoreType.DMA((2,))], "gates"
    )(input_gate, forget_gate)
    gates_other = swap(gates, 1)

    one = shape((rows * value_width // 128 + INFO, 128), BF16)
    key_conv, values, gate_sums, taps, key_edge, levels, *pieces = call(
        functools.partial(chip_kernel, per_core),
        (
            shape((chip_length, part_keys), BF16),
            shape((chip_length, part_values), BF16),
            shape((2, 8, chip_length)),
            shape((lags, part_keys)),
            shape((2, 16, part_keys), BF16),
            shape((2, 8, 128)),
        )
        + (one,) * 4,
        "shahavvh",
        [
            pltpu.VMEM((chip_length, part_keys), BF16),
            pltpu.VMEM((2, max(8, heads), chip_length), F32),
            pltpu.VMEM((2, 8, chip_length), F32),
            pltpu.VMEM((chip_length + 8, key_width), F32),
            pltpu.VMEM((chip_length, part_keys), BF16),
            pltpu.VMEM((part_keys, value_width), BF16),
            pltpu.VMEM((8, key_width), F32),
            pltpu.VMEM((2, 8, 128), F32),
            pltpu.SemaphoreType.DMA((5,)),
        ],
        "chip_state",
        flops=1 << 30,
    )(
        request_lengths, key_input, key_other, value_input, value_other, gates, gates_other,
        kernel_taps,
    )
    states = [pieces[0]] + [swap(pieces[off], 2 * off) for off in (1, 2, 3)]

    count = 16 * seq_count // 2
    lines = FIRST * per_core * (3 * key_width + value_width) // 128 + 3
    lines = -(-lines // 16) * 16
    message = call(
        functools.partial(message_kernel, per_core), shape((1, lines, 128), BF16), "havvv",
        [
            pltpu.VMEM((lines, 128), F32),
            pltpu.VMEM((16, part_keys), BF16),
            pltpu.SemaphoreType.DMA((1,)),
        ],
        "message",
    )(query_input, query_other, key_edge, values, levels)
    bits = seq_count.bit_length() - 1
    steps = [4, 2, 8] if bits == 4 else [1 << b for b in range(1, bits)]
    near, far, offsets = message, swap(message, steps[0]), [0, steps[0] // 2]
    query_conv, query_taps, query_edge = call(
        functools.partial(query_kernel, per_core),
        (
            shape((chip_length, part_keys), BF16),
            shape((lags, part_keys)),
            shape((2, 16, part_keys), BF16),
        ),
        "shah",
        [
            pltpu.VMEM((chip_length, part_keys), BF16),
            pltpu.VMEM((chip_length + 8, key_width), F32),
            pltpu.SemaphoreType.DMA((3,)),
        ],
        "query_conv",
        flops=1 << 30,
    )(request_lengths, query_input, query_other, kernel_taps)
    states, query_conv, far = lax.optimization_barrier((states, query_conv, far))
    total = call(total_kernel, one, "vvvv", [], "group_total")(*states)
    flag = 3
    prefix = swap(total, 12 if bits == 4 else 8)
    near, far, total = lax.optimization_barrier((near, far, total))
    for step in steps[1:]:
        near = call(
            join_kernel, shape((2 * near.shape[0], lines, 128), BF16), "vv", [], "join"
        )(near, far)
        far = swap(near, step)
        offsets = offsets + [off ^ (step // 2) for off in offsets]
    if bits > 4:
        flag = None
        prefix, total = call(
            functools.partial(round_kernel, 3, True), (one, one), "vv", [], "round_state"
        )(total, prefix)
        for bit in range(4, bits):
            prefix, total = call(
                functools.partial(round_kernel, bit, False), (one, one), "vvv", [], "round_state"
            )(prefix, total, swap(total, 1 << bit))
    enter = call(functools.partial(enter_kernel, flag), (one,) * 4, "vvvvv", [], "enter_state")(
        prefix, *states
    )
    gate_sums, near, *enter = lax.optimization_barrier((gate_sums, near, *enter))
    enter = [enter[0]] + [swap(enter[off], 2 * off) for off in (1, 2, 3)]
    *extras, conv_first = call(
        functools.partial(gathered_kernel, per_core, chip_length, tuple(offsets)),
        (
            shape((per_core * count, key_width), BF16),
            shape((per_core * count, value_width), BF16),
            shape((per_core * count, 128)),
            shape((2, 16, part_keys), BF16),
        ),
        "svvvvvv",
        [
            pltpu.VMEM((seq_count // 2, lines, 128), F32),
            pltpu.VMEM((count + 8, key_width), F32),
            pltpu.VMEM((per_core * count, value_width), F32),
            pltpu.VMEM((per_core * count, 128), F32),
            pltpu.VMEM((24, key_width), F32),
        ],
        "gathered_first",
    )(request_lengths, near, far, taps, key_edge, query_taps, query_edge)
    inside = call(
        functools.partial(intra_kernel, per_core),
        (
            shape((chip_length, part_keys), BF16),
            shape((chip_length, part_values)),
            shape((3, chip_length, 128)),
        ),
        "svvvvv",
        [pltpu.VMEM((chip_length, part_keys), BF16)],
        "intra",
        flops=4 << 30,
    )(request_lengths, query_conv, key_conv, conv_first, values, gate_sums)
    half_out = shape((length, part_values), BF16)
    send, *entered = call(
        functools.partial(head_send_kernel, per_core),
        (
            half_out,
            shape((part_keys, value_width), BF16),
            shape((128 * per_core, key_width), BF16),
            shape((8, 128)),
        ),
        "v" * 10, [pltpu.VMEM((4, INFO, 128), BF16)], "head_send",
    )(*enter, *extras, *inside)
    keep = call(
        functools.partial(head_keep_kernel, per_core), half_out, "v" * 6, [], "head_keep",
        flops=1 << 30,
    )(*entered, *inside)
    got = swap(send, 1)

    chunks = 2 if head_count == 2 and out_cols % 256 == 0 else 1
    piece = out_cols // chunks
    arrived = []
    mixed = call(
        own_kernel, shape((length, out_cols)), "vvv", [], "project_own", flops=4 << 30
    )(keep, got, output_weight)
    for off in range(1, head_count):
        kept = call(
            functools.partial(keep_kernel, off), shape((length, out_cols)), "vv", [],
            "project_kept", flops=2 << 30,
        )(keep, output_weight)
        columns, after = [], got
        for chunk in range(chunks):
            part = call(
                functools.partial(send_kernel, off, chunk), shape((length, piece), BF16), "vvv",
                [], "project_other",
            )(after, output_weight, kept)
            columns.append(
                lax.ppermute(part, "head", [(i, i ^ off) for i in range(head_count)])
            )
            after, mixed = lax.optimization_barrier((got, mixed))
        arrived.append(columns)
    out = []
    for chunk in range(chunks):
        out = [
            call(
                functools.partial(sum_kernel, chunk, len(arrived)),
                shape((length, out_cols), BF16),
                "v" * (1 + len(arrived)) + "a" * len(out),
                [pltpu.VMEM((length, piece), BF16), pltpu.SemaphoreType.DMA((4,))],
                "mixed_out", out=pl.ANY, aliases={1 + len(arrived): 0} if out else None,
            )(mixed, *(columns[chunk] for columns in arrived), *out)
        ]
    return out[0]


def solution(mesh):
    placed = (
        P("seq", "head"),
        P("seq", "head"),
        P("seq", "head"),
        P(None, None, "head"),
        P("head", "seq"),
        P("head", "seq"),
        P(),
        P("head", None),
    )
    return jax.shard_map(
        on_device, mesh=mesh, in_specs=placed, out_specs=P("seq", "head"), check_vma=False
    )
```

```python
import functools
import math

import jax
import jax.numpy as jnp
from jax import lax
from jax.experimental import pallas as pl
from jax.experimental.pallas import tpu as pltpu
from jax.sharding import PartitionSpec as P

very_negative = -1e30
FIRST = 3
INFO = 16
TAIL = 16
BF16 = jnp.bfloat16
F32 = jnp.float32


def iota(shape, dim):
    return lax.broadcasted_iota(jnp.int32, shape, dim)


def dot(a, b, contract=((1,), (0,))):
    return lax.dot_general(a, b, (contract, ((), ())), preferred_element_type=F32)


def split3(x):
    high = x.astype(BF16).astype(F32)
    rest = x - high
    mid = rest.astype(BF16).astype(F32)
    return high, mid, (rest - mid).astype(BF16).astype(F32)


def segment_of(lengths_ref, position):
    start = jnp.int32(0)
    count = jnp.zeros_like(position)
    for r in range(lengths_ref.shape[0]):
        count = count + (start <= position).astype(jnp.int32)
        start = start + lengths_ref[r]
    return count - 1


def core_place():
    place = lax.axis_index("seq")
    return lax.rem(place, 2), lax.rem(place // 2, 4)


def piece_of(mine, off):
    piece = lax.bitwise_xor(mine, off)
    if lax.axis_size("seq") == 16:
        piece = lax.bitwise_xor(piece, lax.axis_index("seq") // 8 * 2)
    return piece


def start_copies(sems, pairs):
    copies = [pltpu.make_async_copy(a, b, sems.at[i]) for i, (a, b) in enumerate(pairs)]
    for copy in copies:
        copy.start()
    return copies


def by_core(core, own_ref, other_ref, columns, held):
    rows = own_ref.shape[0]
    return [
        (ref.at[:, columns], held.at[pl.ds(pl.multiple_of(half * rows, rows), rows), :])
        for ref, half in ((own_ref, core), (other_ref, 1 - core))
    ]


def gate_rows(core, per_core, gates, raw, picked):
    _, heads, length = gates[0].shape
    for ref, half in ((gates[0], core), (gates[1], 1 - core)):
        for g in range(2):
            raw[g, 0:heads, pl.ds(pl.multiple_of(half * length, length), length)] = ref[g]
    first = core * per_core if heads > 1 else 0
    picked[...] = jnp.zeros_like(picked)
    for g in range(2):
        for i in range(per_core):
            picked[g, i : i + 1, :] = raw[g, pl.ds(first + i, 1), :]
    forget = picked[1]
    log_forget = -(jnp.maximum(-forget, 0.0) + jnp.log1p(jnp.exp(-jnp.abs(forget))))
    upto = jnp.where(iota((length, length), 0) <= iota((length, length), 1), 1.0, 0.0).astype(BF16)
    parts = split3(log_forget)
    sums = [
        sum(dot(part[:, b * length : (b + 1) * length].astype(BF16), upto) for part in parts)
        for b in range(2)
    ]
    cumulative = jnp.concatenate([sums[0], sums[1] + sums[0][:, length - 1 :]], axis=1)
    return picked[0], cumulative


def same_request(lengths_ref, position):
    lag = iota((position.shape[0], 128), 1)
    here = segment_of(lengths_ref, position)
    return (segment_of(lengths_ref, position - lag) == here).astype(F32)


def conv_rows(same, start, stop, taps, columns, wide):
    total = taps[0:1, columns] * wide[8 + start : 8 + stop, :]
    for lag in range(1, taps.shape[0]):
        total = total + taps[lag : lag + 1, columns] * (
            wide[8 + start - lag : 8 + stop - lag, :] * same[start:stop, lag : lag + 1]
        )
    return (0.5 * total * (1.0 + jnp.tanh(0.5 * total))).astype(BF16)


def write_info(ref, normal, stab, decay):
    lines = [p[:, c : c + 128] for p in split3(normal) for c in range(0, normal.shape[1], 128)]
    lines += [jnp.broadcast_to(p, (1, 128)) for x in (stab, decay) for p in split3(x)]
    row = iota((INFO, 128), 0)
    block = jnp.zeros((INFO, 128), F32)
    for i, line in enumerate(lines):
        block = jnp.where(row == i, line, block)
    ref[ref.shape[0] - INFO :, :] = block.astype(BF16)


def read_info(ref, key_width=256):
    b = ref[ref.shape[0] - INFO :, :].astype(F32)
    k = key_width // 128
    normal = jnp.concatenate(
        [b[i : i + 1] + b[i + k : i + k + 1] + b[i + 2 * k : i + 2 * k + 1] for i in range(k)],
        axis=1,
    )
    sums = [b[i : i + 1] + b[i + 1 : i + 2] + b[i + 2 : i + 3] for i in (3 * k, 3 * k + 3)]
    return normal, sums[0][:, 0:1], sums[1][:, 0:1]


def half_columns(core, width):
    return pl.ds(pl.multiple_of(core * width, 128), width)


def gates_kernel(
    input_ref, forget_ref, key_ref, value_ref, gate_ref, key_send, send_ref, sems
):
    core, _ = core_place()
    width = key_send.shape[1]
    columns = half_columns(1 - core, width) if key_ref.shape[1] > width else pl.ds(0, width)
    copies = start_copies(
        sems,
        [
            (key_ref.at[:, columns], key_send),
            (value_ref.at[:, half_columns(1 - core, send_ref.shape[1])], send_ref),
            (input_ref, gate_ref.at[0]),
            (forget_ref, gate_ref.at[1]),
        ],
    )
    for copy in copies:
        copy.wait()


def own_kernel_parts(key_ref, value_ref, taps_ref, keys, values, taps, sems):
    core, _ = core_place()
    width = keys.shape[1]
    columns = half_columns(core, width) if key_ref.shape[1] > width else pl.ds(0, width)
    copies = start_copies(
        sems,
        [
            (key_ref.at[:, columns], keys),
            (value_ref.at[:, half_columns(core, values.shape[1])], values),
            (taps_ref.at[1, :, columns], taps),
        ],
    )
    for copy in copies:
        copy.wait()


def chip_kernel(
    per_core, lengths_ref, own_keys, own_values, key_other, value_other, gates_ref, gates_other,
    taps,
    conv_ref, values, gate_ref, key_edge, levels_first, out0, out1, out2, out3,
    raw, picked, wide, weighted_ref, whole, normals, levels, sems,
):
    core, mine = core_place()
    rows, width = own_keys.shape
    length = 2 * rows
    key_width = width // per_core
    value_width = values.shape[1] // per_core
    own_rows = pl.ds(pl.multiple_of(core * rows, rows), rows)
    other_rows = pl.ds(pl.multiple_of((1 - core) * rows, rows), rows)
    copies = start_copies(
        sems, [(own_values, values.at[own_rows, :]), (value_other, values.at[other_rows, :])]
    )
    offset = lax.axis_index("seq") // 2 * length
    gate, cumulative = gate_rows(core, per_core, (gates_ref, gates_other), raw, picked)
    gate_ref[0] = gate
    gate_ref[1] = cumulative
    segment = segment_of(lengths_ref, offset + iota((1, length), 1))
    last = segment_of(lengths_ref, jnp.full((1, 1), offset + length - 1, jnp.int32))
    before = segment_of(lengths_ref, jnp.full((1, 1), offset - 1, jnp.int32))
    total = cumulative[:, length - 1 : length]
    tail_weight = jnp.where(segment == last, gate + total - cumulative, very_negative)
    stab = jnp.max(tail_weight, axis=1, keepdims=True)
    factor = jnp.exp(tail_weight - stab).T
    levels[0] = jnp.broadcast_to(stab, (8, 128))
    through = jnp.where(before == last, total, very_negative)
    levels[1] = jnp.broadcast_to(through, (8, 128))
    levels_first[0] = tail_weight[:, 0:128]
    levels_first[1] = levels[1]
    same = same_request(lengths_ref, offset + iota((length, 128), 0))
    normals[...] = jnp.zeros_like(normals)
    step = 128
    for i in range(per_core):
        columns = slice(i * key_width, (i + 1) * key_width)
        own, other = own_keys[:, columns], key_other[:, columns]
        key_edge[0, :, columns] = jnp.where(core == 0, own[0:16], other[0:16])
        key_edge[1, :, columns] = jnp.where(core == 0, other[rows - 16 :], own[rows - 16 :])
        wide[0:8, :] = jnp.zeros((8, key_width), F32)
        wide[pl.ds(pl.multiple_of(8 + core * rows, 8), rows), :] = own.astype(F32)
        wide[pl.ds(pl.multiple_of(8 + (1 - core) * rows, 8), rows), :] = other.astype(F32)
        normal = jnp.zeros((1, key_width), F32)
        for start in range(0, length, step):
            conv = conv_rows(same, start, start + step, taps, columns, wide)
            conv_ref[start : start + step, columns] = conv
            weight = factor[start : start + step, i : i + 1]
            if start == 0:
                weight = jnp.where(iota((step, 1), 0) >= FIRST, weight, 0.0)
            weighted = conv.astype(F32) * weight
            normal = normal + jnp.sum(weighted, axis=0, keepdims=True)
            weighted_ref[start : start + step, columns] = weighted.astype(BF16)
        normals[i : i + 1, :] = normal
    for i in range(per_core):
        columns = slice(i * key_width, (i + 1) * key_width)
        value_columns = slice(i * value_width, (i + 1) * value_width)
        whole[columns, :] = sum(
            dot(weighted_ref[part, columns], ref[:, value_columns], ((0,), (0,)))
            for part, ref in ((own_rows, own_values), (other_rows, value_other))
        ).astype(BF16)
    rows = width // 4
    for off, out in enumerate((out0, out1, out2, out3)):
        piece = piece_of(mine, off)
        content = whole[pl.ds(pl.multiple_of(piece * rows, rows), rows), :]
        for j in range(value_width // 128):
            out[j * rows : (j + 1) * rows, :] = content[:, j * 128 : (j + 1) * 128]
        head = piece // (key_width // rows)
        write_info(
            out,
            normals[pl.ds(head, 1), :],
            levels[0, pl.ds(head, 1), :][:, 0:1],
            levels[1, pl.ds(head, 1), :][:, 0:1],
        )
    for copy in copies:
        copy.wait()


def message_kernel(
    per_core, query_ref, query_other, key_edge, values, levels_first, out_ref, rows_ref, tail, sems
):
    core, _ = core_place()
    width = key_edge.shape[2]
    split = query_ref.shape[1] > width
    columns = pl.ds(pl.multiple_of(core * width, 128) if split else 0, width)
    last = pl.ds(query_ref.shape[0] - 16, 16)
    for ref, here in ((query_ref, core == 1), (query_other, core == 0)):

        def fetch(ref=ref):
            copy = pltpu.make_async_copy(ref.at[last, columns], tail, sems.at[0])
            copy.start()
            copy.wait()

        pl.when(here)(fetch)
    rows_ref[...] = jnp.zeros_like(rows_ref)
    at = 0
    for block in (
        key_edge[0].astype(F32)[0:FIRST],
        values[0:16, :].astype(F32)[0:FIRST],
        key_edge[1].astype(F32)[16 - FIRST :],
        tail[...].astype(F32)[16 - FIRST :],
    ):
        for j in range(block.shape[1] // 128):
            rows_ref[at : at + FIRST, :] = block[:, j * 128 : (j + 1) * 128]
            at += FIRST
    lane, span = iota((1, 128), 1), 64 // per_core
    line = jnp.zeros((1, 128), F32)
    for i in range(per_core):
        ends, decay = levels_first[0, i : i + 1, :], levels_first[1, i : i + 1, :]
        if i > 0:
            ends = pltpu.roll(ends, i * span, 1)
        line = jnp.where((lane >= i * span) & (lane < (i + 1) * span), ends, line)
        line = jnp.where((lane >= 64 + i * span) & (lane < 64 + (i + 1) * span), decay, line)
    for p, part in enumerate(split3(line)):
        rows_ref[at + p : at + p + 1, :] = part
    out_ref[0] = rows_ref[...].astype(BF16)


def join_kernel(first_ref, second_ref, out_ref):
    count = first_ref.shape[0]
    out_ref[0:count] = first_ref[...]
    out_ref[count:] = second_ref[...]


def gathered_kernel(
    per_core, length, offsets, lengths_ref, near_ref, far_ref, taps, key_edge,
    query_taps, query_edge,
    keys_ref, values_ref, levels_ref, conv_ref, by_chip, wide, value_rows, level_rows, narrow,
):
    half = near_ref.shape[0]
    chips = 2 * half
    me = lax.axis_index("seq") // 2
    width = key_edge.shape[2]
    key_width = width // per_core
    value_width = values_ref.shape[1]
    key_blocks, value_blocks = key_width // 128, value_width // 128
    for k, off in enumerate(offsets):
        message = near_ref[k] if k < half else far_ref[k - half]
        by_chip[lax.bitwise_xor(me, off)] = message.astype(F32)
    row = iota((16 * chips, 128), 0)
    position = length * lax.shift_right_logical(row, 4) + lax.bitwise_and(row, 15) - 8
    same = same_request(lengths_ref, position)
    value_rows[...] = jnp.zeros_like(value_rows)
    level_rows[...] = jnp.full_like(level_rows, 2 * very_negative)
    values_at = FIRST * per_core * key_blocks
    tails_at = values_at + FIRST * per_core * value_blocks
    levels_at = tails_at + 2 * FIRST * per_core * key_blocks
    span = 64 // per_core
    lines = [
        sum(by_chip[g, levels_at + p : levels_at + p + 1, :] for p in range(3))
        for g in range(chips)
    ]
    square = iota((FIRST, 128), 0) == iota((FIRST, 128), 1)
    for i in range(per_core):
        wide[...] = jnp.zeros_like(wide)
        since = jnp.zeros((1, 1), F32)
        for g in reversed(range(chips)):
            at = 16 * g + 8
            for j in range(key_blocks):
                columns = slice(j * 128, (j + 1) * 128)
                source = FIRST * (i * key_blocks + j)
                wide[8 + at : 8 + at + FIRST, columns] = by_chip[g, source : source + FIRST, :]
                if g > 0:
                    source += tails_at
                    wide[8 + at - FIRST : 8 + at, columns] = by_chip[
                        g - 1, source : source + FIRST, :
                    ]
            for j in range(value_blocks):
                source = values_at + FIRST * (i * value_blocks + j)
                value_rows[i * 16 * chips + at : i * 16 * chips + at + FIRST, j * 128 : (j + 1) * 128] = (
                    by_chip[g, source : source + FIRST, :]
                )
            ends = lines[g]
            if i > 0:
                ends = pltpu.roll(ends, 128 - i * span, 1)
            ends = jnp.where(g < me, ends + since, 2 * very_negative)
            decay = lines[g][:, 64 + i * span : 64 + i * span + 1]
            since = since + jnp.where(g < me, decay, 0.0)
            column = jnp.sum(jnp.where(square, ends, 0.0), axis=1, keepdims=True)
            level_rows[i * 16 * chips + at : i * 16 * chips + at + FIRST, :] = jnp.broadcast_to(
                column, (FIRST, 128)
            )
        keys_ref[i * 16 * chips : (i + 1) * 16 * chips, :] = conv_rows(
            same, 0, 16 * chips, taps, slice(i * key_width, (i + 1) * key_width), wide
        )
    values_ref[...] = value_rows[...].astype(BF16)
    levels_ref[...] = level_rows[...]
    same = same_request(lengths_ref, me * length + iota((16, 128), 0))
    previous = jnp.maximum(me - 1, 0)
    for which, (weights, edge) in enumerate(((query_taps, query_edge), (taps, key_edge))):
        for i in range(per_core):
            columns = slice(i * key_width, (i + 1) * key_width)
            for j in range(key_blocks):
                source = tails_at + FIRST * ((1 - which) * per_core + i) * key_blocks + FIRST * j
                narrow[8 - FIRST : 8, j * 128 : (j + 1) * 128] = by_chip[
                    previous, source : source + FIRST, :
                ]
            narrow[8:, :] = edge[0, :, columns].astype(F32)
            conv_ref[which, :, columns] = conv_rows(same, 0, 16, weights, columns, narrow)


def shifted_stab(infos, ranks, upto):
    out = []
    for i, (_, stab, _) in enumerate(infos):
        for j, (_, _, decay) in enumerate(infos):
            if i != j:
                inside = (ranks[j] > ranks[i]) & (ranks[j] < upto)
                stab = stab + jnp.where(inside, decay, 0.0)
        out.append(stab)
    return out


def total_kernel(*refs):
    *states, out = refs
    rows = out.shape[0] - INFO
    _, mine = core_place()
    ranks = [lax.bitwise_xor(mine, off) for off in range(4)]
    infos = [read_info(s) for s in states]
    stabs = shifted_stab(infos, ranks, 4)
    m = functools.reduce(jnp.maximum, stabs)
    weights = [jnp.exp(s - m) for s in stabs]
    out[0:rows, :] = sum(w * s[0:rows, :].astype(F32) for w, s in zip(weights, states)).astype(BF16)
    write_info(out, sum(w * i[0] for w, i in zip(weights, infos)), m, sum(i[2] for i in infos))


def is_later(bit):
    return lax.rem(lax.shift_right_logical(lax.axis_index("seq"), bit), 2) == 1


def round_kernel(bit, first, *refs):
    if first:
        total_ref, got_ref, prefix_out, total_out = refs
    else:
        prefix_ref, total_ref, got_ref, prefix_out, total_out = refs
    rows = total_ref.shape[0] - INFO
    later = is_later(bit)
    n_t, m_t, d_t = read_info(total_ref)
    n_g, m_g, d_g = read_info(got_ref)
    here, got = total_ref[0:rows, :].astype(F32), got_ref[0:rows, :].astype(F32)
    a_t = m_t + jnp.where(later, 0.0, d_g)
    a_g = m_g + jnp.where(later, d_t, 0.0)
    m = jnp.maximum(a_t, a_g)
    w_t, w_g = jnp.exp(a_t - m), jnp.exp(a_g - m)
    total_out[0:rows, :] = (w_t * here + w_g * got).astype(BF16)
    write_info(total_out, w_t * n_t + w_g * n_g, m, d_t + d_g)
    if first:
        n_p, m_p, d_p = jnp.zeros_like(n_g), jnp.full_like(m_g, very_negative), jnp.zeros_like(d_g)
        prefix = jnp.zeros_like(got)
    else:
        n_p, m_p, d_p = read_info(prefix_ref)
        prefix = prefix_ref[0:rows, :].astype(F32)
    a_g = jnp.where(later, m_g + d_p, 2 * very_negative)
    m = jnp.maximum(m_p, a_g)
    w_p = jnp.exp(m_p - m)
    w_g = jnp.where(later, jnp.exp(a_g - m), 0.0)
    prefix_out[0:rows, :] = (w_p * prefix + w_g * got).astype(BF16)
    write_info(prefix_out, w_p * n_p + w_g * n_g, m, d_p + jnp.where(later, d_g, 0.0))


def enter_kernel(bit, prefix_ref, *refs):
    states, outs = refs[:4], refs[4:]
    rows = outs[0].shape[0] - INFO
    _, mine = core_place()
    ranks = [lax.bitwise_xor(mine, off) for off in range(4)]
    infos = [read_info(s) for s in states]
    n_p, m_p, _ = read_info(prefix_ref)
    valid = True if bit is None else is_later(bit)
    for off in (1, 2, 3, 0):
        out = outs[off]
        stabs = shifted_stab(infos, ranks, ranks[off])
        m_in = m_p
        for info, rank in zip(infos, ranks):
            m_in = m_in + jnp.where(rank < ranks[off], info[2], 0.0)
        m_in = jnp.where(valid, m_in, very_negative)
        stabs = [
            jnp.where(rank < ranks[off], s, 2 * very_negative) for s, rank in zip(stabs, ranks)
        ]
        m = functools.reduce(jnp.maximum, stabs, m_in)
        w_in = jnp.where(valid, jnp.exp(m_in - m), 0.0)
        total = w_in * prefix_ref[0:rows, :].astype(F32)
        normal = w_in * n_p
        for i in range(4):
            if i != off:
                w = jnp.where(ranks[i] < ranks[off], jnp.exp(stabs[i] - m), 0.0)
                total = total + w * states[i][0:rows, :].astype(F32)
                normal = normal + w * infos[i][0]
        out[0:rows, :] = total.astype(BF16)
        write_info(out, normal, m, jnp.zeros_like(m))


def query_kernel(
    per_core, lengths_ref, query_ref, query_other, taps_ref,
    conv_ref, taps, edge_ref, queries, wide, sems,
):
    core, _ = core_place()
    length, width = queries.shape
    key_width = width // per_core
    split = query_ref.shape[1] > width
    columns = pl.ds(pl.multiple_of(core * width, 128) if split else 0, width)
    copies = start_copies(
        sems,
        [(taps_ref.at[0, :, columns], taps)]
        + by_core(core, query_ref, query_other, columns, queries),
    )
    offset = lax.axis_index("seq") // 2 * length
    same = same_request(lengths_ref, offset + iota((length, 128), 0))
    for copy in copies:
        copy.wait()
    edge_ref[0] = queries[0:16, :]
    edge_ref[1] = queries[length - 16 :, :]
    for i in range(per_core):
        here = slice(i * key_width, (i + 1) * key_width)
        wide[0:8, :] = jnp.zeros((8, key_width), F32)
        wide[8:, :] = queries[:, here].astype(F32)
        for start in range(0, length, 128):
            conv_ref[start : start + 128, here] = conv_rows(
                same, start, start + 128, taps, here, wide
            )


def intra_kernel(
    per_core, lengths_ref, query_conv, key_ref, conv_first, values, gate_ref,
    query_ref, numerator_ref, stats_ref, keys,
):
    length, width = query_ref.shape
    key_width = width // per_core
    value_width = values.shape[1] // per_core
    key_scale = 1.0 / math.sqrt(key_width)
    offset = lax.axis_index("seq") // 2 * length
    query_ref[...] = query_conv[...]
    query_ref[0:16, :] = conv_first[0]
    keys[...] = key_ref[...]
    keys[0:16, :] = conv_first[1]
    gate, cumulative = gate_ref[0], gate_ref[1]
    by_token = cumulative.T
    segment = segment_of(lengths_ref, offset + iota((length, 1), 0))
    segment_row = segment_of(lengths_ref, offset + iota((1, length), 1))
    before = segment_of(lengths_ref, jnp.full((1, 1), offset - 1, jnp.int32))
    step = length // 2
    lane = iota((step, 128), 1)
    stats = [[jnp.zeros((step, 128), F32)] * 3 for _ in range(2)]
    for i in range(per_core):
        here = slice(i * key_width, (i + 1) * key_width)
        value_columns = slice(i * value_width, (i + 1) * value_width)
        for b in range(2):
            rows, stop = slice(b * step, (b + 1) * step), (b + 1) * step
            allowed = segment_row[:, 0:stop] == segment[rows]
            allowed &= iota((step, stop), 1) <= iota((step, stop), 0) + b * step
            total = by_token[rows, i : i + 1]
            log_weight = jnp.where(
                allowed,
                gate[i : i + 1, 0:stop] - cumulative[i : i + 1, 0:stop] + total,
                very_negative,
            )
            row_max = jnp.max(log_weight, axis=1, keepdims=True)
            scores = dot(query_ref[rows, here], keys[0:stop, here], ((1,), (1,))) * key_scale
            weights = scores * jnp.exp(log_weight - row_max)
            numerator_ref[rows, value_columns] = dot(
                weights.astype(BF16), values[0:stop, value_columns]
            )
            linked = jnp.where(segment[rows] == before, total, very_negative)
            found = (jnp.sum(weights, axis=1, keepdims=True), row_max, linked)
            stats[b] = [jnp.where(lane == i, new, old) for new, old in zip(found, stats[b])]
    for b in range(2):
        for k in range(3):
            stats_ref[k, b * step : (b + 1) * step, :] = stats[b][k]


def head_rows(
    per_core, start, memory, parts, stabs, query_ref, numerator_ref, stats_ref, out_ref
):
    step = out_ref.shape[0]
    key_width = query_ref.shape[1] // per_core
    value_width = memory.shape[1]
    key_scale = 1.0 / math.sqrt(key_width)
    span = pl.ds(pl.multiple_of(start, step), step)
    queries = [query_ref[span, i * key_width : (i + 1) * key_width] for i in range(per_core)]
    from_normal = sum(
        dot(q, parts[i * 128 : (i + 1) * 128, :], ((1,), (1,))) for i, q in enumerate(queries)
    )
    from_normal = (
        from_normal
        + pltpu.roll(from_normal, 128 - 8, 1)
        + pltpu.roll(from_normal, 128 - 16, 1)
    )
    row_max = stats_ref[1, span, :]
    carried = stabs[0:1, :] + stats_ref[2, span, :]
    m = jnp.maximum(row_max, carried)
    w_here = jnp.exp(row_max - m)
    w_in = jnp.exp(carried - m) * key_scale
    denominator = w_here * stats_ref[0, span, :] + w_in * from_normal
    scale = 1.0 / jnp.maximum(jnp.abs(denominator), 1.0)
    w_here, w_in = w_here * scale, w_in * scale
    for i in range(per_core):
        columns = slice(i * value_width, (i + 1) * value_width)
        from_memory = dot(queries[i], memory[i * key_width : (i + 1) * key_width, :])
        out_ref[:, columns] = (
            w_here[:, i : i + 1] * numerator_ref[span, columns] + w_in[:, i : i + 1] * from_memory
        ).astype(BF16)


def head_send_kernel(
    per_core, own_ref, got1, got2, got3, keys_ref, values_ref, levels_ref,
    query_ref, numerator_ref, stats_ref, send_ref, memory, parts, stabs, info,
):
    core, mine = core_place()
    key_width = query_ref.shape[1] // per_core
    value_width = memory.shape[1]
    rows = query_ref.shape[1] // 4
    for off, ref in enumerate((own_ref, got1, got2, got3)):
        piece = piece_of(mine, off)
        start = pl.multiple_of(piece * rows, rows)
        for j in range(value_width // 128):
            memory[pl.ds(start, rows), j * 128 : (j + 1) * 128] = ref[j * rows : (j + 1) * rows, :]
        info[piece] = ref[ref.shape[0] - INFO :, :]
    count = keys_ref.shape[0] // per_core
    row, lane = iota((128, key_width), 0), iota((1, 128), 1)
    levels = jnp.full((1, 128), very_negative, F32)
    for i in range(per_core):
        normal, stab, _ = read_info(info.at[i * key_width // rows], key_width)
        here = slice(i * key_width, (i + 1) * key_width)
        extra = slice(i * count, (i + 1) * count)
        weighted = keys_ref[extra, :].astype(F32) * jnp.exp(levels_ref[extra, 0:1] - stab)
        normal = normal + jnp.sum(weighted, axis=0, keepdims=True)
        memory[here, :] = (
            memory[here, :].astype(F32)
            + dot(weighted.astype(BF16), values_ref[extra, :], ((0,), (0,)))
        ).astype(BF16)
        levels = jnp.where(lane == i, stab, levels)
        block = jnp.zeros((128, key_width), F32)
        for k, part in enumerate(split3(normal)):
            block = jnp.where(row == 8 * k + i, part, block)
        parts[i * 128 : (i + 1) * 128, :] = block.astype(BF16)
    stabs[...] = jnp.broadcast_to(levels, stabs.shape)
    start = (1 - core) * send_ref.shape[0]
    head_rows(
        per_core, start, memory, parts, stabs, query_ref, numerator_ref, stats_ref, send_ref
    )


def head_keep_kernel(
    per_core, memory, parts, stabs, query_ref, numerator_ref, stats_ref, keep_ref
):
    core, _ = core_place()
    start = core * keep_ref.shape[0]
    head_rows(
        per_core, start, memory, parts, stabs, query_ref, numerator_ref, stats_ref, keep_ref
    )


def weight_part(weight_ref, half, rows, start, width):
    return weight_ref[
        pl.ds(pl.multiple_of(half * rows, 128), rows), pl.ds(pl.multiple_of(start, 128), width)
    ]


def keep_kernel(off, head_ref, weight_ref, part_ref):
    core, _ = core_place()
    rows, width = head_ref.shape[1], part_ref.shape[1]
    start = lax.bitwise_xor(lax.axis_index("head"), off) * width
    part_ref[...] = dot(head_ref[...], weight_part(weight_ref, core, rows, start, width))


def send_kernel(off, chunk, head_ref, weight_ref, kept_ref, part_ref):
    core, _ = core_place()
    rows, piece, width = head_ref.shape[1], part_ref.shape[1], kept_ref.shape[1]
    start = lax.bitwise_xor(lax.axis_index("head"), off) * width + chunk * piece
    part_ref[...] = (
        dot(head_ref[...], weight_part(weight_ref, 1 - core, rows, start, piece))
        + kept_ref[:, chunk * piece : (chunk + 1) * piece]
    ).astype(part_ref.dtype)


def own_kernel(keep_ref, got_ref, weight_ref, part_ref):
    core, _ = core_place()
    rows, width = keep_ref.shape[1], part_ref.shape[1]
    start = lax.axis_index("head") * width
    part_ref[...] = dot(
        keep_ref[...], weight_part(weight_ref, core, rows, start, width)
    ) + dot(got_ref[...], weight_part(weight_ref, 1 - core, rows, start, width))


def sum_kernel(chunk, count, own_ref, *refs):
    arrived, (out_ref, held, sems) = refs[:count], refs[-3:]
    width = held.shape[1]
    columns = pl.ds(chunk * width, width)
    parts = sems.shape[0]
    step = own_ref.shape[0] // parts
    copies = []
    for part in range(parts):
        rows = slice(part * step, (part + 1) * step)
        total = own_ref[rows, chunk * width : (chunk + 1) * width]
        for ref in arrived:
            total = total + ref[rows, :].astype(F32)
        held[rows, :] = total.astype(held.dtype)
        span = pl.ds(part * step, step)
        copies.append(
            pltpu.make_async_copy(held.at[span, :], out_ref.at[span, columns], sems.at[part])
        )
        copies[-1].start()
    for copy in copies:
        copy.wait()


def call(kernel, out_shape, spaces, scratch, name, flops=0, nbytes=0, limit=24, out=pltpu.VMEM,
         aliases=None):
    place = {"v": pltpu.VMEM, "s": pltpu.SMEM, "a": pl.ANY, "h": pl.ANY}
    outs = jax.tree.map(lambda _: pl.BlockSpec(memory_space=out), out_shape)
    inner = pl.pallas_call(
        kernel,
        out_shape=out_shape,
        in_specs=[pl.BlockSpec(memory_space=place[s]) for s in spaces],
        out_specs=outs,
        scratch_shapes=scratch,
        compiler_params=pltpu.CompilerParams(vmem_limit_bytes=limit << 20),
        cost_estimate=pl.CostEstimate(flops=flops, bytes_accessed=nbytes, transcendentals=0),
        name=name,
        input_output_aliases=aliases or {},
    )

    def run(*args):
        return inner(
            *(
                pltpu.with_memory_space_constraint(x, pltpu.HBM) if s in "hs" else x
                for s, x in zip(spaces, args, strict=True)
            )
        )

    return run


def on_device(
    query_input, key_input, value_input, kernel_taps, input_gate, forget_gate, request_lengths,
    output_weight,
):
    seq_count, head_count = lax.axis_size("seq"), lax.axis_size("head")
    length, key_cols = query_input.shape
    heads = input_gate.shape[0]
    value_cols = value_input.shape[1]
    out_cols = output_weight.shape[1] // head_count
    chip_length = 2 * length
    key_width = key_cols // heads
    per_core = max(1, heads // 2)
    part_keys, part_values = per_core * key_width, value_cols // 2
    value_width = part_values // per_core
    lags = kernel_taps.shape[1]
    rows = part_keys // 4

    def shape(dims, dtype=F32):
        return jax.ShapeDtypeStruct(dims, dtype)

    def swap(x, off):
        return lax.ppermute(x, "seq", [(i, i ^ off) for i in range(seq_count)])

    gates, key_send, value_send = call(
        gates_kernel,
        (
            shape((2, heads, length)),
            shape((length, part_keys), BF16),
            shape((length, part_values), BF16),
        ),
        "hhhh", [pltpu.SemaphoreType.DMA((4,))], "gates", flops=4 << 30,
    )(input_gate, forget_gate, key_input, value_input)
    gates_other, key_other, value_other = swap(gates, 1), swap(key_send, 1), swap(value_send, 1)
    key_after, value_after, gates = lax.optimization_barrier((key_input, value_input, gates))
    own_keys, own_values, taps = call(
        own_kernel_parts,
        (
            shape((length, part_keys), BF16),
            shape((length, part_values), BF16),
            shape((lags, part_keys)),
        ),
        "hhh", [pltpu.SemaphoreType.DMA((3,))], "own_part", flops=4 << 30,
    )(key_after, value_after, kernel_taps)
    query_after, gates = lax.optimization_barrier((query_input, gates))
    query_other = swap(query_after, 1)

    one = shape((rows * value_width // 128 + INFO, 128), BF16)
    key_conv, values, gate_sums, key_edge, levels, *pieces = call(
        functools.partial(chip_kernel, per_core),
        (
            shape((chip_length, part_keys), BF16),
            shape((chip_length, part_values), BF16),
            shape((2, 8, chip_length)),
            shape((2, 16, part_keys), BF16),
            shape((2, 8, 128)),
        )
        + (one,) * 4,
        "s" + "v" * 7,
        [
            pltpu.VMEM((2, max(8, heads), chip_length), F32),
            pltpu.VMEM((2, 8, chip_length), F32),
            pltpu.VMEM((chip_length + 8, key_width), F32),
            pltpu.VMEM((chip_length, part_keys), BF16),
            pltpu.VMEM((part_keys, value_width), BF16),
            pltpu.VMEM((8, key_width), F32),
            pltpu.VMEM((2, 8, 128), F32),
            pltpu.SemaphoreType.DMA((2,)),
        ],
        "chip_state",
        flops=1 << 30,
    )(
        request_lengths, own_keys, own_values, key_other, value_other, gates, gates_other, taps
    )
    states = [pieces[0]] + [swap(pieces[off], 2 * off) for off in (1, 2, 3)]

    count = 16 * seq_count // 2
    lines = FIRST * per_core * (3 * key_width + value_width) // 128 + 3
    lines = -(-lines // 16) * 16
    message = call(
        functools.partial(message_kernel, per_core), shape((1, lines, 128), BF16), "havvv",
        [
            pltpu.VMEM((lines, 128), F32),
            pltpu.VMEM((16, part_keys), BF16),
            pltpu.SemaphoreType.DMA((1,)),
        ],
        "message",
    )(query_input, query_other, key_edge, values, levels)
    bits = seq_count.bit_length() - 1
    steps = [4, 2, 8] if bits == 4 else [1 << b for b in range(1, bits)]
    near, far, offsets = message, swap(message, steps[0]), [0, steps[0] // 2]
    query_conv, query_taps, query_edge = call(
        functools.partial(query_kernel, per_core),
        (
            shape((chip_length, part_keys), BF16),
            shape((lags, part_keys)),
            shape((2, 16, part_keys), BF16),
        ),
        "shah",
        [
            pltpu.VMEM((chip_length, part_keys), BF16),
            pltpu.VMEM((chip_length + 8, key_width), F32),
            pltpu.SemaphoreType.DMA((3,)),
        ],
        "query_conv",
        flops=1 << 30,
    )(request_lengths, query_input, query_other, kernel_taps)
    states, query_conv, far = lax.optimization_barrier((states, query_conv, far))
    total = call(total_kernel, one, "vvvv", [], "group_total")(*states)
    flag = 3
    prefix = swap(total, 12 if bits == 4 else 8)
    near, far, total = lax.optimization_barrier((near, far, total))
    for step in steps[1:]:
        near = call(
            join_kernel, shape((2 * near.shape[0], lines, 128), BF16), "vv", [], "join"
        )(near, far)
        far = swap(near, step)
        offsets = offsets + [off ^ (step // 2) for off in offsets]
    if bits > 4:
        flag = None
        prefix, total = call(
            functools.partial(round_kernel, 3, True), (one, one), "vv", [], "round_state"
        )(total, prefix)
        for bit in range(4, bits):
            prefix, total = call(
                functools.partial(round_kernel, bit, False), (one, one), "vvv", [], "round_state"
            )(prefix, total, swap(total, 1 << bit))
    enter = call(functools.partial(enter_kernel, flag), (one,) * 4, "vvvvv", [], "enter_state")(
        prefix, *states
    )
    gate_sums, near, *enter = lax.optimization_barrier((gate_sums, near, *enter))
    enter = [enter[0]] + [swap(enter[off], 2 * off) for off in (1, 2, 3)]
    *extras, conv_first = call(
        functools.partial(gathered_kernel, per_core, chip_length, tuple(offsets)),
        (
            shape((per_core * count, key_width), BF16),
            shape((per_core * count, value_width), BF16),
            shape((per_core * count, 128)),
            shape((2, 16, part_keys), BF16),
        ),
        "svvvvvv",
        [
            pltpu.VMEM((seq_count // 2, lines, 128), F32),
            pltpu.VMEM((count + 8, key_width), F32),
            pltpu.VMEM((per_core * count, value_width), F32),
            pltpu.VMEM((per_core * count, 128), F32),
            pltpu.VMEM((24, key_width), F32),
        ],
        "gathered_first",
    )(request_lengths, near, far, taps, key_edge, query_taps, query_edge)
    inside = call(
        functools.partial(intra_kernel, per_core),
        (
            shape((chip_length, part_keys), BF16),
            shape((chip_length, part_values)),
            shape((3, chip_length, 128)),
        ),
        "svvvvv",
        [pltpu.VMEM((chip_length, part_keys), BF16)],
        "intra",
        flops=4 << 30,
    )(request_lengths, query_conv, key_conv, conv_first, values, gate_sums)
    half_out = shape((length, part_values), BF16)
    send, *entered = call(
        functools.partial(head_send_kernel, per_core),
        (
            half_out,
            shape((part_keys, value_width), BF16),
            shape((128 * per_core, key_width), BF16),
            shape((8, 128)),
        ),
        "v" * 10, [pltpu.VMEM((4, INFO, 128), BF16)], "head_send",
    )(*enter, *extras, *inside)
    keep = call(
        functools.partial(head_keep_kernel, per_core), half_out, "v" * 6, [], "head_keep",
        flops=1 << 30,
    )(*entered, *inside)
    got = swap(send, 1)

    chunks = 2 if head_count == 2 and out_cols % 256 == 0 else 1
    piece = out_cols // chunks
    arrived = []
    mixed = call(
        own_kernel, shape((length, out_cols)), "vvv", [], "project_own", flops=4 << 30
    )(keep, got, output_weight)
    for off in range(1, head_count):
        kept = call(
            functools.partial(keep_kernel, off), shape((length, out_cols)), "vv", [],
            "project_kept", flops=2 << 30,
        )(keep, output_weight)
        columns, after = [], got
        for chunk in range(chunks):
            part = call(
                functools.partial(send_kernel, off, chunk), shape((length, piece), BF16), "vvv",
                [], "project_other",
            )(after, output_weight, kept)
            columns.append(
                lax.ppermute(part, "head", [(i, i ^ off) for i in range(head_count)])
            )
            after, mixed = lax.optimization_barrier((got, mixed))
        arrived.append(columns)
    out = []
    for chunk in range(chunks):
        out = [
            call(
                functools.partial(sum_kernel, chunk, len(arrived)),
                shape((length, out_cols), BF16),
                "v" * (1 + len(arrived)) + "a" * len(out),
                [pltpu.VMEM((length, piece), BF16), pltpu.SemaphoreType.DMA((4,))],
                "mixed_out", out=pl.ANY, aliases={1 + len(arrived): 0} if out else None,
            )(mixed, *(columns[chunk] for columns in arrived), *out)
        ]
    return out[0]


def solution(mesh):
    placed = (
        P("seq", "head"),
        P("seq", "head"),
        P("seq", "head"),
        P(None, None, "head"),
        P("head", "seq"),
        P("head", "seq"),
        P(),
        P("head", None),
    )
    return jax.shard_map(
        on_device, mesh=mesh, in_specs=placed, out_specs=P("seq", "head"), check_vma=False
    )
```

```python
import functools
import math

import jax
import jax.numpy as jnp
from jax import lax
from jax.experimental import pallas as pl
from jax.experimental.pallas import tpu as pltpu
from jax.sharding import PartitionSpec as P

very_negative = -1e30
FIRST = 3
INFO = 16
TAIL = 16
BF16 = jnp.bfloat16
F32 = jnp.float32


def iota(shape, dim):
    return lax.broadcasted_iota(jnp.int32, shape, dim)


def dot(a, b, contract=((1,), (0,))):
    return lax.dot_general(a, b, (contract, ((), ())), preferred_element_type=F32)


def split3(x):
    high = x.astype(BF16).astype(F32)
    rest = x - high
    mid = rest.astype(BF16).astype(F32)
    return high, mid, (rest - mid).astype(BF16).astype(F32)


def segment_of(lengths_ref, position):
    start = jnp.int32(0)
    count = jnp.zeros_like(position)
    for r in range(lengths_ref.shape[0]):
        count = count + (start <= position).astype(jnp.int32)
        start = start + lengths_ref[r]
    return count - 1


def core_place():
    place = lax.axis_index("seq")
    return lax.rem(place, 2), lax.rem(place // 2, 4)


def piece_of(mine, off):
    piece = lax.bitwise_xor(mine, off)
    if lax.axis_size("seq") == 16:
        piece = lax.bitwise_xor(piece, lax.axis_index("seq") // 8 * 2)
    return piece


def start_copies(sems, pairs):
    copies = [pltpu.make_async_copy(a, b, sems.at[i]) for i, (a, b) in enumerate(pairs)]
    for copy in copies:
        copy.start()
    return copies


def by_core(core, own_ref, other_ref, columns, held):
    rows = own_ref.shape[0]
    return [
        (ref.at[:, columns], held.at[pl.ds(pl.multiple_of(half * rows, rows), rows), :])
        for ref, half in ((own_ref, core), (other_ref, 1 - core))
    ]


def gate_rows(core, per_core, gates, raw, picked):
    _, heads, length = gates[0].shape
    for ref, half in ((gates[0], core), (gates[1], 1 - core)):
        for g in range(2):
            raw[g, 0:heads, pl.ds(pl.multiple_of(half * length, length), length)] = ref[g]
    first = core * per_core if heads > 1 else 0
    picked[...] = jnp.zeros_like(picked)
    for g in range(2):
        for i in range(per_core):
            picked[g, i : i + 1, :] = raw[g, pl.ds(first + i, 1), :]
    forget = picked[1]
    log_forget = -(jnp.maximum(-forget, 0.0) + jnp.log1p(jnp.exp(-jnp.abs(forget))))
    upto = jnp.where(iota((length, length), 0) <= iota((length, length), 1), 1.0, 0.0).astype(BF16)
    parts = split3(log_forget)
    sums = [
        sum(dot(part[:, b * length : (b + 1) * length].astype(BF16), upto) for part in parts)
        for b in range(2)
    ]
    cumulative = jnp.concatenate([sums[0], sums[1] + sums[0][:, length - 1 :]], axis=1)
    return picked[0], cumulative


def same_request(lengths_ref, position):
    lag = iota((position.shape[0], 128), 1)
    here = segment_of(lengths_ref, position)
    return (segment_of(lengths_ref, position - lag) == here).astype(F32)


def conv_rows(same, start, stop, taps, columns, wide):
    total = taps[0:1, columns] * wide[8 + start : 8 + stop, :]
    for lag in range(1, taps.shape[0]):
        total = total + taps[lag : lag + 1, columns] * (
            wide[8 + start - lag : 8 + stop - lag, :] * same[start:stop, lag : lag + 1]
        )
    return (0.5 * total * (1.0 + jnp.tanh(0.5 * total))).astype(BF16)


def write_info(ref, normal, stab, decay):
    lines = [p[:, c : c + 128] for p in split3(normal) for c in range(0, normal.shape[1], 128)]
    lines += [jnp.broadcast_to(p, (1, 128)) for x in (stab, decay) for p in split3(x)]
    row = iota((INFO, 128), 0)
    block = jnp.zeros((INFO, 128), F32)
    for i, line in enumerate(lines):
        block = jnp.where(row == i, line, block)
    ref[ref.shape[0] - INFO :, :] = block.astype(BF16)


def read_info(ref, key_width=256):
    b = ref[ref.shape[0] - INFO :, :].astype(F32)
    k = key_width // 128
    normal = jnp.concatenate(
        [b[i : i + 1] + b[i + k : i + k + 1] + b[i + 2 * k : i + 2 * k + 1] for i in range(k)],
        axis=1,
    )
    sums = [b[i : i + 1] + b[i + 1 : i + 2] + b[i + 2 : i + 3] for i in (3 * k, 3 * k + 3)]
    return normal, sums[0][:, 0:1], sums[1][:, 0:1]


def half_columns(core, width):
    return pl.ds(pl.multiple_of(core * width, 128), width)


def gates_kernel(
    input_ref, forget_ref, key_ref, value_ref, gate_ref, key_send, send_ref, sems
):
    core, _ = core_place()
    width = key_send.shape[1]
    columns = half_columns(1 - core, width) if key_ref.shape[1] > width else pl.ds(0, width)
    copies = start_copies(
        sems,
        [
            (key_ref.at[:, columns], key_send),
            (value_ref.at[:, half_columns(1 - core, send_ref.shape[1])], send_ref),
            (input_ref, gate_ref.at[0]),
            (forget_ref, gate_ref.at[1]),
        ],
    )
    for copy in copies:
        copy.wait()


def own_kernel_parts(key_ref, value_ref, taps_ref, keys, values, taps, sems):
    core, _ = core_place()
    width = keys.shape[1]
    columns = half_columns(core, width) if key_ref.shape[1] > width else pl.ds(0, width)
    copies = start_copies(
        sems,
        [
            (key_ref.at[:, columns], keys),
            (value_ref.at[:, half_columns(core, values.shape[1])], values),
            (taps_ref.at[1, :, columns], taps),
        ],
    )
    for copy in copies:
        copy.wait()


def chip_kernel(
    per_core, lengths_ref, own_keys, own_values, key_other, value_other, gates_ref, gates_other,
    taps,
    conv_ref, gate_ref, key_edge, levels_first, out0, out1, out2, out3,
    raw, picked, wide, weighted_ref, whole, normals, levels,
):
    core, mine = core_place()
    rows, width = own_keys.shape
    length = 2 * rows
    key_width = width // per_core
    value_width = own_values.shape[1] // per_core
    own_rows = pl.ds(pl.multiple_of(core * rows, rows), rows)
    other_rows = pl.ds(pl.multiple_of((1 - core) * rows, rows), rows)
    offset = lax.axis_index("seq") // 2 * length
    gate, cumulative = gate_rows(core, per_core, (gates_ref, gates_other), raw, picked)
    gate_ref[0] = gate
    gate_ref[1] = cumulative
    segment = segment_of(lengths_ref, offset + iota((1, length), 1))
    last = segment_of(lengths_ref, jnp.full((1, 1), offset + length - 1, jnp.int32))
    before = segment_of(lengths_ref, jnp.full((1, 1), offset - 1, jnp.int32))
    total = cumulative[:, length - 1 : length]
    tail_weight = jnp.where(segment == last, gate + total - cumulative, very_negative)
    stab = jnp.max(tail_weight, axis=1, keepdims=True)
    factor = jnp.exp(tail_weight - stab).T
    levels[0] = jnp.broadcast_to(stab, (8, 128))
    through = jnp.where(before == last, total, very_negative)
    levels[1] = jnp.broadcast_to(through, (8, 128))
    levels_first[0] = tail_weight[:, 0:128]
    levels_first[1] = levels[1]
    same = same_request(lengths_ref, offset + iota((length, 128), 0))
    normals[...] = jnp.zeros_like(normals)
    step = 128
    for i in range(per_core):
        columns = slice(i * key_width, (i + 1) * key_width)
        own, other = own_keys[:, columns], key_other[:, columns]
        key_edge[0, :, columns] = jnp.where(core == 0, own[0:16], other[0:16])
        key_edge[1, :, columns] = jnp.where(core == 0, other[rows - 16 :], own[rows - 16 :])
        wide[0:8, :] = jnp.zeros((8, key_width), F32)
        wide[pl.ds(pl.multiple_of(8 + core * rows, 8), rows), :] = own.astype(F32)
        wide[pl.ds(pl.multiple_of(8 + (1 - core) * rows, 8), rows), :] = other.astype(F32)
        normal = jnp.zeros((1, key_width), F32)
        for start in range(0, length, step):
            conv = conv_rows(same, start, start + step, taps, columns, wide)
            conv_ref[start : start + step, columns] = conv
            weight = factor[start : start + step, i : i + 1]
            if start == 0:
                weight = jnp.where(iota((step, 1), 0) >= FIRST, weight, 0.0)
            weighted = conv.astype(F32) * weight
            normal = normal + jnp.sum(weighted, axis=0, keepdims=True)
            weighted_ref[start : start + step, columns] = weighted.astype(BF16)
        normals[i : i + 1, :] = normal
    for i in range(per_core):
        columns = slice(i * key_width, (i + 1) * key_width)
        value_columns = slice(i * value_width, (i + 1) * value_width)
        whole[columns, :] = sum(
            dot(weighted_ref[part, columns], ref[:, value_columns], ((0,), (0,)))
            for part, ref in ((own_rows, own_values), (other_rows, value_other))
        ).astype(BF16)
    rows = width // 4
    for off, out in enumerate((out0, out1, out2, out3)):
        piece = piece_of(mine, off)
        content = whole[pl.ds(pl.multiple_of(piece * rows, rows), rows), :]
        for j in range(value_width // 128):
            out[j * rows : (j + 1) * rows, :] = content[:, j * 128 : (j + 1) * 128]
        head = piece // (key_width // rows)
        write_info(
            out,
            normals[pl.ds(head, 1), :],
            levels[0, pl.ds(head, 1), :][:, 0:1],
            levels[1, pl.ds(head, 1), :][:, 0:1],
        )


def message_kernel(
    per_core, query_ref, query_other, key_edge, own_values, value_other, levels_first,
    out_ref, rows_ref, tail, sems,
):
    core, _ = core_place()
    width = key_edge.shape[2]
    split = query_ref.shape[1] > width
    columns = pl.ds(pl.multiple_of(core * width, 128) if split else 0, width)
    last = pl.ds(query_ref.shape[0] - 16, 16)
    for ref, here in ((query_ref, core == 1), (query_other, core == 0)):

        def fetch(ref=ref):
            copy = pltpu.make_async_copy(ref.at[last, columns], tail, sems.at[0])
            copy.start()
            copy.wait()

        pl.when(here)(fetch)
    rows_ref[...] = jnp.zeros_like(rows_ref)
    at = 0
    for block in (
        key_edge[0].astype(F32)[0:FIRST],
        jnp.where(core == 0, own_values[0:16, :], value_other[0:16, :]).astype(F32)[0:FIRST],
        key_edge[1].astype(F32)[16 - FIRST :],
        tail[...].astype(F32)[16 - FIRST :],
    ):
        for j in range(block.shape[1] // 128):
            rows_ref[at : at + FIRST, :] = block[:, j * 128 : (j + 1) * 128]
            at += FIRST
    lane, span = iota((1, 128), 1), 64 // per_core
    line = jnp.zeros((1, 128), F32)
    for i in range(per_core):
        ends, decay = levels_first[0, i : i + 1, :], levels_first[1, i : i + 1, :]
        if i > 0:
            ends = pltpu.roll(ends, i * span, 1)
        line = jnp.where((lane >= i * span) & (lane < (i + 1) * span), ends, line)
        line = jnp.where((lane >= 64 + i * span) & (lane < 64 + (i + 1) * span), decay, line)
    for p, part in enumerate(split3(line)):
        rows_ref[at + p : at + p + 1, :] = part
    out_ref[0] = rows_ref[...].astype(BF16)


def join_kernel(first_ref, second_ref, out_ref):
    count = first_ref.shape[0]
    out_ref[0:count] = first_ref[...]
    out_ref[count:] = second_ref[...]


def gathered_kernel(
    per_core, length, offsets, lengths_ref, near_ref, far_ref, taps, key_edge,
    query_taps, query_edge,
    keys_ref, values_ref, levels_ref, conv_ref, by_chip, wide, value_rows, level_rows, narrow,
):
    half = near_ref.shape[0]
    chips = 2 * half
    me = lax.axis_index("seq") // 2
    width = key_edge.shape[2]
    key_width = width // per_core
    value_width = values_ref.shape[1]
    key_blocks, value_blocks = key_width // 128, value_width // 128
    for k, off in enumerate(offsets):
        message = near_ref[k] if k < half else far_ref[k - half]
        by_chip[lax.bitwise_xor(me, off)] = message.astype(F32)
    row = iota((16 * chips, 128), 0)
    position = length * lax.shift_right_logical(row, 4) + lax.bitwise_and(row, 15) - 8
    same = same_request(lengths_ref, position)
    value_rows[...] = jnp.zeros_like(value_rows)
    level_rows[...] = jnp.full_like(level_rows, 2 * very_negative)
    values_at = FIRST * per_core * key_blocks
    tails_at = values_at + FIRST * per_core * value_blocks
    levels_at = tails_at + 2 * FIRST * per_core * key_blocks
    span = 64 // per_core
    lines = [
        sum(by_chip[g, levels_at + p : levels_at + p + 1, :] for p in range(3))
        for g in range(chips)
    ]
    square = iota((FIRST, 128), 0) == iota((FIRST, 128), 1)
    for i in range(per_core):
        wide[...] = jnp.zeros_like(wide)
        since = jnp.zeros((1, 1), F32)
        for g in reversed(range(chips)):
            at = 16 * g + 8
            for j in range(key_blocks):
                columns = slice(j * 128, (j + 1) * 128)
                source = FIRST * (i * key_blocks + j)
                wide[8 + at : 8 + at + FIRST, columns] = by_chip[g, source : source + FIRST, :]
                if g > 0:
                    source += tails_at
                    wide[8 + at - FIRST : 8 + at, columns] = by_chip[
                        g - 1, source : source + FIRST, :
                    ]
            for j in range(value_blocks):
                source = values_at + FIRST * (i * value_blocks + j)
                value_rows[i * 16 * chips + at : i * 16 * chips + at + FIRST, j * 128 : (j + 1) * 128] = (
                    by_chip[g, source : source + FIRST, :]
                )
            ends = lines[g]
            if i > 0:
                ends = pltpu.roll(ends, 128 - i * span, 1)
            ends = jnp.where(g < me, ends + since, 2 * very_negative)
            decay = lines[g][:, 64 + i * span : 64 + i * span + 1]
            since = since + jnp.where(g < me, decay, 0.0)
            column = jnp.sum(jnp.where(square, ends, 0.0), axis=1, keepdims=True)
            level_rows[i * 16 * chips + at : i * 16 * chips + at + FIRST, :] = jnp.broadcast_to(
                column, (FIRST, 128)
            )
        keys_ref[i * 16 * chips : (i + 1) * 16 * chips, :] = conv_rows(
            same, 0, 16 * chips, taps, slice(i * key_width, (i + 1) * key_width), wide
        )
    values_ref[...] = value_rows[...].astype(BF16)
    levels_ref[...] = level_rows[...]
    same = same_request(lengths_ref, me * length + iota((16, 128), 0))
    previous = jnp.maximum(me - 1, 0)
    for which, (weights, edge) in enumerate(((query_taps, query_edge), (taps, key_edge))):
        for i in range(per_core):
            columns = slice(i * key_width, (i + 1) * key_width)
            for j in range(key_blocks):
                source = tails_at + FIRST * ((1 - which) * per_core + i) * key_blocks + FIRST * j
                narrow[8 - FIRST : 8, j * 128 : (j + 1) * 128] = by_chip[
                    previous, source : source + FIRST, :
                ]
            narrow[8:, :] = edge[0, :, columns].astype(F32)
            conv_ref[which, :, columns] = conv_rows(same, 0, 16, weights, columns, narrow)


def shifted_stab(infos, ranks, upto):
    out = []
    for i, (_, stab, _) in enumerate(infos):
        for j, (_, _, decay) in enumerate(infos):
            if i != j:
                inside = (ranks[j] > ranks[i]) & (ranks[j] < upto)
                stab = stab + jnp.where(inside, decay, 0.0)
        out.append(stab)
    return out


def total_kernel(*refs):
    *states, out = refs
    rows = out.shape[0] - INFO
    _, mine = core_place()
    ranks = [lax.bitwise_xor(mine, off) for off in range(4)]
    infos = [read_info(s) for s in states]
    stabs = shifted_stab(infos, ranks, 4)
    m = functools.reduce(jnp.maximum, stabs)
    weights = [jnp.exp(s - m) for s in stabs]
    out[0:rows, :] = sum(w * s[0:rows, :].astype(F32) for w, s in zip(weights, states)).astype(BF16)
    write_info(out, sum(w * i[0] for w, i in zip(weights, infos)), m, sum(i[2] for i in infos))


def is_later(bit):
    return lax.rem(lax.shift_right_logical(lax.axis_index("seq"), bit), 2) == 1


def round_kernel(bit, first, *refs):
    if first:
        total_ref, got_ref, prefix_out, total_out = refs
    else:
        prefix_ref, total_ref, got_ref, prefix_out, total_out = refs
    rows = total_ref.shape[0] - INFO
    later = is_later(bit)
    n_t, m_t, d_t = read_info(total_ref)
    n_g, m_g, d_g = read_info(got_ref)
    here, got = total_ref[0:rows, :].astype(F32), got_ref[0:rows, :].astype(F32)
    a_t = m_t + jnp.where(later, 0.0, d_g)
    a_g = m_g + jnp.where(later, d_t, 0.0)
    m = jnp.maximum(a_t, a_g)
    w_t, w_g = jnp.exp(a_t - m), jnp.exp(a_g - m)
    total_out[0:rows, :] = (w_t * here + w_g * got).astype(BF16)
    write_info(total_out, w_t * n_t + w_g * n_g, m, d_t + d_g)
    if first:
        n_p, m_p, d_p = jnp.zeros_like(n_g), jnp.full_like(m_g, very_negative), jnp.zeros_like(d_g)
        prefix = jnp.zeros_like(got)
    else:
        n_p, m_p, d_p = read_info(prefix_ref)
        prefix = prefix_ref[0:rows, :].astype(F32)
    a_g = jnp.where(later, m_g + d_p, 2 * very_negative)
    m = jnp.maximum(m_p, a_g)
    w_p = jnp.exp(m_p - m)
    w_g = jnp.where(later, jnp.exp(a_g - m), 0.0)
    prefix_out[0:rows, :] = (w_p * prefix + w_g * got).astype(BF16)
    write_info(prefix_out, w_p * n_p + w_g * n_g, m, d_p + jnp.where(later, d_g, 0.0))


def enter_kernel(bit, prefix_ref, *refs):
    states, outs = refs[:4], refs[4:]
    rows = outs[0].shape[0] - INFO
    _, mine = core_place()
    ranks = [lax.bitwise_xor(mine, off) for off in range(4)]
    infos = [read_info(s) for s in states]
    n_p, m_p, _ = read_info(prefix_ref)
    valid = True if bit is None else is_later(bit)
    weights = []
    for off, out in enumerate(outs):
        stabs = shifted_stab(infos, ranks, ranks[off])
        m_in = m_p
        for info, rank in zip(infos, ranks):
            m_in = m_in + jnp.where(rank < ranks[off], info[2], 0.0)
        m_in = jnp.where(valid, m_in, very_negative)
        stabs = [
            jnp.where(rank < ranks[off], s, 2 * very_negative) for s, rank in zip(stabs, ranks)
        ]
        m = functools.reduce(jnp.maximum, stabs, m_in)
        mine_in = [jnp.where(valid, jnp.exp(m_in - m), 0.0)] + [
            jnp.where(rank < ranks[off], jnp.exp(s - m), 0.0) for s, rank in zip(stabs, ranks)
        ]
        weights.append(mine_in)
        normals = [n_p] + [info[0] for info in infos]
        write_info(out, sum(w * n for w, n in zip(mine_in, normals)), m, jnp.zeros_like(m))
    step = math.gcd(rows, 64)
    for at in range(0, rows, step):
        parts = [r[at : at + step, :].astype(F32) for r in (prefix_ref, *states)]
        for off, out in enumerate(outs):
            out[at : at + step, :] = sum(
                w * part
                for k, (w, part) in enumerate(zip(weights[off], parts))
                if k != off + 1
            ).astype(BF16)


def query_kernel(
    per_core, lengths_ref, query_ref, query_other, taps_ref, own_values, value_other,
    conv_ref, taps, edge_ref, values, queries, wide, sems,
):
    core, _ = core_place()
    length, width = queries.shape
    key_width = width // per_core
    split = query_ref.shape[1] > width
    columns = pl.ds(pl.multiple_of(core * width, 128) if split else 0, width)
    copies = start_copies(
        sems,
        [(taps_ref.at[0, :, columns], taps)]
        + by_core(core, query_ref, query_other, columns, queries)
        + by_core(core, own_values, value_other, slice(None), values),
    )
    offset = lax.axis_index("seq") // 2 * length
    same = same_request(lengths_ref, offset + iota((length, 128), 0))
    for copy in copies:
        copy.wait()
    edge_ref[0] = queries[0:16, :]
    edge_ref[1] = queries[length - 16 :, :]
    for i in range(per_core):
        here = slice(i * key_width, (i + 1) * key_width)
        wide[0:8, :] = jnp.zeros((8, key_width), F32)
        wide[8:, :] = queries[:, here].astype(F32)
        for start in range(0, length, 128):
            conv_ref[start : start + 128, here] = conv_rows(
                same, start, start + 128, taps, here, wide
            )


def intra_kernel(
    per_core, lengths_ref, query_conv, key_ref, conv_first, values, gate_ref,
    query_ref, numerator_ref, stats_ref, keys,
):
    length, width = query_ref.shape
    key_width = width // per_core
    value_width = values.shape[1] // per_core
    key_scale = 1.0 / math.sqrt(key_width)
    offset = lax.axis_index("seq") // 2 * length
    query_ref[...] = query_conv[...]
    query_ref[0:16, :] = conv_first[0]
    keys[...] = key_ref[...]
    keys[0:16, :] = conv_first[1]
    gate, cumulative = gate_ref[0], gate_ref[1]
    by_token = cumulative.T
    segment = segment_of(lengths_ref, offset + iota((length, 1), 0))
    segment_row = segment_of(lengths_ref, offset + iota((1, length), 1))
    before = segment_of(lengths_ref, jnp.full((1, 1), offset - 1, jnp.int32))
    step = length // 2
    lane = iota((step, 128), 1)
    stats = [[jnp.zeros((step, 128), F32)] * 3 for _ in range(2)]
    for i in range(per_core):
        here = slice(i * key_width, (i + 1) * key_width)
        value_columns = slice(i * value_width, (i + 1) * value_width)
        for b in range(2):
            rows, stop = slice(b * step, (b + 1) * step), (b + 1) * step
            allowed = segment_row[:, 0:stop] == segment[rows]
            allowed &= iota((step, stop), 1) <= iota((step, stop), 0) + b * step
            total = by_token[rows, i : i + 1]
            log_weight = jnp.where(
                allowed,
                gate[i : i + 1, 0:stop] - cumulative[i : i + 1, 0:stop] + total,
                very_negative,
            )
            row_max = jnp.max(log_weight, axis=1, keepdims=True)
            scores = dot(query_ref[rows, here], keys[0:stop, here], ((1,), (1,))) * key_scale
            weights = scores * jnp.exp(log_weight - row_max)
            numerator_ref[rows, value_columns] = dot(
                weights.astype(BF16), values[0:stop, value_columns]
            )
            linked = jnp.where(segment[rows] == before, total, very_negative)
            found = (jnp.sum(weights, axis=1, keepdims=True), row_max, linked)
            stats[b] = [jnp.where(lane == i, new, old) for new, old in zip(found, stats[b])]
    for b in range(2):
        for k in range(3):
            stats_ref[k, b * step : (b + 1) * step, :] = stats[b][k]


def head_rows(
    per_core, start, memory, parts, stabs, query_ref, numerator_ref, stats_ref, out_ref
):
    step = out_ref.shape[0]
    key_width = query_ref.shape[1] // per_core
    value_width = memory.shape[1]
    key_scale = 1.0 / math.sqrt(key_width)
    span = pl.ds(pl.multiple_of(start, step), step)
    queries = [query_ref[span, i * key_width : (i + 1) * key_width] for i in range(per_core)]
    from_normal = sum(
        dot(q, parts[i * 128 : (i + 1) * 128, :], ((1,), (1,))) for i, q in enumerate(queries)
    )
    from_normal = (
        from_normal
        + pltpu.roll(from_normal, 128 - 8, 1)
        + pltpu.roll(from_normal, 128 - 16, 1)
    )
    row_max = stats_ref[1, span, :]
    carried = stabs[0:1, :] + stats_ref[2, span, :]
    m = jnp.maximum(row_max, carried)
    w_here = jnp.exp(row_max - m)
    w_in = jnp.exp(carried - m) * key_scale
    denominator = w_here * stats_ref[0, span, :] + w_in * from_normal
    scale = 1.0 / jnp.maximum(jnp.abs(denominator), 1.0)
    w_here, w_in = w_here * scale, w_in * scale
    for i in range(per_core):
        columns = slice(i * value_width, (i + 1) * value_width)
        from_memory = dot(queries[i], memory[i * key_width : (i + 1) * key_width, :])
        out_ref[:, columns] = (
            w_here[:, i : i + 1] * numerator_ref[span, columns] + w_in[:, i : i + 1] * from_memory
        ).astype(BF16)


def head_send_kernel(
    per_core, own_ref, got1, got2, got3, keys_ref, values_ref, levels_ref,
    query_ref, numerator_ref, stats_ref, send_ref, memory, parts, stabs, info,
):
    core, mine = core_place()
    key_width = query_ref.shape[1] // per_core
    value_width = memory.shape[1]
    rows = query_ref.shape[1] // 4
    for off, ref in enumerate((own_ref, got1, got2, got3)):
        piece = piece_of(mine, off)
        start = pl.multiple_of(piece * rows, rows)
        for j in range(value_width // 128):
            memory[pl.ds(start, rows), j * 128 : (j + 1) * 128] = ref[j * rows : (j + 1) * rows, :]
        info[piece] = ref[ref.shape[0] - INFO :, :]
    count = keys_ref.shape[0] // per_core
    row, lane = iota((128, key_width), 0), iota((1, 128), 1)
    levels = jnp.full((1, 128), very_negative, F32)
    for i in range(per_core):
        normal, stab, _ = read_info(info.at[i * key_width // rows], key_width)
        here = slice(i * key_width, (i + 1) * key_width)
        extra = slice(i * count, (i + 1) * count)
        weighted = keys_ref[extra, :].astype(F32) * jnp.exp(levels_ref[extra, 0:1] - stab)
        normal = normal + jnp.sum(weighted, axis=0, keepdims=True)
        memory[here, :] = (
            memory[here, :].astype(F32)
            + dot(weighted.astype(BF16), values_ref[extra, :], ((0,), (0,)))
        ).astype(BF16)
        levels = jnp.where(lane == i, stab, levels)
        block = jnp.zeros((128, key_width), F32)
        for k, part in enumerate(split3(normal)):
            block = jnp.where(row == 8 * k + i, part, block)
        parts[i * 128 : (i + 1) * 128, :] = block.astype(BF16)
    stabs[...] = jnp.broadcast_to(levels, stabs.shape)
    start = (1 - core) * send_ref.shape[0]
    head_rows(
        per_core, start, memory, parts, stabs, query_ref, numerator_ref, stats_ref, send_ref
    )


def head_keep_kernel(
    per_core, memory, parts, stabs, query_ref, numerator_ref, stats_ref, keep_ref
):
    core, _ = core_place()
    start = core * keep_ref.shape[0]
    head_rows(
        per_core, start, memory, parts, stabs, query_ref, numerator_ref, stats_ref, keep_ref
    )


def weight_part(weight_ref, half, rows, start, width):
    return weight_ref[
        pl.ds(pl.multiple_of(half * rows, 128), rows), pl.ds(pl.multiple_of(start, 128), width)
    ]


def keep_kernel(off, head_ref, weight_ref, part_ref):
    core, _ = core_place()
    rows, width = head_ref.shape[1], part_ref.shape[1]
    start = lax.bitwise_xor(lax.axis_index("head"), off) * width
    part_ref[...] = dot(head_ref[...], weight_part(weight_ref, core, rows, start, width))


def send_kernel(off, chunk, head_ref, weight_ref, kept_ref, part_ref):
    core, _ = core_place()
    rows, piece, width = head_ref.shape[1], part_ref.shape[1], kept_ref.shape[1]
    start = lax.bitwise_xor(lax.axis_index("head"), off) * width + chunk * piece
    part_ref[...] = (
        dot(head_ref[...], weight_part(weight_ref, 1 - core, rows, start, piece))
        + kept_ref[:, chunk * piece : (chunk + 1) * piece]
    ).astype(part_ref.dtype)


def own_kernel(keep_ref, got_ref, weight_ref, part_ref):
    core, _ = core_place()
    rows, width = keep_ref.shape[1], part_ref.shape[1]
    start = lax.axis_index("head") * width
    part_ref[...] = dot(
        keep_ref[...], weight_part(weight_ref, core, rows, start, width)
    ) + dot(got_ref[...], weight_part(weight_ref, 1 - core, rows, start, width))


def sum_kernel(chunk, count, own_ref, *refs):
    arrived, (out_ref, held, sems) = refs[:count], refs[-3:]
    width = held.shape[1]
    columns = pl.ds(chunk * width, width)
    parts = sems.shape[0]
    step = own_ref.shape[0] // parts
    copies = []
    for part in range(parts):
        rows = slice(part * step, (part + 1) * step)
        total = own_ref[rows, chunk * width : (chunk + 1) * width]
        for ref in arrived:
            total = total + ref[rows, :].astype(F32)
        held[rows, :] = total.astype(held.dtype)
        span = pl.ds(part * step, step)
        copies.append(
            pltpu.make_async_copy(held.at[span, :], out_ref.at[span, columns], sems.at[part])
        )
        copies[-1].start()
    for copy in copies:
        copy.wait()


def call(kernel, out_shape, spaces, scratch, name, flops=0, nbytes=0, limit=24, out=pltpu.VMEM,
         aliases=None):
    place = {"v": pltpu.VMEM, "s": pltpu.SMEM, "a": pl.ANY, "h": pl.ANY}
    outs = jax.tree.map(lambda _: pl.BlockSpec(memory_space=out), out_shape)
    inner = pl.pallas_call(
        kernel,
        out_shape=out_shape,
        in_specs=[pl.BlockSpec(memory_space=place[s]) for s in spaces],
        out_specs=outs,
        scratch_shapes=scratch,
        compiler_params=pltpu.CompilerParams(vmem_limit_bytes=limit << 20),
        cost_estimate=pl.CostEstimate(flops=flops, bytes_accessed=nbytes, transcendentals=0),
        name=name,
        input_output_aliases=aliases or {},
    )

    def run(*args):
        return inner(
            *(
                pltpu.with_memory_space_constraint(x, pltpu.HBM) if s in "hs" else x
                for s, x in zip(spaces, args, strict=True)
            )
        )

    return run


def on_device(
    query_input, key_input, value_input, kernel_taps, input_gate, forget_gate, request_lengths,
    output_weight,
):
    seq_count, head_count = lax.axis_size("seq"), lax.axis_size("head")
    length, key_cols = query_input.shape
    heads = input_gate.shape[0]
    value_cols = value_input.shape[1]
    out_cols = output_weight.shape[1] // head_count
    chip_length = 2 * length
    key_width = key_cols // heads
    per_core = max(1, heads // 2)
    part_keys, part_values = per_core * key_width, value_cols // 2
    value_width = part_values // per_core
    lags = kernel_taps.shape[1]
    rows = part_keys // 4

    def shape(dims, dtype=F32):
        return jax.ShapeDtypeStruct(dims, dtype)

    def swap(x, off):
        return lax.ppermute(x, "seq", [(i, i ^ off) for i in range(seq_count)])

    gates, key_send, value_send = call(
        gates_kernel,
        (
            shape((2, heads, length)),
            shape((length, part_keys), BF16),
            shape((length, part_values), BF16),
        ),
        "hhhh", [pltpu.SemaphoreType.DMA((4,))], "gates", flops=4 << 30,
    )(input_gate, forget_gate, key_input, value_input)
    gates_other, key_other, value_other = swap(gates, 1), swap(key_send, 1), swap(value_send, 1)
    key_after, value_after, gates = lax.optimization_barrier((key_input, value_input, gates))
    own_keys, own_values, taps = call(
        own_kernel_parts,
        (
            shape((length, part_keys), BF16),
            shape((length, part_values), BF16),
            shape((lags, part_keys)),
        ),
        "hhh", [pltpu.SemaphoreType.DMA((3,))], "own_part", flops=4 << 30,
    )(key_after, value_after, kernel_taps)
    query_after, gates = lax.optimization_barrier((query_input, gates))
    query_other = swap(query_after, 1)

    one = shape((rows * value_width // 128 + INFO, 128), BF16)
    key_conv, gate_sums, key_edge, levels, *pieces = call(
        functools.partial(chip_kernel, per_core),
        (
            shape((chip_length, part_keys), BF16),
            shape((2, 8, chip_length)),
            shape((2, 16, part_keys), BF16),
            shape((2, 8, 128)),
        )
        + (one,) * 4,
        "s" + "v" * 7,
        [
            pltpu.VMEM((2, max(8, heads), chip_length), F32),
            pltpu.VMEM((2, 8, chip_length), F32),
            pltpu.VMEM((chip_length + 8, key_width), F32),
            pltpu.VMEM((chip_length, part_keys), BF16),
            pltpu.VMEM((part_keys, value_width), BF16),
            pltpu.VMEM((8, key_width), F32),
            pltpu.VMEM((2, 8, 128), F32),
        ],
        "chip_state",
        flops=1 << 30,
    )(
        request_lengths, own_keys, own_values, key_other, value_other, gates, gates_other, taps
    )
    states = [pieces[0]] + [swap(pieces[off], 2 * off) for off in (1, 2, 3)]

    count = 16 * seq_count // 2
    lines = FIRST * per_core * (3 * key_width + value_width) // 128 + 3
    lines = -(-lines // 16) * 16
    message = call(
        functools.partial(message_kernel, per_core), shape((1, lines, 128), BF16), "havvvv",
        [
            pltpu.VMEM((lines, 128), F32),
            pltpu.VMEM((16, part_keys), BF16),
            pltpu.SemaphoreType.DMA((1,)),
        ],
        "message",
    )(query_input, query_other, key_edge, own_values, value_other, levels)
    bits = seq_count.bit_length() - 1
    steps = [4, 2, 8] if bits == 4 else [1 << b for b in range(1, bits)]
    near, far, offsets = message, swap(message, steps[0]), [0, steps[0] // 2]
    query_conv, query_taps, query_edge, values = call(
        functools.partial(query_kernel, per_core),
        (
            shape((chip_length, part_keys), BF16),
            shape((lags, part_keys)),
            shape((2, 16, part_keys), BF16),
            shape((chip_length, part_values), BF16),
        ),
        "shahvv",
        [
            pltpu.VMEM((chip_length, part_keys), BF16),
            pltpu.VMEM((chip_length + 8, key_width), F32),
            pltpu.SemaphoreType.DMA((5,)),
        ],
        "query_conv",
        flops=1 << 30,
    )(request_lengths, query_input, query_other, kernel_taps, own_values, value_other)
    states, query_conv, far = lax.optimization_barrier((states, query_conv, far))
    total = call(total_kernel, one, "vvvv", [], "group_total")(*states)
    flag = 3
    prefix = swap(total, 12 if bits == 4 else 8)
    near, far, total = lax.optimization_barrier((near, far, total))
    for step in steps[1:]:
        near = call(
            join_kernel, shape((2 * near.shape[0], lines, 128), BF16), "vv", [], "join"
        )(near, far)
        far = swap(near, step)
        offsets = offsets + [off ^ (step // 2) for off in offsets]
    if bits > 4:
        flag = None
        prefix, total = call(
            functools.partial(round_kernel, 3, True), (one, one), "vv", [], "round_state"
        )(total, prefix)
        for bit in range(4, bits):
            prefix, total = call(
                functools.partial(round_kernel, bit, False), (one, one), "vvv", [], "round_state"
            )(prefix, total, swap(total, 1 << bit))
    enter = call(functools.partial(enter_kernel, flag), (one,) * 4, "vvvvv", [], "enter_state")(
        prefix, *states
    )
    gate_sums, near, *enter = lax.optimization_barrier((gate_sums, near, *enter))
    enter = [enter[0]] + [swap(enter[off], 2 * off) for off in (1, 2, 3)]
    *extras, conv_first = call(
        functools.partial(gathered_kernel, per_core, chip_length, tuple(offsets)),
        (
            shape((per_core * count, key_width), BF16),
            shape((per_core * count, value_width), BF16),
            shape((per_core * count, 128)),
            shape((2, 16, part_keys), BF16),
        ),
        "svvvvvv",
        [
            pltpu.VMEM((seq_count // 2, lines, 128), F32),
            pltpu.VMEM((count + 8, key_width), F32),
            pltpu.VMEM((per_core * count, value_width), F32),
            pltpu.VMEM((per_core * count, 128), F32),
            pltpu.VMEM((24, key_width), F32),
        ],
        "gathered_first",
    )(request_lengths, near, far, taps, key_edge, query_taps, query_edge)
    inside = call(
        functools.partial(intra_kernel, per_core),
        (
            shape((chip_length, part_keys), BF16),
            shape((chip_length, part_values)),
            shape((3, chip_length, 128)),
        ),
        "svvvvv",
        [pltpu.VMEM((chip_length, part_keys), BF16)],
        "intra",
        flops=4 << 30,
    )(request_lengths, query_conv, key_conv, conv_first, values, gate_sums)
    half_out = shape((length, part_values), BF16)
    send, *entered = call(
        functools.partial(head_send_kernel, per_core),
        (
            half_out,
            shape((part_keys, value_width), BF16),
            shape((128 * per_core, key_width), BF16),
            shape((8, 128)),
        ),
        "v" * 10, [pltpu.VMEM((4, INFO, 128), BF16)], "head_send",
    )(*enter, *extras, *inside)
    keep = call(
        functools.partial(head_keep_kernel, per_core), half_out, "v" * 6, [], "head_keep",
        flops=1 << 30,
    )(*entered, *inside)
    got = swap(send, 1)

    chunks = 2 if head_count == 2 and out_cols % 256 == 0 else 1
    piece = out_cols // chunks
    arrived = []
    mixed = call(
        own_kernel, shape((length, out_cols)), "vvv", [], "project_own", flops=4 << 30
    )(keep, got, output_weight)
    for off in range(1, head_count):
        kept = call(
            functools.partial(keep_kernel, off), shape((length, out_cols)), "vv", [],
            "project_kept", flops=2 << 30,
        )(keep, output_weight)
        columns, after = [], got
        for chunk in range(chunks):
            part = call(
                functools.partial(send_kernel, off, chunk), shape((length, piece), BF16), "vvv",
                [], "project_other",
            )(after, output_weight, kept)
            columns.append(
                lax.ppermute(part, "head", [(i, i ^ off) for i in range(head_count)])
            )
            after, mixed = lax.optimization_barrier((got, mixed))
        arrived.append(columns)
    out = []
    for chunk in range(chunks):
        out = [
            call(
                functools.partial(sum_kernel, chunk, len(arrived)),
                shape((length, out_cols), BF16),
                "v" * (1 + len(arrived)) + "a" * len(out),
                [pltpu.VMEM((length, piece), BF16), pltpu.SemaphoreType.DMA((2,))],
                "mixed_out", out=pl.ANY, aliases={1 + len(arrived): 0} if out else None,
            )(mixed, *(columns[chunk] for columns in arrived), *out)
        ]
    return out[0]


def solution(mesh):
    placed = (
        P("seq", "head"),
        P("seq", "head"),
        P("seq", "head"),
        P(None, None, "head"),
        P("head", "seq"),
        P("head", "seq"),
        P(),
        P("head", None),
    )
    return jax.shard_map(
        on_device, mesh=mesh, in_specs=placed, out_specs=P("seq", "head"), check_vma=False
    )
```

```python
import functools
import math

import jax
import jax.numpy as jnp
from jax import lax
from jax.experimental import pallas as pl
from jax.experimental.pallas import tpu as pltpu
from jax.sharding import PartitionSpec as P

very_negative = -1e30
FIRST = 3
INFO = 16
TAIL = 16
BF16 = jnp.bfloat16
F32 = jnp.float32


def iota(shape, dim):
    return lax.broadcasted_iota(jnp.int32, shape, dim)


def dot(a, b, contract=((1,), (0,))):
    return lax.dot_general(a, b, (contract, ((), ())), preferred_element_type=F32)


def split3(x):
    high = x.astype(BF16).astype(F32)
    rest = x - high
    mid = rest.astype(BF16).astype(F32)
    return high, mid, (rest - mid).astype(BF16).astype(F32)


def segment_of(lengths_ref, position):
    start = jnp.int32(0)
    count = jnp.zeros_like(position)
    for r in range(lengths_ref.shape[0]):
        count = count + (start <= position).astype(jnp.int32)
        start = start + lengths_ref[r]
    return count - 1


def core_place():
    place = lax.axis_index("seq")
    return lax.rem(place, 2), lax.rem(place // 2, 4)


def piece_of(mine, off):
    piece = lax.bitwise_xor(mine, off)
    if lax.axis_size("seq") == 16:
        piece = lax.bitwise_xor(piece, lax.axis_index("seq") // 8 * 2)
    return piece


def start_copies(sems, pairs):
    copies = [pltpu.make_async_copy(a, b, sems.at[i]) for i, (a, b) in enumerate(pairs)]
    for copy in copies:
        copy.start()
    return copies


def by_core(core, own_ref, other_ref, columns, held):
    rows = own_ref.shape[0]
    return [
        (ref.at[:, columns], held.at[pl.ds(pl.multiple_of(half * rows, rows), rows), :])
        for ref, half in ((own_ref, core), (other_ref, 1 - core))
    ]


def gate_rows(core, per_core, gates, raw, picked):
    _, heads, length = gates[0].shape
    for ref, half in ((gates[0], core), (gates[1], 1 - core)):
        for g in range(2):
            raw[g, 0:heads, pl.ds(pl.multiple_of(half * length, length), length)] = ref[g]
    first = core * per_core if heads > 1 else 0
    picked[...] = jnp.zeros_like(picked)
    for g in range(2):
        for i in range(per_core):
            picked[g, i : i + 1, :] = raw[g, pl.ds(first + i, 1), :]
    forget = picked[1]
    log_forget = -(jnp.maximum(-forget, 0.0) + jnp.log1p(jnp.exp(-jnp.abs(forget))))
    upto = jnp.where(iota((length, length), 0) <= iota((length, length), 1), 1.0, 0.0).astype(BF16)
    parts = split3(log_forget)
    sums = [
        sum(dot(part[:, b * length : (b + 1) * length].astype(BF16), upto) for part in parts)
        for b in range(2)
    ]
    cumulative = jnp.concatenate([sums[0], sums[1] + sums[0][:, length - 1 :]], axis=1)
    return picked[0], cumulative


def same_request(lengths_ref, position):
    lag = iota((position.shape[0], 128), 1)
    here = segment_of(lengths_ref, position)
    return (segment_of(lengths_ref, position - lag) == here).astype(F32)


def lag_masks(same, start, stop, lags, width):
    return [
        None if lag == 0 else jnp.broadcast_to(same[start:stop, lag : lag + 1], (stop - start, width))
        for lag in range(lags)
    ]


def conv_rows(same, start, stop, taps, columns, wide, masks=None):
    if masks is None:
        masks = lag_masks(same, start, stop, taps.shape[0], wide.shape[1])
    total = taps[0:1, columns] * wide[8 + start : 8 + stop, :]
    for lag in range(1, taps.shape[0]):
        total = total + taps[lag : lag + 1, columns] * (
            wide[8 + start - lag : 8 + stop - lag, :] * masks[lag]
        )
    return (0.5 * total * (1.0 + jnp.tanh(0.5 * total))).astype(BF16)


def write_info(ref, normal, stab, decay):
    lines = [p[:, c : c + 128] for p in split3(normal) for c in range(0, normal.shape[1], 128)]
    lines += [jnp.broadcast_to(p, (1, 128)) for x in (stab, decay) for p in split3(x)]
    row = iota((INFO, 128), 0)
    block = jnp.zeros((INFO, 128), F32)
    for i, line in enumerate(lines):
        block = jnp.where(row == i, line, block)
    ref[ref.shape[0] - INFO :, :] = block.astype(BF16)


def read_info(ref, key_width=256):
    b = ref[ref.shape[0] - INFO :, :].astype(F32)
    k = key_width // 128
    normal = jnp.concatenate(
        [b[i : i + 1] + b[i + k : i + k + 1] + b[i + 2 * k : i + 2 * k + 1] for i in range(k)],
        axis=1,
    )
    sums = [b[i : i + 1] + b[i + 1 : i + 2] + b[i + 2 : i + 3] for i in (3 * k, 3 * k + 3)]
    return normal, sums[0][:, 0:1], sums[1][:, 0:1]


def half_columns(core, width):
    return pl.ds(pl.multiple_of(core * width, 128), width)


def gates_kernel(
    input_ref, forget_ref, key_ref, value_ref, gate_ref, key_send, send_ref, sems
):
    core, _ = core_place()
    width = key_send.shape[1]
    columns = half_columns(1 - core, width) if key_ref.shape[1] > width else pl.ds(0, width)
    copies = start_copies(
        sems,
        [
            (key_ref.at[:, columns], key_send),
            (value_ref.at[:, half_columns(1 - core, send_ref.shape[1])], send_ref),
            (input_ref, gate_ref.at[0]),
            (forget_ref, gate_ref.at[1]),
        ],
    )
    for copy in copies:
        copy.wait()


def own_kernel_parts(key_ref, value_ref, taps_ref, keys, values, taps, sems):
    core, _ = core_place()
    width = keys.shape[1]
    columns = half_columns(core, width) if key_ref.shape[1] > width else pl.ds(0, width)
    copies = start_copies(
        sems,
        [
            (key_ref.at[:, columns], keys),
            (value_ref.at[:, half_columns(core, values.shape[1])], values),
            (taps_ref.at[1, :, columns], taps),
        ],
    )
    for copy in copies:
        copy.wait()


def chip_kernel(
    per_core, lengths_ref, own_keys, own_values, key_other, value_other, gates_ref, gates_other,
    taps,
    conv_ref, gate_ref, key_edge, levels_first, out0, out1, out2, out3,
    raw, picked, wide, weighted_ref, whole, normals, levels,
):
    core, mine = core_place()
    rows, width = own_keys.shape
    length = 2 * rows
    key_width = width // per_core
    value_width = own_values.shape[1] // per_core
    own_rows = pl.ds(pl.multiple_of(core * rows, rows), rows)
    other_rows = pl.ds(pl.multiple_of((1 - core) * rows, rows), rows)
    offset = lax.axis_index("seq") // 2 * length
    gate, cumulative = gate_rows(core, per_core, (gates_ref, gates_other), raw, picked)
    gate_ref[0] = gate
    gate_ref[1] = cumulative
    segment = segment_of(lengths_ref, offset + iota((1, length), 1))
    last = segment_of(lengths_ref, jnp.full((1, 1), offset + length - 1, jnp.int32))
    before = segment_of(lengths_ref, jnp.full((1, 1), offset - 1, jnp.int32))
    total = cumulative[:, length - 1 : length]
    tail_weight = jnp.where(segment == last, gate + total - cumulative, very_negative)
    stab = jnp.max(tail_weight, axis=1, keepdims=True)
    factor = jnp.exp(tail_weight - stab).T
    levels[0] = jnp.broadcast_to(stab, (8, 128))
    through = jnp.where(before == last, total, very_negative)
    levels[1] = jnp.broadcast_to(through, (8, 128))
    levels_first[0] = tail_weight[:, 0:128]
    levels_first[1] = levels[1]
    same = same_request(lengths_ref, offset + iota((length, 128), 0))
    normals[...] = jnp.zeros_like(normals)
    step = 128
    key_edge[0] = jnp.where(core == 0, own_keys[0:16, :], key_other[0:16, :])
    key_edge[1] = jnp.where(core == 0, key_other[rows - 16 :, :], own_keys[rows - 16 :, :])
    for i in range(per_core):
        columns = slice(i * key_width, (i + 1) * key_width)
        wide[i, 0:8, :] = jnp.zeros((8, key_width), F32)
        for ref, half in ((own_keys, core), (key_other, 1 - core)):
            span = pl.ds(pl.multiple_of(8 + half * rows, 8), rows)
            wide[i, span, :] = ref[:, columns].astype(F32)
    totals = [jnp.zeros((1, key_width), F32) for _ in range(per_core)]
    for start in range(0, length, step):
        masks = lag_masks(same, start, start + step, taps.shape[0], key_width)
        for i in range(per_core):
            columns = slice(i * key_width, (i + 1) * key_width)
            conv = conv_rows(same, start, start + step, taps, columns, wide.at[i], masks)
            conv_ref[start : start + step, columns] = conv
            weight = factor[start : start + step, i : i + 1]
            if start == 0:
                weight = jnp.where(iota((step, 1), 0) >= FIRST, weight, 0.0)
            weighted = conv.astype(F32) * weight
            totals[i] = totals[i] + jnp.sum(weighted, axis=0, keepdims=True)
            weighted_ref[start : start + step, columns] = weighted.astype(BF16)
    for i in range(per_core):
        normals[i : i + 1, :] = totals[i]
    for i in range(per_core):
        columns = slice(i * key_width, (i + 1) * key_width)
        value_columns = slice(i * value_width, (i + 1) * value_width)
        whole[columns, :] = sum(
            dot(weighted_ref[part, columns], ref[:, value_columns], ((0,), (0,)))
            for part, ref in ((own_rows, own_values), (other_rows, value_other))
        ).astype(BF16)
    rows = width // 4
    for off, out in enumerate((out0, out1, out2, out3)):
        piece = piece_of(mine, off)
        content = whole[pl.ds(pl.multiple_of(piece * rows, rows), rows), :]
        for j in range(value_width // 128):
            out[j * rows : (j + 1) * rows, :] = content[:, j * 128 : (j + 1) * 128]
        head = piece // (key_width // rows)
        write_info(
            out,
            normals[pl.ds(head, 1), :],
            levels[0, pl.ds(head, 1), :][:, 0:1],
            levels[1, pl.ds(head, 1), :][:, 0:1],
        )


def message_kernel(
    per_core, query_ref, query_other, key_edge, own_values, value_other, levels_first,
    out_ref, rows_ref, tail, sems,
):
    core, _ = core_place()
    width = key_edge.shape[2]
    split = query_ref.shape[1] > width
    columns = pl.ds(pl.multiple_of(core * width, 128) if split else 0, width)
    last = pl.ds(query_ref.shape[0] - 16, 16)
    for ref, here in ((query_ref, core == 1), (query_other, core == 0)):

        def fetch(ref=ref):
            copy = pltpu.make_async_copy(ref.at[last, columns], tail, sems.at[0])
            copy.start()
            copy.wait()

        pl.when(here)(fetch)
    rows_ref[...] = jnp.zeros_like(rows_ref)
    at = 0
    for block in (
        key_edge[0].astype(F32)[0:FIRST],
        jnp.where(core == 0, own_values[0:16, :], value_other[0:16, :]).astype(F32)[0:FIRST],
        key_edge[1].astype(F32)[16 - FIRST :],
        tail[...].astype(F32)[16 - FIRST :],
    ):
        for j in range(block.shape[1] // 128):
            rows_ref[at : at + FIRST, :] = block[:, j * 128 : (j + 1) * 128]
            at += FIRST
    lane, span = iota((1, 128), 1), 64 // per_core
    line = jnp.zeros((1, 128), F32)
    for i in range(per_core):
        ends, decay = levels_first[0, i : i + 1, :], levels_first[1, i : i + 1, :]
        if i > 0:
            ends = pltpu.roll(ends, i * span, 1)
        line = jnp.where((lane >= i * span) & (lane < (i + 1) * span), ends, line)
        line = jnp.where((lane >= 64 + i * span) & (lane < 64 + (i + 1) * span), decay, line)
    for p, part in enumerate(split3(line)):
        rows_ref[at + p : at + p + 1, :] = part
    out_ref[0] = rows_ref[...].astype(BF16)


def join_kernel(first_ref, second_ref, out_ref):
    count = first_ref.shape[0]
    out_ref[0:count] = first_ref[...]
    out_ref[count:] = second_ref[...]


def gathered_kernel(
    per_core, length, offsets, lengths_ref, near_ref, far_ref, taps, key_edge,
    query_taps, query_edge,
    keys_ref, values_ref, levels_ref, conv_ref, by_chip, wide, value_rows, level_rows, narrow,
):
    half = near_ref.shape[0]
    chips = 2 * half
    me = lax.axis_index("seq") // 2
    width = key_edge.shape[2]
    key_width = width // per_core
    value_width = values_ref.shape[1]
    key_blocks, value_blocks = key_width // 128, value_width // 128
    for k, off in enumerate(offsets):
        message = near_ref[k] if k < half else far_ref[k - half]
        by_chip[lax.bitwise_xor(me, off)] = message.astype(F32)
    row = iota((16 * chips, 128), 0)
    position = length * lax.shift_right_logical(row, 4) + lax.bitwise_and(row, 15) - 8
    same = same_request(lengths_ref, position)
    value_rows[...] = jnp.zeros_like(value_rows)
    level_rows[...] = jnp.full_like(level_rows, 2 * very_negative)
    values_at = FIRST * per_core * key_blocks
    tails_at = values_at + FIRST * per_core * value_blocks
    levels_at = tails_at + 2 * FIRST * per_core * key_blocks
    span = 64 // per_core
    lines = [
        sum(by_chip[g, levels_at + p : levels_at + p + 1, :] for p in range(3))
        for g in range(chips)
    ]
    square = iota((FIRST, 128), 0) == iota((FIRST, 128), 1)
    for i in range(per_core):
        wide[...] = jnp.zeros_like(wide)
        since = jnp.zeros((1, 1), F32)
        for g in reversed(range(chips)):
            at = 16 * g + 8
            for j in range(key_blocks):
                columns = slice(j * 128, (j + 1) * 128)
                source = FIRST * (i * key_blocks + j)
                wide[8 + at : 8 + at + FIRST, columns] = by_chip[g, source : source + FIRST, :]
                if g > 0:
                    source += tails_at
                    wide[8 + at - FIRST : 8 + at, columns] = by_chip[
                        g - 1, source : source + FIRST, :
                    ]
            for j in range(value_blocks):
                source = values_at + FIRST * (i * value_blocks + j)
                value_rows[i * 16 * chips + at : i * 16 * chips + at + FIRST, j * 128 : (j + 1) * 128] = (
                    by_chip[g, source : source + FIRST, :]
                )
            ends = lines[g]
            if i > 0:
                ends = pltpu.roll(ends, 128 - i * span, 1)
            ends = jnp.where(g < me, ends + since, 2 * very_negative)
            decay = lines[g][:, 64 + i * span : 64 + i * span + 1]
            since = since + jnp.where(g < me, decay, 0.0)
            column = jnp.sum(jnp.where(square, ends, 0.0), axis=1, keepdims=True)
            level_rows[i * 16 * chips + at : i * 16 * chips + at + FIRST, :] = jnp.broadcast_to(
                column, (FIRST, 128)
            )
        keys_ref[i * 16 * chips : (i + 1) * 16 * chips, :] = conv_rows(
            same, 0, 16 * chips, taps, slice(i * key_width, (i + 1) * key_width), wide
        )
    values_ref[...] = value_rows[...].astype(BF16)
    levels_ref[...] = level_rows[...]
    same = same_request(lengths_ref, me * length + iota((16, 128), 0))
    previous = jnp.maximum(me - 1, 0)
    for which, (weights, edge) in enumerate(((query_taps, query_edge), (taps, key_edge))):
        for i in range(per_core):
            columns = slice(i * key_width, (i + 1) * key_width)
            for j in range(key_blocks):
                source = tails_at + FIRST * ((1 - which) * per_core + i) * key_blocks + FIRST * j
                narrow[8 - FIRST : 8, j * 128 : (j + 1) * 128] = by_chip[
                    previous, source : source + FIRST, :
                ]
            narrow[8:, :] = edge[0, :, columns].astype(F32)
            conv_ref[which, :, columns] = conv_rows(same, 0, 16, weights, columns, narrow)


def shifted_stab(infos, ranks, upto):
    out = []
    for i, (_, stab, _) in enumerate(infos):
        for j, (_, _, decay) in enumerate(infos):
            if i != j:
                inside = (ranks[j] > ranks[i]) & (ranks[j] < upto)
                stab = stab + jnp.where(inside, decay, 0.0)
        out.append(stab)
    return out


def total_kernel(*refs):
    *states, out = refs
    rows = out.shape[0] - INFO
    _, mine = core_place()
    ranks = [lax.bitwise_xor(mine, off) for off in range(4)]
    infos = [read_info(s) for s in states]
    stabs = shifted_stab(infos, ranks, 4)
    m = functools.reduce(jnp.maximum, stabs)
    weights = [jnp.exp(s - m) for s in stabs]
    out[0:rows, :] = sum(w * s[0:rows, :].astype(F32) for w, s in zip(weights, states)).astype(BF16)
    write_info(out, sum(w * i[0] for w, i in zip(weights, infos)), m, sum(i[2] for i in infos))


def is_later(bit):
    return lax.rem(lax.shift_right_logical(lax.axis_index("seq"), bit), 2) == 1


def round_kernel(bit, first, *refs):
    if first:
        total_ref, got_ref, prefix_out, total_out = refs
    else:
        prefix_ref, total_ref, got_ref, prefix_out, total_out = refs
    rows = total_ref.shape[0] - INFO
    later = is_later(bit)
    n_t, m_t, d_t = read_info(total_ref)
    n_g, m_g, d_g = read_info(got_ref)
    here, got = total_ref[0:rows, :].astype(F32), got_ref[0:rows, :].astype(F32)
    a_t = m_t + jnp.where(later, 0.0, d_g)
    a_g = m_g + jnp.where(later, d_t, 0.0)
    m = jnp.maximum(a_t, a_g)
    w_t, w_g = jnp.exp(a_t - m), jnp.exp(a_g - m)
    total_out[0:rows, :] = (w_t * here + w_g * got).astype(BF16)
    write_info(total_out, w_t * n_t + w_g * n_g, m, d_t + d_g)
    if first:
        n_p, m_p, d_p = jnp.zeros_like(n_g), jnp.full_like(m_g, very_negative), jnp.zeros_like(d_g)
        prefix = jnp.zeros_like(got)
    else:
        n_p, m_p, d_p = read_info(prefix_ref)
        prefix = prefix_ref[0:rows, :].astype(F32)
    a_g = jnp.where(later, m_g + d_p, 2 * very_negative)
    m = jnp.maximum(m_p, a_g)
    w_p = jnp.exp(m_p - m)
    w_g = jnp.where(later, jnp.exp(a_g - m), 0.0)
    prefix_out[0:rows, :] = (w_p * prefix + w_g * got).astype(BF16)
    write_info(prefix_out, w_p * n_p + w_g * n_g, m, d_p + jnp.where(later, d_g, 0.0))


def enter_kernel(bit, prefix_ref, *refs):
    states, outs = refs[:4], refs[4:]
    rows = outs[0].shape[0] - INFO
    _, mine = core_place()
    ranks = [lax.bitwise_xor(mine, off) for off in range(4)]
    infos = [read_info(s) for s in states]
    n_p, m_p, _ = read_info(prefix_ref)
    valid = True if bit is None else is_later(bit)
    weights = []
    for off, out in enumerate(outs):
        stabs = shifted_stab(infos, ranks, ranks[off])
        m_in = m_p
        for info, rank in zip(infos, ranks):
            m_in = m_in + jnp.where(rank < ranks[off], info[2], 0.0)
        m_in = jnp.where(valid, m_in, very_negative)
        stabs = [
            jnp.where(rank < ranks[off], s, 2 * very_negative) for s, rank in zip(stabs, ranks)
        ]
        m = functools.reduce(jnp.maximum, stabs, m_in)
        mine_in = [jnp.where(valid, jnp.exp(m_in - m), 0.0)] + [
            jnp.where(rank < ranks[off], jnp.exp(s - m), 0.0) for s, rank in zip(stabs, ranks)
        ]
        weights.append(mine_in)
        normals = [n_p] + [info[0] for info in infos]
        write_info(out, sum(w * n for w, n in zip(mine_in, normals)), m, jnp.zeros_like(m))
    step = math.gcd(rows, 64)
    for at in range(0, rows, step):
        parts = [r[at : at + step, :].astype(F32) for r in (prefix_ref, *states)]
        for off, out in enumerate(outs):
            out[at : at + step, :] = sum(
                w * part
                for k, (w, part) in enumerate(zip(weights[off], parts))
                if k != off + 1
            ).astype(BF16)


def query_kernel(
    per_core, lengths_ref, query_ref, query_other, taps_ref, own_values, value_other,
    conv_ref, taps, edge_ref, values, queries, wide, sems,
):
    core, _ = core_place()
    length, width = queries.shape
    key_width = width // per_core
    split = query_ref.shape[1] > width
    columns = pl.ds(pl.multiple_of(core * width, 128) if split else 0, width)
    copies = start_copies(
        sems,
        [(taps_ref.at[0, :, columns], taps)]
        + by_core(core, query_ref, query_other, columns, queries)
        + by_core(core, own_values, value_other, slice(None), values),
    )
    offset = lax.axis_index("seq") // 2 * length
    same = same_request(lengths_ref, offset + iota((length, 128), 0))
    for copy in copies:
        copy.wait()
    edge_ref[0] = queries[0:16, :]
    edge_ref[1] = queries[length - 16 :, :]
    for i in range(per_core):
        here = slice(i * key_width, (i + 1) * key_width)
        wide[0:8, :] = jnp.zeros((8, key_width), F32)
        wide[8:, :] = queries[:, here].astype(F32)
        for start in range(0, length, 128):
            conv_ref[start : start + 128, here] = conv_rows(
                same, start, start + 128, taps, here, wide
            )


def intra_kernel(
    per_core, lengths_ref, query_conv, key_ref, conv_first, values, gate_ref,
    query_ref, numerator_ref, stats_ref, keys,
):
    length, width = query_ref.shape
    key_width = width // per_core
    value_width = values.shape[1] // per_core
    key_scale = 1.0 / math.sqrt(key_width)
    offset = lax.axis_index("seq") // 2 * length
    query_ref[...] = query_conv[...]
    query_ref[0:16, :] = conv_first[0]
    keys[...] = key_ref[...]
    keys[0:16, :] = conv_first[1]
    gate, cumulative = gate_ref[0], gate_ref[1]
    by_token = cumulative.T
    segment = segment_of(lengths_ref, offset + iota((length, 1), 0))
    segment_row = segment_of(lengths_ref, offset + iota((1, length), 1))
    before = segment_of(lengths_ref, jnp.full((1, 1), offset - 1, jnp.int32))
    step = length // 2
    lane = iota((step, 128), 1)
    stats = [[jnp.zeros((step, 128), F32)] * 3 for _ in range(2)]
    for i in range(per_core):
        here = slice(i * key_width, (i + 1) * key_width)
        value_columns = slice(i * value_width, (i + 1) * value_width)
        for b in range(2):
            rows, stop = slice(b * step, (b + 1) * step), (b + 1) * step
            allowed = segment_row[:, 0:stop] == segment[rows]
            allowed &= iota((step, stop), 1) <= iota((step, stop), 0) + b * step
            total = by_token[rows, i : i + 1]
            log_weight = jnp.where(
                allowed,
                gate[i : i + 1, 0:stop] - cumulative[i : i + 1, 0:stop] + total,
                very_negative,
            )
            row_max = jnp.max(log_weight, axis=1, keepdims=True)
            scores = dot(query_ref[rows, here], keys[0:stop, here], ((1,), (1,))) * key_scale
            weights = scores * jnp.exp(log_weight - row_max)
            numerator_ref[rows, value_columns] = dot(
                weights.astype(BF16), values[0:stop, value_columns]
            )
            linked = jnp.where(segment[rows] == before, total, very_negative)
            found = (jnp.sum(weights, axis=1, keepdims=True), row_max, linked)
            stats[b] = [jnp.where(lane == i, new, old) for new, old in zip(found, stats[b])]
    for b in range(2):
        for k in range(3):
            stats_ref[k, b * step : (b + 1) * step, :] = stats[b][k]


def head_rows(
    per_core, start, memory, parts, stabs, query_ref, numerator_ref, stats_ref, out_ref
):
    step = out_ref.shape[0]
    key_width = query_ref.shape[1] // per_core
    value_width = memory.shape[1]
    key_scale = 1.0 / math.sqrt(key_width)
    span = pl.ds(pl.multiple_of(start, step), step)
    queries = [query_ref[span, i * key_width : (i + 1) * key_width] for i in range(per_core)]
    from_normal = sum(
        dot(q, parts[i * 128 : (i + 1) * 128, :], ((1,), (1,))) for i, q in enumerate(queries)
    )
    from_normal = (
        from_normal
        + pltpu.roll(from_normal, 128 - 8, 1)
        + pltpu.roll(from_normal, 128 - 16, 1)
    )
    row_max = stats_ref[1, span, :]
    carried = stabs[0:1, :] + stats_ref[2, span, :]
    m = jnp.maximum(row_max, carried)
    w_here = jnp.exp(row_max - m)
    w_in = jnp.exp(carried - m) * key_scale
    denominator = w_here * stats_ref[0, span, :] + w_in * from_normal
    scale = 1.0 / jnp.maximum(jnp.abs(denominator), 1.0)
    w_here, w_in = w_here * scale, w_in * scale
    for i in range(per_core):
        columns = slice(i * value_width, (i + 1) * value_width)
        from_memory = dot(queries[i], memory[i * key_width : (i + 1) * key_width, :])
        out_ref[:, columns] = (
            w_here[:, i : i + 1] * numerator_ref[span, columns] + w_in[:, i : i + 1] * from_memory
        ).astype(BF16)


def head_send_kernel(
    per_core, own_ref, got1, got2, got3, keys_ref, values_ref, levels_ref,
    query_ref, numerator_ref, stats_ref, send_ref, memory, parts, stabs, info,
):
    core, mine = core_place()
    key_width = query_ref.shape[1] // per_core
    value_width = memory.shape[1]
    rows = query_ref.shape[1] // 4
    for off, ref in enumerate((own_ref, got1, got2, got3)):
        piece = piece_of(mine, off)
        start = pl.multiple_of(piece * rows, rows)
        for j in range(value_width // 128):
            memory[pl.ds(start, rows), j * 128 : (j + 1) * 128] = ref[j * rows : (j + 1) * rows, :]
        info[piece] = ref[ref.shape[0] - INFO :, :]
    count = keys_ref.shape[0] // per_core
    row, lane = iota((128, key_width), 0), iota((1, 128), 1)
    levels = jnp.full((1, 128), very_negative, F32)
    for i in range(per_core):
        normal, stab, _ = read_info(info.at[i * key_width // rows], key_width)
        here = slice(i * key_width, (i + 1) * key_width)
        extra = slice(i * count, (i + 1) * count)
        weighted = keys_ref[extra, :].astype(F32) * jnp.exp(levels_ref[extra, 0:1] - stab)
        normal = normal + jnp.sum(weighted, axis=0, keepdims=True)
        memory[here, :] = (
            memory[here, :].astype(F32)
            + dot(weighted.astype(BF16), values_ref[extra, :], ((0,), (0,)))
        ).astype(BF16)
        levels = jnp.where(lane == i, stab, levels)
        block = jnp.zeros((128, key_width), F32)
        for k, part in enumerate(split3(normal)):
            block = jnp.where(row == 8 * k + i, part, block)
        parts[i * 128 : (i + 1) * 128, :] = block.astype(BF16)
    stabs[...] = jnp.broadcast_to(levels, stabs.shape)
    start = (1 - core) * send_ref.shape[0]
    head_rows(
        per_core, start, memory, parts, stabs, query_ref, numerator_ref, stats_ref, send_ref
    )


def head_keep_kernel(
    per_core, memory, parts, stabs, query_ref, numerator_ref, stats_ref, keep_ref
):
    core, _ = core_place()
    start = core * keep_ref.shape[0]
    head_rows(
        per_core, start, memory, parts, stabs, query_ref, numerator_ref, stats_ref, keep_ref
    )


def weight_part(weight_ref, half, rows, start, width):
    return weight_ref[
        pl.ds(pl.multiple_of(half * rows, 128), rows), pl.ds(pl.multiple_of(start, 128), width)
    ]


def keep_kernel(off, head_ref, weight_ref, part_ref):
    core, _ = core_place()
    rows, width = head_ref.shape[1], part_ref.shape[1]
    start = lax.bitwise_xor(lax.axis_index("head"), off) * width
    part_ref[...] = dot(head_ref[...], weight_part(weight_ref, core, rows, start, width))


def send_kernel(off, chunk, head_ref, weight_ref, kept_ref, part_ref):
    core, _ = core_place()
    rows, piece, width = head_ref.shape[1], part_ref.shape[1], kept_ref.shape[1]
    start = lax.bitwise_xor(lax.axis_index("head"), off) * width + chunk * piece
    part_ref[...] = (
        dot(head_ref[...], weight_part(weight_ref, 1 - core, rows, start, piece))
        + kept_ref[:, chunk * piece : (chunk + 1) * piece]
    ).astype(part_ref.dtype)


def own_kernel(keep_ref, got_ref, weight_ref, part_ref):
    core, _ = core_place()
    rows, width = keep_ref.shape[1], part_ref.shape[1]
    start = lax.axis_index("head") * width
    part_ref[...] = dot(
        keep_ref[...], weight_part(weight_ref, core, rows, start, width)
    ) + dot(got_ref[...], weight_part(weight_ref, 1 - core, rows, start, width))


def sum_kernel(chunk, count, own_ref, *refs):
    arrived, (out_ref, held, sems) = refs[:count], refs[-3:]
    width = held.shape[1]
    columns = pl.ds(chunk * width, width)
    parts = sems.shape[0]
    step = own_ref.shape[0] // parts
    copies = []
    for part in range(parts):
        rows = slice(part * step, (part + 1) * step)
        total = own_ref[rows, chunk * width : (chunk + 1) * width]
        for ref in arrived:
            total = total + ref[rows, :].astype(F32)
        held[rows, :] = total.astype(held.dtype)
        span = pl.ds(part * step, step)
        copies.append(
            pltpu.make_async_copy(held.at[span, :], out_ref.at[span, columns], sems.at[part])
        )
        copies[-1].start()
    for copy in copies:
        copy.wait()


def call(kernel, out_shape, spaces, scratch, name, flops=0, nbytes=0, limit=24, out=pltpu.VMEM,
         aliases=None):
    place = {"v": pltpu.VMEM, "s": pltpu.SMEM, "a": pl.ANY, "h": pl.ANY}
    outs = jax.tree.map(lambda _: pl.BlockSpec(memory_space=out), out_shape)
    inner = pl.pallas_call(
        kernel,
        out_shape=out_shape,
        in_specs=[pl.BlockSpec(memory_space=place[s]) for s in spaces],
        out_specs=outs,
        scratch_shapes=scratch,
        compiler_params=pltpu.CompilerParams(vmem_limit_bytes=limit << 20),
        cost_estimate=pl.CostEstimate(flops=flops, bytes_accessed=nbytes, transcendentals=0),
        name=name,
        input_output_aliases=aliases or {},
    )

    def run(*args):
        return inner(
            *(
                pltpu.with_memory_space_constraint(x, pltpu.HBM) if s in "hs" else x
                for s, x in zip(spaces, args, strict=True)
            )
        )

    return run


def on_device(
    query_input, key_input, value_input, kernel_taps, input_gate, forget_gate, request_lengths,
    output_weight,
):
    seq_count, head_count = lax.axis_size("seq"), lax.axis_size("head")
    length, key_cols = query_input.shape
    heads = input_gate.shape[0]
    value_cols = value_input.shape[1]
    out_cols = output_weight.shape[1] // head_count
    chip_length = 2 * length
    key_width = key_cols // heads
    per_core = max(1, heads // 2)
    part_keys, part_values = per_core * key_width, value_cols // 2
    value_width = part_values // per_core
    lags = kernel_taps.shape[1]
    rows = part_keys // 4

    def shape(dims, dtype=F32):
        return jax.ShapeDtypeStruct(dims, dtype)

    def swap(x, off):
        return lax.ppermute(x, "seq", [(i, i ^ off) for i in range(seq_count)])

    gates, key_send, value_send = call(
        gates_kernel,
        (
            shape((2, heads, length)),
            shape((length, part_keys), BF16),
            shape((length, part_values), BF16),
        ),
        "hhhh", [pltpu.SemaphoreType.DMA((4,))], "gates", flops=4 << 30,
    )(input_gate, forget_gate, key_input, value_input)
    gates_other, key_other, value_other = swap(gates, 1), swap(key_send, 1), swap(value_send, 1)
    key_after, value_after, gates = lax.optimization_barrier((key_input, value_input, gates))
    own_keys, own_values, taps = call(
        own_kernel_parts,
        (
            shape((length, part_keys), BF16),
            shape((length, part_values), BF16),
            shape((lags, part_keys)),
        ),
        "hhh", [pltpu.SemaphoreType.DMA((3,))], "own_part", flops=4 << 30,
    )(key_after, value_after, kernel_taps)
    query_after, gates = lax.optimization_barrier((query_input, gates))
    query_other = swap(query_after, 1)

    one = shape((rows * value_width // 128 + INFO, 128), BF16)
    key_conv, gate_sums, key_edge, levels, *pieces = call(
        functools.partial(chip_kernel, per_core),
        (
            shape((chip_length, part_keys), BF16),
            shape((2, 8, chip_length)),
            shape((2, 16, part_keys), BF16),
            shape((2, 8, 128)),
        )
        + (one,) * 4,
        "s" + "v" * 7,
        [
            pltpu.VMEM((2, max(8, heads), chip_length), F32),
            pltpu.VMEM((2, 8, chip_length), F32),
            pltpu.VMEM((per_core, chip_length + 8, key_width), F32),
            pltpu.VMEM((chip_length, part_keys), BF16),
            pltpu.VMEM((part_keys, value_width), BF16),
            pltpu.VMEM((8, key_width), F32),
            pltpu.VMEM((2, 8, 128), F32),
        ],
        "chip_state",
        flops=1 << 30,
    )(
        request_lengths, own_keys, own_values, key_other, value_other, gates, gates_other, taps
    )
    states = [pieces[0]] + [swap(pieces[off], 2 * off) for off in (1, 2, 3)]

    count = 16 * seq_count // 2
    lines = FIRST * per_core * (3 * key_width + value_width) // 128 + 3
    lines = -(-lines // 16) * 16
    message = call(
        functools.partial(message_kernel, per_core), shape((1, lines, 128), BF16), "havvvv",
        [
            pltpu.VMEM((lines, 128), F32),
            pltpu.VMEM((16, part_keys), BF16),
            pltpu.SemaphoreType.DMA((1,)),
        ],
        "message",
    )(query_input, query_other, key_edge, own_values, value_other, levels)
    bits = seq_count.bit_length() - 1
    steps = [4, 2, 8] if bits == 4 else [1 << b for b in range(1, bits)]
    near, far, offsets = message, swap(message, steps[0]), [0, steps[0] // 2]
    query_conv, query_taps, query_edge, values = call(
        functools.partial(query_kernel, per_core),
        (
            shape((chip_length, part_keys), BF16),
            shape((lags, part_keys)),
            shape((2, 16, part_keys), BF16),
            shape((chip_length, part_values), BF16),
        ),
        "shahvv",
        [
            pltpu.VMEM((chip_length, part_keys), BF16),
            pltpu.VMEM((chip_length + 8, key_width), F32),
            pltpu.SemaphoreType.DMA((5,)),
        ],
        "query_conv",
        flops=1 << 30,
    )(request_lengths, query_input, query_other, kernel_taps, own_values, value_other)
    states, query_conv, far = lax.optimization_barrier((states, query_conv, far))
    total = call(total_kernel, one, "vvvv", [], "group_total")(*states)
    flag = 3
    prefix = swap(total, 12 if bits == 4 else 8)
    near, far, total = lax.optimization_barrier((near, far, total))
    for step in steps[1:]:
        near = call(
            join_kernel, shape((2 * near.shape[0], lines, 128), BF16), "vv", [], "join"
        )(near, far)
        far = swap(near, step)
        offsets = offsets + [off ^ (step // 2) for off in offsets]
    if bits > 4:
        flag = None
        prefix, total = call(
            functools.partial(round_kernel, 3, True), (one, one), "vv", [], "round_state"
        )(total, prefix)
        for bit in range(4, bits):
            prefix, total = call(
                functools.partial(round_kernel, bit, False), (one, one), "vvv", [], "round_state"
            )(prefix, total, swap(total, 1 << bit))
    enter = call(functools.partial(enter_kernel, flag), (one,) * 4, "vvvvv", [], "enter_state")(
        prefix, *states
    )
    gate_sums, near, *enter = lax.optimization_barrier((gate_sums, near, *enter))
    enter = [enter[0]] + [swap(enter[off], 2 * off) for off in (1, 2, 3)]
    *extras, conv_first = call(
        functools.partial(gathered_kernel, per_core, chip_length, tuple(offsets)),
        (
            shape((per_core * count, key_width), BF16),
            shape((per_core * count, value_width), BF16),
            shape((per_core * count, 128)),
            shape((2, 16, part_keys), BF16),
        ),
        "svvvvvv",
        [
            pltpu.VMEM((seq_count // 2, lines, 128), F32),
            pltpu.VMEM((count + 8, key_width), F32),
            pltpu.VMEM((per_core * count, value_width), F32),
            pltpu.VMEM((per_core * count, 128), F32),
            pltpu.VMEM((24, key_width), F32),
        ],
        "gathered_first",
    )(request_lengths, near, far, taps, key_edge, query_taps, query_edge)
    inside = call(
        functools.partial(intra_kernel, per_core),
        (
            shape((chip_length, part_keys), BF16),
            shape((chip_length, part_values)),
            shape((3, chip_length, 128)),
        ),
        "svvvvv",
        [pltpu.VMEM((chip_length, part_keys), BF16)],
        "intra",
        flops=4 << 30,
    )(request_lengths, query_conv, key_conv, conv_first, values, gate_sums)
    half_out = shape((length, part_values), BF16)
    send, *entered = call(
        functools.partial(head_send_kernel, per_core),
        (
            half_out,
            shape((part_keys, value_width), BF16),
            shape((128 * per_core, key_width), BF16),
            shape((8, 128)),
        ),
        "v" * 10, [pltpu.VMEM((4, INFO, 128), BF16)], "head_send",
    )(*enter, *extras, *inside)
    keep = call(
        functools.partial(head_keep_kernel, per_core), half_out, "v" * 6, [], "head_keep",
        flops=1 << 30,
    )(*entered, *inside)
    got = swap(send, 1)

    chunks = 2 if head_count == 2 and out_cols % 256 == 0 else 1
    piece = out_cols // chunks
    arrived = []
    mixed = call(
        own_kernel, shape((length, out_cols)), "vvv", [], "project_own", flops=4 << 30
    )(keep, got, output_weight)
    for off in range(1, head_count):
        kept = call(
            functools.partial(keep_kernel, off), shape((length, out_cols)), "vv", [],
            "project_kept", flops=2 << 30,
        )(keep, output_weight)
        columns, after = [], got
        for chunk in range(chunks):
            part = call(
                functools.partial(send_kernel, off, chunk), shape((length, piece), BF16), "vvv",
                [], "project_other",
            )(after, output_weight, kept)
            columns.append(
                lax.ppermute(part, "head", [(i, i ^ off) for i in range(head_count)])
            )
            after, mixed = lax.optimization_barrier((got, mixed))
        arrived.append(columns)
    out = []
    for chunk in range(chunks):
        out = [
            call(
                functools.partial(sum_kernel, chunk, len(arrived)),
                shape((length, out_cols), BF16),
                "v" * (1 + len(arrived)) + "a" * len(out),
                [pltpu.VMEM((length, piece), BF16), pltpu.SemaphoreType.DMA((2,))],
                "mixed_out", out=pl.ANY, aliases={1 + len(arrived): 0} if out else None,
            )(mixed, *(columns[chunk] for columns in arrived), *out)
        ]
    return out[0]


def solution(mesh):
    placed = (
        P("seq", "head"),
        P("seq", "head"),
        P("seq", "head"),
        P(None, None, "head"),
        P("head", "seq"),
        P("head", "seq"),
        P(),
        P("head", None),
    )
    return jax.shard_map(
        on_device, mesh=mesh, in_specs=placed, out_specs=P("seq", "head"), check_vma=False
    )
```

```python
import functools
import math

import jax
import jax.numpy as jnp
from jax import lax
from jax.experimental import pallas as pl
from jax.experimental.pallas import tpu as pltpu
from jax.sharding import PartitionSpec as P

very_negative = -1e30
FIRST = 3
INFO = 16
TAIL = 16
BF16 = jnp.bfloat16
F32 = jnp.float32


def iota(shape, dim):
    return lax.broadcasted_iota(jnp.int32, shape, dim)


def dot(a, b, contract=((1,), (0,))):
    return lax.dot_general(a, b, (contract, ((), ())), preferred_element_type=F32)


def split3(x):
    high = x.astype(BF16).astype(F32)
    rest = x - high
    mid = rest.astype(BF16).astype(F32)
    return high, mid, (rest - mid).astype(BF16).astype(F32)


def segment_of(lengths_ref, position):
    start = jnp.int32(0)
    count = jnp.zeros_like(position)
    for r in range(lengths_ref.shape[0]):
        count = count + (start <= position).astype(jnp.int32)
        start = start + lengths_ref[r]
    return count - 1


def core_place():
    place = lax.axis_index("seq")
    return lax.rem(place, 2), lax.rem(place // 2, 4)


def piece_of(mine, off):
    piece = lax.bitwise_xor(mine, off)
    if lax.axis_size("seq") == 16:
        piece = lax.bitwise_xor(piece, lax.axis_index("seq") // 8 * 2)
    return piece


def start_copies(sems, pairs):
    copies = [pltpu.make_async_copy(a, b, sems.at[i]) for i, (a, b) in enumerate(pairs)]
    for copy in copies:
        copy.start()
    return copies


def by_core(core, own_ref, other_ref, columns, held):
    rows = own_ref.shape[0]
    return [
        (ref.at[:, columns], held.at[pl.ds(pl.multiple_of(half * rows, rows), rows), :])
        for ref, half in ((own_ref, core), (other_ref, 1 - core))
    ]


def gate_rows(core, per_core, gates, raw, picked):
    _, heads, length = gates[0].shape
    for ref, half in ((gates[0], core), (gates[1], 1 - core)):
        for g in range(2):
            raw[g, 0:heads, pl.ds(pl.multiple_of(half * length, length), length)] = ref[g]
    first = core * per_core if heads > 1 else 0
    picked[...] = jnp.zeros_like(picked)
    for g in range(2):
        for i in range(per_core):
            picked[g, i : i + 1, :] = raw[g, pl.ds(first + i, 1), :]
    forget = picked[1]
    log_forget = -(jnp.maximum(-forget, 0.0) + jnp.log1p(jnp.exp(-jnp.abs(forget))))
    upto = jnp.where(iota((length, length), 0) <= iota((length, length), 1), 1.0, 0.0).astype(BF16)
    parts = split3(log_forget)
    sums = [
        sum(dot(part[:, b * length : (b + 1) * length].astype(BF16), upto) for part in parts)
        for b in range(2)
    ]
    cumulative = jnp.concatenate([sums[0], sums[1] + sums[0][:, length - 1 :]], axis=1)
    return picked[0], cumulative


def same_request(lengths_ref, position):
    lag = iota((position.shape[0], 128), 1)
    here = segment_of(lengths_ref, position)
    return (segment_of(lengths_ref, position - lag) == here).astype(F32)


def lag_masks(same, start, stop, lags, width):
    return [
        None if lag == 0 else jnp.broadcast_to(same[start:stop, lag : lag + 1], (stop - start, width))
        for lag in range(lags)
    ]


def conv_rows(same, start, stop, taps, columns, wide, masks=None):
    if masks is None:
        masks = lag_masks(same, start, stop, taps.shape[0], wide.shape[1])
    total = taps[0:1, columns] * wide[8 + start : 8 + stop, :]
    for lag in range(1, taps.shape[0]):
        total = total + taps[lag : lag + 1, columns] * (
            wide[8 + start - lag : 8 + stop - lag, :] * masks[lag]
        )
    return (0.5 * total * (1.0 + jnp.tanh(0.5 * total))).astype(BF16)


def write_info(ref, normal, stab, decay):
    lines = [p[:, c : c + 128] for p in split3(normal) for c in range(0, normal.shape[1], 128)]
    lines += [jnp.broadcast_to(p, (1, 128)) for x in (stab, decay) for p in split3(x)]
    row = iota((INFO, 128), 0)
    block = jnp.zeros((INFO, 128), F32)
    for i, line in enumerate(lines):
        block = jnp.where(row == i, line, block)
    ref[ref.shape[0] - INFO :, :] = block.astype(BF16)


def read_info(ref, key_width=256):
    b = ref[ref.shape[0] - INFO :, :].astype(F32)
    k = key_width // 128
    normal = jnp.concatenate(
        [b[i : i + 1] + b[i + k : i + k + 1] + b[i + 2 * k : i + 2 * k + 1] for i in range(k)],
        axis=1,
    )
    sums = [b[i : i + 1] + b[i + 1 : i + 2] + b[i + 2 : i + 3] for i in (3 * k, 3 * k + 3)]
    return normal, sums[0][:, 0:1], sums[1][:, 0:1]


def half_columns(core, width):
    return pl.ds(pl.multiple_of(core * width, 128), width)


def gates_kernel(
    input_ref, forget_ref, key_ref, value_ref, gate_ref, key_send, send_ref, sems
):
    core, _ = core_place()
    width = key_send.shape[1]
    columns = half_columns(1 - core, width) if key_ref.shape[1] > width else pl.ds(0, width)
    copies = start_copies(
        sems,
        [
            (key_ref.at[:, columns], key_send),
            (value_ref.at[:, half_columns(1 - core, send_ref.shape[1])], send_ref),
            (input_ref, gate_ref.at[0]),
            (forget_ref, gate_ref.at[1]),
        ],
    )
    for copy in copies:
        copy.wait()


def own_kernel_parts(key_ref, value_ref, taps_ref, keys, values, taps, sems):
    core, _ = core_place()
    width = keys.shape[1]
    columns = half_columns(core, width) if key_ref.shape[1] > width else pl.ds(0, width)
    copies = start_copies(
        sems,
        [
            (key_ref.at[:, columns], keys),
            (value_ref.at[:, half_columns(core, values.shape[1])], values),
            (taps_ref.at[1, :, columns], taps),
        ],
    )
    for copy in copies:
        copy.wait()


def chip_kernel(
    per_core, lengths_ref, own_keys, own_values, key_other, value_other, gates_ref, gates_other,
    taps,
    conv_ref, gate_ref, key_edge, levels_first, out0, out1, out2, out3,
    raw, picked, wide, weighted_ref, whole, normals, levels,
):
    core, mine = core_place()
    rows, width = own_keys.shape
    length = 2 * rows
    key_width = width // per_core
    value_width = own_values.shape[1] // per_core
    own_rows = pl.ds(pl.multiple_of(core * rows, rows), rows)
    other_rows = pl.ds(pl.multiple_of((1 - core) * rows, rows), rows)
    offset = lax.axis_index("seq") // 2 * length
    gate, cumulative = gate_rows(core, per_core, (gates_ref, gates_other), raw, picked)
    gate_ref[0] = gate
    gate_ref[1] = cumulative
    segment = segment_of(lengths_ref, offset + iota((1, length), 1))
    last = segment_of(lengths_ref, jnp.full((1, 1), offset + length - 1, jnp.int32))
    before = segment_of(lengths_ref, jnp.full((1, 1), offset - 1, jnp.int32))
    total = cumulative[:, length - 1 : length]
    tail_weight = jnp.where(segment == last, gate + total - cumulative, very_negative)
    stab = jnp.max(tail_weight, axis=1, keepdims=True)
    factor = jnp.exp(tail_weight - stab).T
    levels[0] = jnp.broadcast_to(stab, (8, 128))
    through = jnp.where(before == last, total, very_negative)
    levels[1] = jnp.broadcast_to(through, (8, 128))
    levels_first[0] = tail_weight[:, 0:128]
    levels_first[1] = levels[1]
    same = same_request(lengths_ref, offset + iota((length, 128), 0))
    normals[...] = jnp.zeros_like(normals)
    step = 128
    key_edge[0] = jnp.where(core == 0, own_keys[0:16, :], key_other[0:16, :])
    key_edge[1] = jnp.where(core == 0, key_other[rows - 16 :, :], own_keys[rows - 16 :, :])
    for i in range(per_core):
        columns = slice(i * key_width, (i + 1) * key_width)
        wide[i, 0:8, :] = jnp.zeros((8, key_width), F32)
        for ref, half in ((own_keys, core), (key_other, 1 - core)):
            span = pl.ds(pl.multiple_of(8 + half * rows, 8), rows)
            wide[i, span, :] = ref[:, columns].astype(F32)
    totals = [jnp.zeros((1, key_width), F32) for _ in range(per_core)]
    for start in range(0, length, step):
        masks = lag_masks(same, start, start + step, taps.shape[0], key_width)
        for i in range(per_core):
            columns = slice(i * key_width, (i + 1) * key_width)
            conv = conv_rows(same, start, start + step, taps, columns, wide.at[i], masks)
            conv_ref[start : start + step, columns] = conv
            weight = factor[start : start + step, i : i + 1]
            if start == 0:
                weight = jnp.where(iota((step, 1), 0) >= FIRST, weight, 0.0)
            weighted = conv.astype(F32) * weight
            totals[i] = totals[i] + jnp.sum(weighted, axis=0, keepdims=True)
            weighted_ref[start : start + step, columns] = weighted.astype(BF16)
    for i in range(per_core):
        normals[i : i + 1, :] = totals[i]
    for i in range(per_core):
        columns = slice(i * key_width, (i + 1) * key_width)
        value_columns = slice(i * value_width, (i + 1) * value_width)
        whole[columns, :] = sum(
            dot(weighted_ref[part, columns], ref[:, value_columns], ((0,), (0,)))
            for part, ref in ((own_rows, own_values), (other_rows, value_other))
        ).astype(BF16)
    rows = width // 4
    for off, out in enumerate((out0, out1, out2, out3)):
        piece = piece_of(mine, off)
        content = whole[pl.ds(pl.multiple_of(piece * rows, rows), rows), :]
        for j in range(value_width // 128):
            out[j * rows : (j + 1) * rows, :] = content[:, j * 128 : (j + 1) * 128]
        head = piece // (key_width // rows)
        write_info(
            out,
            normals[pl.ds(head, 1), :],
            levels[0, pl.ds(head, 1), :][:, 0:1],
            levels[1, pl.ds(head, 1), :][:, 0:1],
        )


def message_kernel(
    per_core, query_ref, query_other, key_edge, own_values, value_other, levels_first,
    out_ref, rows_ref, tail, sems,
):
    core, _ = core_place()
    width = key_edge.shape[2]
    split = query_ref.shape[1] > width
    columns = pl.ds(pl.multiple_of(core * width, 128) if split else 0, width)
    last = pl.ds(query_ref.shape[0] - 16, 16)
    for ref, here in ((query_ref, core == 1), (query_other, core == 0)):

        def fetch(ref=ref):
            copy = pltpu.make_async_copy(ref.at[last, columns], tail, sems.at[0])
            copy.start()
            copy.wait()

        pl.when(here)(fetch)
    rows_ref[...] = jnp.zeros_like(rows_ref)
    at = 0
    for block in (
        key_edge[0].astype(F32)[0:FIRST],
        jnp.where(core == 0, own_values[0:16, :], value_other[0:16, :]).astype(F32)[0:FIRST],
        key_edge[1].astype(F32)[16 - FIRST :],
        tail[...].astype(F32)[16 - FIRST :],
    ):
        for j in range(block.shape[1] // 128):
            rows_ref[at : at + FIRST, :] = block[:, j * 128 : (j + 1) * 128]
            at += FIRST
    lane, span = iota((1, 128), 1), 64 // per_core
    line = jnp.zeros((1, 128), F32)
    for i in range(per_core):
        ends, decay = levels_first[0, i : i + 1, :], levels_first[1, i : i + 1, :]
        if i > 0:
            ends = pltpu.roll(ends, i * span, 1)
        line = jnp.where((lane >= i * span) & (lane < (i + 1) * span), ends, line)
        line = jnp.where((lane >= 64 + i * span) & (lane < 64 + (i + 1) * span), decay, line)
    for p, part in enumerate(split3(line)):
        rows_ref[at + p : at + p + 1, :] = part
    out_ref[0] = rows_ref[...].astype(BF16)


def join_kernel(first_ref, second_ref, out_ref):
    count = first_ref.shape[0]
    out_ref[0:count] = first_ref[...]
    out_ref[count:] = second_ref[...]


def gathered_kernel(
    per_core, length, offsets, lengths_ref, near_ref, far_ref, taps, key_edge,
    query_taps, query_edge,
    keys_ref, values_ref, levels_ref, conv_ref, by_chip, wide, value_rows, level_rows, narrow,
):
    half = near_ref.shape[0]
    chips = 2 * half
    me = lax.axis_index("seq") // 2
    width = key_edge.shape[2]
    key_width = width // per_core
    value_width = values_ref.shape[1]
    key_blocks, value_blocks = key_width // 128, value_width // 128
    for k, off in enumerate(offsets):
        message = near_ref[k] if k < half else far_ref[k - half]
        by_chip[lax.bitwise_xor(me, off)] = message.astype(F32)
    row = iota((16 * chips, 128), 0)
    position = length * lax.shift_right_logical(row, 4) + lax.bitwise_and(row, 15) - 8
    same = same_request(lengths_ref, position)
    value_rows[...] = jnp.zeros_like(value_rows)
    level_rows[...] = jnp.full_like(level_rows, 2 * very_negative)
    values_at = FIRST * per_core * key_blocks
    tails_at = values_at + FIRST * per_core * value_blocks
    levels_at = tails_at + 2 * FIRST * per_core * key_blocks
    span = 64 // per_core
    lines = [
        sum(by_chip[g, levels_at + p : levels_at + p + 1, :] for p in range(3))
        for g in range(chips)
    ]
    square = iota((FIRST, 128), 0) == iota((FIRST, 128), 1)
    for i in range(per_core):
        wide[...] = jnp.zeros_like(wide)
        since = jnp.zeros((1, 1), F32)
        for g in reversed(range(chips)):
            at = 16 * g + 8
            for j in range(key_blocks):
                columns = slice(j * 128, (j + 1) * 128)
                source = FIRST * (i * key_blocks + j)
                wide[8 + at : 8 + at + FIRST, columns] = by_chip[g, source : source + FIRST, :]
                if g > 0:
                    source += tails_at
                    wide[8 + at - FIRST : 8 + at, columns] = by_chip[
                        g - 1, source : source + FIRST, :
                    ]
            for j in range(value_blocks):
                source = values_at + FIRST * (i * value_blocks + j)
                value_rows[i * 16 * chips + at : i * 16 * chips + at + FIRST, j * 128 : (j + 1) * 128] = (
                    by_chip[g, source : source + FIRST, :]
                )
            ends = lines[g]
            if i > 0:
                ends = pltpu.roll(ends, 128 - i * span, 1)
            ends = jnp.where(g < me, ends + since, 2 * very_negative)
            decay = lines[g][:, 64 + i * span : 64 + i * span + 1]
            since = since + jnp.where(g < me, decay, 0.0)
            column = jnp.sum(jnp.where(square, ends, 0.0), axis=1, keepdims=True)
            level_rows[i * 16 * chips + at : i * 16 * chips + at + FIRST, :] = jnp.broadcast_to(
                column, (FIRST, 128)
            )
        keys_ref[i * 16 * chips : (i + 1) * 16 * chips, :] = conv_rows(
            same, 0, 16 * chips, taps, slice(i * key_width, (i + 1) * key_width), wide
        )
    values_ref[...] = value_rows[...].astype(BF16)
    levels_ref[...] = level_rows[...]
    same = same_request(lengths_ref, me * length + iota((16, 128), 0))
    previous = jnp.maximum(me - 1, 0)
    for which, (weights, edge) in enumerate(((query_taps, query_edge), (taps, key_edge))):
        for i in range(per_core):
            columns = slice(i * key_width, (i + 1) * key_width)
            for j in range(key_blocks):
                source = tails_at + FIRST * ((1 - which) * per_core + i) * key_blocks + FIRST * j
                narrow[8 - FIRST : 8, j * 128 : (j + 1) * 128] = by_chip[
                    previous, source : source + FIRST, :
                ]
            narrow[8:, :] = edge[0, :, columns].astype(F32)
            conv_ref[which, :, columns] = conv_rows(same, 0, 16, weights, columns, narrow)


def shifted_stab(infos, ranks, upto):
    out = []
    for i, (_, stab, _) in enumerate(infos):
        for j, (_, _, decay) in enumerate(infos):
            if i != j:
                inside = (ranks[j] > ranks[i]) & (ranks[j] < upto)
                stab = stab + jnp.where(inside, decay, 0.0)
        out.append(stab)
    return out


def total_kernel(*refs):
    *states, out = refs
    rows = out.shape[0] - INFO
    _, mine = core_place()
    ranks = [lax.bitwise_xor(mine, off) for off in range(4)]
    infos = [read_info(s) for s in states]
    stabs = shifted_stab(infos, ranks, 4)
    m = functools.reduce(jnp.maximum, stabs)
    weights = [jnp.exp(s - m) for s in stabs]
    step = math.gcd(rows, 64)
    for at in range(0, rows, step):
        span = slice(at, at + step)
        out[span, :] = sum(w * s[span, :].astype(F32) for w, s in zip(weights, states)).astype(BF16)
    write_info(out, sum(w * i[0] for w, i in zip(weights, infos)), m, sum(i[2] for i in infos))


def is_later(bit):
    return lax.rem(lax.shift_right_logical(lax.axis_index("seq"), bit), 2) == 1


def round_kernel(bit, first, *refs):
    if first:
        total_ref, got_ref, prefix_out, total_out = refs
    else:
        prefix_ref, total_ref, got_ref, prefix_out, total_out = refs
    rows = total_ref.shape[0] - INFO
    later = is_later(bit)
    n_t, m_t, d_t = read_info(total_ref)
    n_g, m_g, d_g = read_info(got_ref)
    here, got = total_ref[0:rows, :].astype(F32), got_ref[0:rows, :].astype(F32)
    a_t = m_t + jnp.where(later, 0.0, d_g)
    a_g = m_g + jnp.where(later, d_t, 0.0)
    m = jnp.maximum(a_t, a_g)
    w_t, w_g = jnp.exp(a_t - m), jnp.exp(a_g - m)
    total_out[0:rows, :] = (w_t * here + w_g * got).astype(BF16)
    write_info(total_out, w_t * n_t + w_g * n_g, m, d_t + d_g)
    if first:
        n_p, m_p, d_p = jnp.zeros_like(n_g), jnp.full_like(m_g, very_negative), jnp.zeros_like(d_g)
        prefix = jnp.zeros_like(got)
    else:
        n_p, m_p, d_p = read_info(prefix_ref)
        prefix = prefix_ref[0:rows, :].astype(F32)
    a_g = jnp.where(later, m_g + d_p, 2 * very_negative)
    m = jnp.maximum(m_p, a_g)
    w_p = jnp.exp(m_p - m)
    w_g = jnp.where(later, jnp.exp(a_g - m), 0.0)
    prefix_out[0:rows, :] = (w_p * prefix + w_g * got).astype(BF16)
    write_info(prefix_out, w_p * n_p + w_g * n_g, m, d_p + jnp.where(later, d_g, 0.0))


def enter_kernel(bit, prefix_ref, *refs):
    states, outs = refs[:4], refs[4:]
    rows = outs[0].shape[0] - INFO
    _, mine = core_place()
    ranks = [lax.bitwise_xor(mine, off) for off in range(4)]
    infos = [read_info(s) for s in states]
    n_p, m_p, _ = read_info(prefix_ref)
    valid = True if bit is None else is_later(bit)
    weights = []
    for off, out in enumerate(outs):
        stabs = shifted_stab(infos, ranks, ranks[off])
        m_in = m_p
        for info, rank in zip(infos, ranks):
            m_in = m_in + jnp.where(rank < ranks[off], info[2], 0.0)
        m_in = jnp.where(valid, m_in, very_negative)
        stabs = [
            jnp.where(rank < ranks[off], s, 2 * very_negative) for s, rank in zip(stabs, ranks)
        ]
        m = functools.reduce(jnp.maximum, stabs, m_in)
        mine_in = [jnp.where(valid, jnp.exp(m_in - m), 0.0)] + [
            jnp.where(rank < ranks[off], jnp.exp(s - m), 0.0) for s, rank in zip(stabs, ranks)
        ]
        weights.append(mine_in)
        normals = [n_p] + [info[0] for info in infos]
        write_info(out, sum(w * n for w, n in zip(mine_in, normals)), m, jnp.zeros_like(m))
    step = math.gcd(rows, 64)
    for at in range(0, rows, step):
        parts = [r[at : at + step, :].astype(F32) for r in (prefix_ref, *states)]
        for off, out in enumerate(outs):
            out[at : at + step, :] = sum(
                w * part
                for k, (w, part) in enumerate(zip(weights[off], parts))
                if k != off + 1
            ).astype(BF16)


def query_kernel(
    per_core, lengths_ref, query_ref, query_other, taps_ref, own_values, value_other,
    conv_ref, taps, edge_ref, values, queries, wide, sems,
):
    core, _ = core_place()
    length, width = queries.shape
    key_width = width // per_core
    split = query_ref.shape[1] > width
    columns = pl.ds(pl.multiple_of(core * width, 128) if split else 0, width)
    copies = start_copies(
        sems,
        [(taps_ref.at[0, :, columns], taps)]
        + by_core(core, query_ref, query_other, columns, queries)
        + by_core(core, own_values, value_other, slice(None), values),
    )
    offset = lax.axis_index("seq") // 2 * length
    same = same_request(lengths_ref, offset + iota((length, 128), 0))
    for copy in copies:
        copy.wait()
    edge_ref[0] = queries[0:16, :]
    edge_ref[1] = queries[length - 16 :, :]
    for i in range(per_core):
        here = slice(i * key_width, (i + 1) * key_width)
        wide[0:8, :] = jnp.zeros((8, key_width), F32)
        wide[8:, :] = queries[:, here].astype(F32)
        for start in range(0, length, 128):
            conv_ref[start : start + 128, here] = conv_rows(
                same, start, start + 128, taps, here, wide
            )


def intra_kernel(
    per_core, lengths_ref, query_conv, key_ref, conv_first, values, gate_ref,
    query_ref, numerator_ref, stats_ref, keys,
):
    length, width = query_ref.shape
    key_width = width // per_core
    value_width = values.shape[1] // per_core
    key_scale = 1.0 / math.sqrt(key_width)
    offset = lax.axis_index("seq") // 2 * length
    query_ref[...] = query_conv[...]
    query_ref[0:16, :] = conv_first[0]
    keys[...] = key_ref[...]
    keys[0:16, :] = conv_first[1]
    gate, cumulative = gate_ref[0], gate_ref[1]
    by_token = cumulative.T
    segment = segment_of(lengths_ref, offset + iota((length, 1), 0))
    segment_row = segment_of(lengths_ref, offset + iota((1, length), 1))
    before = segment_of(lengths_ref, jnp.full((1, 1), offset - 1, jnp.int32))
    step = length // 2
    lane = iota((step, 128), 1)
    stats = [[jnp.zeros((step, 128), F32)] * 3 for _ in range(2)]
    for i in range(per_core):
        here = slice(i * key_width, (i + 1) * key_width)
        value_columns = slice(i * value_width, (i + 1) * value_width)
        for b in range(2):
            rows, stop = slice(b * step, (b + 1) * step), (b + 1) * step
            allowed = segment_row[:, 0:stop] == segment[rows]
            allowed &= iota((step, stop), 1) <= iota((step, stop), 0) + b * step
            total = by_token[rows, i : i + 1]
            log_weight = jnp.where(
                allowed,
                gate[i : i + 1, 0:stop] - cumulative[i : i + 1, 0:stop] + total,
                very_negative,
            )
            row_max = jnp.max(log_weight, axis=1, keepdims=True)
            scores = dot(query_ref[rows, here], keys[0:stop, here], ((1,), (1,))) * key_scale
            weights = scores * jnp.exp(log_weight - row_max)
            numerator_ref[rows, value_columns] = dot(
                weights.astype(BF16), values[0:stop, value_columns]
            )
            linked = jnp.where(segment[rows] == before, total, very_negative)
            found = (jnp.sum(weights, axis=1, keepdims=True), row_max, linked)
            stats[b] = [jnp.where(lane == i, new, old) for new, old in zip(found, stats[b])]
    for b in range(2):
        for k in range(3):
            stats_ref[k, b * step : (b + 1) * step, :] = stats[b][k]


def head_rows(
    per_core, start, memory, parts, stabs, query_ref, numerator_ref, stats_ref, out_ref
):
    step = out_ref.shape[0]
    key_width = query_ref.shape[1] // per_core
    value_width = memory.shape[1]
    key_scale = 1.0 / math.sqrt(key_width)
    span = pl.ds(pl.multiple_of(start, step), step)
    queries = [query_ref[span, i * key_width : (i + 1) * key_width] for i in range(per_core)]
    from_normal = sum(
        dot(q, parts[i * 128 : (i + 1) * 128, :], ((1,), (1,))) for i, q in enumerate(queries)
    )
    from_normal = (
        from_normal
        + pltpu.roll(from_normal, 128 - 8, 1)
        + pltpu.roll(from_normal, 128 - 16, 1)
    )
    row_max = stats_ref[1, span, :]
    carried = stabs[0:1, :] + stats_ref[2, span, :]
    m = jnp.maximum(row_max, carried)
    w_here = jnp.exp(row_max - m)
    w_in = jnp.exp(carried - m) * key_scale
    denominator = w_here * stats_ref[0, span, :] + w_in * from_normal
    scale = 1.0 / jnp.maximum(jnp.abs(denominator), 1.0)
    w_here, w_in = w_here * scale, w_in * scale
    for i in range(per_core):
        columns = slice(i * value_width, (i + 1) * value_width)
        from_memory = dot(queries[i], memory[i * key_width : (i + 1) * key_width, :])
        out_ref[:, columns] = (
            w_here[:, i : i + 1] * numerator_ref[span, columns] + w_in[:, i : i + 1] * from_memory
        ).astype(BF16)


def head_send_kernel(
    per_core, own_ref, got1, got2, got3, keys_ref, values_ref, levels_ref,
    query_ref, numerator_ref, stats_ref, send_ref, memory, parts, stabs, info,
):
    core, mine = core_place()
    key_width = query_ref.shape[1] // per_core
    value_width = memory.shape[1]
    rows = query_ref.shape[1] // 4
    for off, ref in enumerate((own_ref, got1, got2, got3)):
        piece = piece_of(mine, off)
        start = pl.multiple_of(piece * rows, rows)
        for j in range(value_width // 128):
            memory[pl.ds(start, rows), j * 128 : (j + 1) * 128] = ref[j * rows : (j + 1) * rows, :]
        info[piece] = ref[ref.shape[0] - INFO :, :]
    count = keys_ref.shape[0] // per_core
    row, lane = iota((128, key_width), 0), iota((1, 128), 1)
    levels = jnp.full((1, 128), very_negative, F32)
    for i in range(per_core):
        normal, stab, _ = read_info(info.at[i * key_width // rows], key_width)
        here = slice(i * key_width, (i + 1) * key_width)
        extra = slice(i * count, (i + 1) * count)
        weighted = keys_ref[extra, :].astype(F32) * jnp.exp(levels_ref[extra, 0:1] - stab)
        normal = normal + jnp.sum(weighted, axis=0, keepdims=True)
        memory[here, :] = (
            memory[here, :].astype(F32)
            + dot(weighted.astype(BF16), values_ref[extra, :], ((0,), (0,)))
        ).astype(BF16)
        levels = jnp.where(lane == i, stab, levels)
        block = jnp.zeros((128, key_width), F32)
        for k, part in enumerate(split3(normal)):
            block = jnp.where(row == 8 * k + i, part, block)
        parts[i * 128 : (i + 1) * 128, :] = block.astype(BF16)
    stabs[...] = jnp.broadcast_to(levels, stabs.shape)
    start = (1 - core) * send_ref.shape[0]
    head_rows(
        per_core, start, memory, parts, stabs, query_ref, numerator_ref, stats_ref, send_ref
    )


def head_keep_kernel(
    per_core, memory, parts, stabs, query_ref, numerator_ref, stats_ref, keep_ref
):
    core, _ = core_place()
    start = core * keep_ref.shape[0]
    head_rows(
        per_core, start, memory, parts, stabs, query_ref, numerator_ref, stats_ref, keep_ref
    )


def weight_part(weight_ref, half, rows, start, width):
    return weight_ref[
        pl.ds(pl.multiple_of(half * rows, 128), rows), pl.ds(pl.multiple_of(start, 128), width)
    ]


def keep_kernel(off, head_ref, weight_ref, part_ref):
    core, _ = core_place()
    rows, width = head_ref.shape[1], part_ref.shape[1]
    start = lax.bitwise_xor(lax.axis_index("head"), off) * width
    part_ref[...] = dot(head_ref[...], weight_part(weight_ref, core, rows, start, width))


def send_kernel(off, chunk, head_ref, weight_ref, kept_ref, part_ref):
    core, _ = core_place()
    rows, piece, width = head_ref.shape[1], part_ref.shape[1], kept_ref.shape[1]
    start = lax.bitwise_xor(lax.axis_index("head"), off) * width + chunk * piece
    part_ref[...] = (
        dot(head_ref[...], weight_part(weight_ref, 1 - core, rows, start, piece))
        + kept_ref[:, chunk * piece : (chunk + 1) * piece]
    ).astype(part_ref.dtype)


def own_kernel(keep_ref, got_ref, weight_ref, part_ref):
    core, _ = core_place()
    rows, width = keep_ref.shape[1], part_ref.shape[1]
    start = lax.axis_index("head") * width
    part_ref[...] = dot(
        keep_ref[...], weight_part(weight_ref, core, rows, start, width)
    ) + dot(got_ref[...], weight_part(weight_ref, 1 - core, rows, start, width))


def sum_kernel(chunk, count, own_ref, *refs):
    arrived, (out_ref, held, sems) = refs[:count], refs[-3:]
    width = held.shape[1]
    columns = pl.ds(chunk * width, width)
    parts = sems.shape[0]
    step = own_ref.shape[0] // parts
    copies = []
    for part in range(parts):
        rows = slice(part * step, (part + 1) * step)
        total = own_ref[rows, chunk * width : (chunk + 1) * width]
        for ref in arrived:
            total = total + ref[rows, :].astype(F32)
        held[rows, :] = total.astype(held.dtype)
        span = pl.ds(part * step, step)
        copies.append(
            pltpu.make_async_copy(held.at[span, :], out_ref.at[span, columns], sems.at[part])
        )
        copies[-1].start()
    for copy in copies:
        copy.wait()


def call(kernel, out_shape, spaces, scratch, name, flops=0, nbytes=0, limit=24, out=pltpu.VMEM,
         aliases=None):
    place = {"v": pltpu.VMEM, "s": pltpu.SMEM, "a": pl.ANY, "h": pl.ANY}
    outs = jax.tree.map(lambda _: pl.BlockSpec(memory_space=out), out_shape)
    inner = pl.pallas_call(
        kernel,
        out_shape=out_shape,
        in_specs=[pl.BlockSpec(memory_space=place[s]) for s in spaces],
        out_specs=outs,
        scratch_shapes=scratch,
        compiler_params=pltpu.CompilerParams(vmem_limit_bytes=limit << 20),
        cost_estimate=pl.CostEstimate(flops=flops, bytes_accessed=nbytes, transcendentals=0),
        name=name,
        input_output_aliases=aliases or {},
    )

    def run(*args):
        return inner(
            *(
                pltpu.with_memory_space_constraint(x, pltpu.HBM) if s in "hs" else x
                for s, x in zip(spaces, args, strict=True)
            )
        )

    return run


def on_device(
    query_input, key_input, value_input, kernel_taps, input_gate, forget_gate, request_lengths,
    output_weight,
):
    seq_count, head_count = lax.axis_size("seq"), lax.axis_size("head")
    length, key_cols = query_input.shape
    heads = input_gate.shape[0]
    value_cols = value_input.shape[1]
    out_cols = output_weight.shape[1] // head_count
    chip_length = 2 * length
    key_width = key_cols // heads
    per_core = max(1, heads // 2)
    part_keys, part_values = per_core * key_width, value_cols // 2
    value_width = part_values // per_core
    lags = kernel_taps.shape[1]
    rows = part_keys // 4

    def shape(dims, dtype=F32):
        return jax.ShapeDtypeStruct(dims, dtype)

    def swap(x, off):
        return lax.ppermute(x, "seq", [(i, i ^ off) for i in range(seq_count)])

    gates, key_send, value_send = call(
        gates_kernel,
        (
            shape((2, heads, length)),
            shape((length, part_keys), BF16),
            shape((length, part_values), BF16),
        ),
        "hhhh", [pltpu.SemaphoreType.DMA((4,))], "gates", flops=4 << 30,
    )(input_gate, forget_gate, key_input, value_input)
    gates_other, key_other, value_other = swap(gates, 1), swap(key_send, 1), swap(value_send, 1)
    key_after, value_after, gates = lax.optimization_barrier((key_input, value_input, gates))
    own_keys, own_values, taps = call(
        own_kernel_parts,
        (
            shape((length, part_keys), BF16),
            shape((length, part_values), BF16),
            shape((lags, part_keys)),
        ),
        "hhh", [pltpu.SemaphoreType.DMA((3,))], "own_part", flops=4 << 30,
    )(key_after, value_after, kernel_taps)
    query_after, gates = lax.optimization_barrier((query_input, gates))
    query_other = swap(query_after, 1)

    one = shape((rows * value_width // 128 + INFO, 128), BF16)
    key_conv, gate_sums, key_edge, levels, *pieces = call(
        functools.partial(chip_kernel, per_core),
        (
            shape((chip_length, part_keys), BF16),
            shape((2, 8, chip_length)),
            shape((2, 16, part_keys), BF16),
            shape((2, 8, 128)),
        )
        + (one,) * 4,
        "s" + "v" * 7,
        [
            pltpu.VMEM((2, max(8, heads), chip_length), F32),
            pltpu.VMEM((2, 8, chip_length), F32),
            pltpu.VMEM((per_core, chip_length + 8, key_width), F32),
            pltpu.VMEM((chip_length, part_keys), BF16),
            pltpu.VMEM((part_keys, value_width), BF16),
            pltpu.VMEM((8, key_width), F32),
            pltpu.VMEM((2, 8, 128), F32),
        ],
        "chip_state",
        flops=1 << 30,
    )(
        request_lengths, own_keys, own_values, key_other, value_other, gates, gates_other, taps
    )
    states = [pieces[0]] + [swap(pieces[off], 2 * off) for off in (1, 2, 3)]

    count = 16 * seq_count // 2
    lines = FIRST * per_core * (3 * key_width + value_width) // 128 + 3
    lines = -(-lines // 16) * 16
    message = call(
        functools.partial(message_kernel, per_core), shape((1, lines, 128), BF16), "havvvv",
        [
            pltpu.VMEM((lines, 128), F32),
            pltpu.VMEM((16, part_keys), BF16),
            pltpu.SemaphoreType.DMA((1,)),
        ],
        "message",
    )(query_input, query_other, key_edge, own_values, value_other, levels)
    bits = seq_count.bit_length() - 1
    steps = [4, 2, 8] if bits == 4 else [1 << b for b in range(1, bits)]
    near, far, offsets = message, swap(message, steps[0]), [0, steps[0] // 2]
    query_conv, query_taps, query_edge, values = call(
        functools.partial(query_kernel, per_core),
        (
            shape((chip_length, part_keys), BF16),
            shape((lags, part_keys)),
            shape((2, 16, part_keys), BF16),
            shape((chip_length, part_values), BF16),
        ),
        "shahvv",
        [
            pltpu.VMEM((chip_length, part_keys), BF16),
            pltpu.VMEM((chip_length + 8, key_width), F32),
            pltpu.SemaphoreType.DMA((5,)),
        ],
        "query_conv",
        flops=1 << 30,
    )(request_lengths, query_input, query_other, kernel_taps, own_values, value_other)
    states, query_conv, far = lax.optimization_barrier((states, query_conv, far))
    total = call(total_kernel, one, "vvvv", [], "group_total")(*states)
    flag = 3
    prefix = swap(total, 12 if bits == 4 else 8)
    near, far, total = lax.optimization_barrier((near, far, total))
    for step in steps[1:]:
        near = call(
            join_kernel, shape((2 * near.shape[0], lines, 128), BF16), "vv", [], "join"
        )(near, far)
        far = swap(near, step)
        offsets = offsets + [off ^ (step // 2) for off in offsets]
    if bits > 4:
        flag = None
        prefix, total = call(
            functools.partial(round_kernel, 3, True), (one, one), "vv", [], "round_state"
        )(total, prefix)
        for bit in range(4, bits):
            prefix, total = call(
                functools.partial(round_kernel, bit, False), (one, one), "vvv", [], "round_state"
            )(prefix, total, swap(total, 1 << bit))
    enter = call(functools.partial(enter_kernel, flag), (one,) * 4, "vvvvv", [], "enter_state")(
        prefix, *states
    )
    gate_sums, near, *enter = lax.optimization_barrier((gate_sums, near, *enter))
    enter = [enter[0]] + [swap(enter[off], 2 * off) for off in (1, 2, 3)]
    *extras, conv_first = call(
        functools.partial(gathered_kernel, per_core, chip_length, tuple(offsets)),
        (
            shape((per_core * count, key_width), BF16),
            shape((per_core * count, value_width), BF16),
            shape((per_core * count, 128)),
            shape((2, 16, part_keys), BF16),
        ),
        "svvvvvv",
        [
            pltpu.VMEM((seq_count // 2, lines, 128), F32),
            pltpu.VMEM((count + 8, key_width), F32),
            pltpu.VMEM((per_core * count, value_width), F32),
            pltpu.VMEM((per_core * count, 128), F32),
            pltpu.VMEM((24, key_width), F32),
        ],
        "gathered_first",
    )(request_lengths, near, far, taps, key_edge, query_taps, query_edge)
    inside = call(
        functools.partial(intra_kernel, per_core),
        (
            shape((chip_length, part_keys), BF16),
            shape((chip_length, part_values)),
            shape((3, chip_length, 128)),
        ),
        "svvvvv",
        [pltpu.VMEM((chip_length, part_keys), BF16)],
        "intra",
        flops=4 << 30,
    )(request_lengths, query_conv, key_conv, conv_first, values, gate_sums)
    half_out = shape((length, part_values), BF16)
    send, *entered = call(
        functools.partial(head_send_kernel, per_core),
        (
            half_out,
            shape((part_keys, value_width), BF16),
            shape((128 * per_core, key_width), BF16),
            shape((8, 128)),
        ),
        "v" * 10, [pltpu.VMEM((4, INFO, 128), BF16)], "head_send",
    )(*enter, *extras, *inside)
    keep = call(
        functools.partial(head_keep_kernel, per_core), half_out, "v" * 6, [], "head_keep",
        flops=1 << 30,
    )(*entered, *inside)
    got = swap(send, 1)

    chunks = 2 if head_count == 2 and out_cols % 256 == 0 else 1
    piece = out_cols // chunks
    arrived = []
    mixed = call(
        own_kernel, shape((length, out_cols)), "vvv", [], "project_own", flops=4 << 30
    )(keep, got, output_weight)
    for off in range(1, head_count):
        kept = call(
            functools.partial(keep_kernel, off), shape((length, out_cols)), "vv", [],
            "project_kept", flops=2 << 30,
        )(keep, output_weight)
        columns, after = [], got
        for chunk in range(chunks):
            part = call(
                functools.partial(send_kernel, off, chunk), shape((length, piece), BF16), "vvv",
                [], "project_other",
            )(after, output_weight, kept)
            columns.append(
                lax.ppermute(part, "head", [(i, i ^ off) for i in range(head_count)])
            )
            after, mixed = lax.optimization_barrier((got, mixed))
        arrived.append(columns)
    out = []
    for chunk in range(chunks):
        out = [
            call(
                functools.partial(sum_kernel, chunk, len(arrived)),
                shape((length, out_cols), BF16),
                "v" * (1 + len(arrived)) + "a" * len(out),
                [pltpu.VMEM((length, piece), BF16), pltpu.SemaphoreType.DMA((2,))],
                "mixed_out", out=pl.ANY, aliases={1 + len(arrived): 0} if out else None,
            )(mixed, *(columns[chunk] for columns in arrived), *out)
        ]
    return out[0]


def solution(mesh):
    placed = (
        P("seq", "head"),
        P("seq", "head"),
        P("seq", "head"),
        P(None, None, "head"),
        P("head", "seq"),
        P("head", "seq"),
        P(),
        P("head", None),
    )
    return jax.shard_map(
        on_device, mesh=mesh, in_specs=placed, out_specs=P("seq", "head"), check_vma=False
    )
```

```python
import functools
import math

import jax
import jax.numpy as jnp
from jax import lax
from jax.experimental import pallas as pl
from jax.experimental.pallas import tpu as pltpu
from jax.sharding import PartitionSpec as P

very_negative = -1e30
FIRST = 3
INFO = 16
TAIL = 16
BF16 = jnp.bfloat16
F32 = jnp.float32


def iota(shape, dim):
    return lax.broadcasted_iota(jnp.int32, shape, dim)


def dot(a, b, contract=((1,), (0,))):
    return lax.dot_general(a, b, (contract, ((), ())), preferred_element_type=F32)


def split3(x):
    high = x.astype(BF16).astype(F32)
    rest = x - high
    mid = rest.astype(BF16).astype(F32)
    return high, mid, (rest - mid).astype(BF16).astype(F32)


def segment_of(lengths_ref, position):
    start = jnp.int32(0)
    count = jnp.zeros_like(position)
    for r in range(lengths_ref.shape[0]):
        count = count + (start <= position).astype(jnp.int32)
        start = start + lengths_ref[r]
    return count - 1


def core_place():
    place = lax.axis_index("seq")
    return lax.rem(place, 2), lax.rem(place // 2, 4)


def piece_of(mine, off):
    piece = lax.bitwise_xor(mine, off)
    if lax.axis_size("seq") == 16:
        piece = lax.bitwise_xor(piece, lax.axis_index("seq") // 8 * 2)
    return piece


def start_copies(sems, pairs):
    copies = [pltpu.make_async_copy(a, b, sems.at[i]) for i, (a, b) in enumerate(pairs)]
    for copy in copies:
        copy.start()
    return copies


def by_core(core, own_ref, other_ref, columns, held):
    rows = own_ref.shape[0]
    return [
        (ref.at[:, columns], held.at[pl.ds(pl.multiple_of(half * rows, rows), rows), :])
        for ref, half in ((own_ref, core), (other_ref, 1 - core))
    ]


def gate_rows(core, per_core, gates, raw, picked):
    _, heads, length = gates[0].shape
    for ref, half in ((gates[0], core), (gates[1], 1 - core)):
        for g in range(2):
            raw[g, 0:heads, pl.ds(pl.multiple_of(half * length, length), length)] = ref[g]
    first = core * per_core if heads > 1 else 0
    picked[...] = jnp.zeros_like(picked)
    for g in range(2):
        for i in range(per_core):
            picked[g, i : i + 1, :] = raw[g, pl.ds(first + i, 1), :]
    forget = picked[1]
    log_forget = -(jnp.maximum(-forget, 0.0) + jnp.log1p(jnp.exp(-jnp.abs(forget))))
    upto = jnp.where(iota((length, length), 0) <= iota((length, length), 1), 1.0, 0.0).astype(BF16)
    parts = split3(log_forget)
    sums = [
        sum(dot(part[:, b * length : (b + 1) * length].astype(BF16), upto) for part in parts)
        for b in range(2)
    ]
    cumulative = jnp.concatenate([sums[0], sums[1] + sums[0][:, length - 1 :]], axis=1)
    return picked[0], cumulative


def same_request(lengths_ref, position):
    lag = iota((position.shape[0], 128), 1)
    here = segment_of(lengths_ref, position)
    return (segment_of(lengths_ref, position - lag) == here).astype(F32)


def lag_masks(same, start, stop, lags, width):
    return [
        None if lag == 0 else jnp.broadcast_to(same[start:stop, lag : lag + 1], (stop - start, width))
        for lag in range(lags)
    ]


def conv_rows(same, start, stop, taps, columns, wide, masks=None):
    if masks is None:
        masks = lag_masks(same, start, stop, taps.shape[0], wide.shape[1])
    total = taps[0:1, columns] * wide[8 + start : 8 + stop, :]
    for lag in range(1, taps.shape[0]):
        total = total + taps[lag : lag + 1, columns] * (
            wide[8 + start - lag : 8 + stop - lag, :] * masks[lag]
        )
    return (0.5 * total * (1.0 + jnp.tanh(0.5 * total))).astype(BF16)


def write_info(ref, normal, stab, decay):
    lines = [p[:, c : c + 128] for p in split3(normal) for c in range(0, normal.shape[1], 128)]
    lines += [jnp.broadcast_to(p, (1, 128)) for x in (stab, decay) for p in split3(x)]
    row = iota((INFO, 128), 0)
    block = jnp.zeros((INFO, 128), F32)
    for i, line in enumerate(lines):
        block = jnp.where(row == i, line, block)
    ref[ref.shape[0] - INFO :, :] = block.astype(BF16)


def read_info(ref, key_width=256):
    b = ref[ref.shape[0] - INFO :, :].astype(F32)
    k = key_width // 128
    normal = jnp.concatenate(
        [b[i : i + 1] + b[i + k : i + k + 1] + b[i + 2 * k : i + 2 * k + 1] for i in range(k)],
        axis=1,
    )
    sums = [b[i : i + 1] + b[i + 1 : i + 2] + b[i + 2 : i + 3] for i in (3 * k, 3 * k + 3)]
    return normal, sums[0][:, 0:1], sums[1][:, 0:1]


def half_columns(core, width):
    return pl.ds(pl.multiple_of(core * width, 128), width)


def gates_kernel(
    input_ref, forget_ref, key_ref, value_ref, gate_ref, key_send, send_ref, sems
):
    core, _ = core_place()
    width = key_send.shape[1]
    columns = half_columns(1 - core, width) if key_ref.shape[1] > width else pl.ds(0, width)
    copies = start_copies(
        sems,
        [
            (key_ref.at[:, columns], key_send),
            (value_ref.at[:, half_columns(1 - core, send_ref.shape[1])], send_ref),
            (input_ref, gate_ref.at[0]),
            (forget_ref, gate_ref.at[1]),
        ],
    )
    for copy in copies:
        copy.wait()


def own_kernel_parts(key_ref, value_ref, taps_ref, keys, values, taps, sems):
    core, _ = core_place()
    width = keys.shape[1]
    columns = half_columns(core, width) if key_ref.shape[1] > width else pl.ds(0, width)
    copies = start_copies(
        sems,
        [
            (key_ref.at[:, columns], keys),
            (value_ref.at[:, half_columns(core, values.shape[1])], values),
            (taps_ref.at[1, :, columns], taps),
        ],
    )
    for copy in copies:
        copy.wait()


def chip_kernel(
    per_core, lengths_ref, own_keys, own_values, key_other, value_other, gates_ref, gates_other,
    taps,
    conv_ref, gate_ref, key_edge, levels_first, out0, out1, out2, out3,
    raw, picked, wide, weighted_ref, whole, normals, levels,
):
    core, mine = core_place()
    rows, width = own_keys.shape
    length = 2 * rows
    key_width = width // per_core
    value_width = own_values.shape[1] // per_core
    own_rows = pl.ds(pl.multiple_of(core * rows, rows), rows)
    other_rows = pl.ds(pl.multiple_of((1 - core) * rows, rows), rows)
    offset = lax.axis_index("seq") // 2 * length
    gate, cumulative = gate_rows(core, per_core, (gates_ref, gates_other), raw, picked)
    gate_ref[0] = gate
    gate_ref[1] = cumulative
    segment = segment_of(lengths_ref, offset + iota((1, length), 1))
    last = segment_of(lengths_ref, jnp.full((1, 1), offset + length - 1, jnp.int32))
    before = segment_of(lengths_ref, jnp.full((1, 1), offset - 1, jnp.int32))
    total = cumulative[:, length - 1 : length]
    tail_weight = jnp.where(segment == last, gate + total - cumulative, very_negative)
    stab = jnp.max(tail_weight, axis=1, keepdims=True)
    factor = jnp.exp(tail_weight - stab).T
    levels[0] = jnp.broadcast_to(stab, (8, 128))
    through = jnp.where(before == last, total, very_negative)
    levels[1] = jnp.broadcast_to(through, (8, 128))
    levels_first[0] = tail_weight[:, 0:128]
    levels_first[1] = levels[1]
    same = same_request(lengths_ref, offset + iota((length, 128), 0))
    normals[...] = jnp.zeros_like(normals)
    step = 256
    key_edge[0] = jnp.where(core == 0, own_keys[0:16, :], key_other[0:16, :])
    key_edge[1] = jnp.where(core == 0, key_other[rows - 16 :, :], own_keys[rows - 16 :, :])
    for i in range(per_core):
        columns = slice(i * key_width, (i + 1) * key_width)
        wide[i, 0:8, :] = jnp.zeros((8, key_width), F32)
        for ref, half in ((own_keys, core), (key_other, 1 - core)):
            span = pl.ds(pl.multiple_of(8 + half * rows, 8), rows)
            wide[i, span, :] = ref[:, columns].astype(F32)
    totals = [jnp.zeros((1, key_width), F32) for _ in range(per_core)]
    for start in range(0, length, step):
        masks = lag_masks(same, start, start + step, taps.shape[0], key_width)
        for i in range(per_core):
            columns = slice(i * key_width, (i + 1) * key_width)
            conv = conv_rows(same, start, start + step, taps, columns, wide.at[i], masks)
            conv_ref[start : start + step, columns] = conv
            weight = factor[start : start + step, i : i + 1]
            if start == 0:
                weight = jnp.where(iota((step, 1), 0) >= FIRST, weight, 0.0)
            weighted = conv.astype(F32) * weight
            totals[i] = totals[i] + jnp.sum(weighted, axis=0, keepdims=True)
            weighted_ref[start : start + step, columns] = weighted.astype(BF16)
    for i in range(per_core):
        normals[i : i + 1, :] = totals[i]
    for i in range(per_core):
        columns = slice(i * key_width, (i + 1) * key_width)
        value_columns = slice(i * value_width, (i + 1) * value_width)
        whole[columns, :] = sum(
            dot(weighted_ref[part, columns], ref[:, value_columns], ((0,), (0,)))
            for part, ref in ((own_rows, own_values), (other_rows, value_other))
        ).astype(BF16)
    rows = width // 4
    for off, out in enumerate((out0, out1, out2, out3)):
        piece = piece_of(mine, off)
        content = whole[pl.ds(pl.multiple_of(piece * rows, rows), rows), :]
        for j in range(value_width // 128):
            out[j * rows : (j + 1) * rows, :] = content[:, j * 128 : (j + 1) * 128]
        head = piece // (key_width // rows)
        write_info(
            out,
            normals[pl.ds(head, 1), :],
            levels[0, pl.ds(head, 1), :][:, 0:1],
            levels[1, pl.ds(head, 1), :][:, 0:1],
        )


def message_kernel(
    per_core, query_ref, query_other, key_edge, own_values, value_other, levels_first,
    out_ref, rows_ref, tail, sems,
):
    core, _ = core_place()
    width = key_edge.shape[2]
    split = query_ref.shape[1] > width
    columns = pl.ds(pl.multiple_of(core * width, 128) if split else 0, width)
    last = pl.ds(query_ref.shape[0] - 16, 16)
    for ref, here in ((query_ref, core == 1), (query_other, core == 0)):

        def fetch(ref=ref):
            copy = pltpu.make_async_copy(ref.at[last, columns], tail, sems.at[0])
            copy.start()
            copy.wait()

        pl.when(here)(fetch)
    rows_ref[...] = jnp.zeros_like(rows_ref)
    at = 0
    for block in (
        key_edge[0].astype(F32)[0:FIRST],
        jnp.where(core == 0, own_values[0:16, :], value_other[0:16, :]).astype(F32)[0:FIRST],
        key_edge[1].astype(F32)[16 - FIRST :],
        tail[...].astype(F32)[16 - FIRST :],
    ):
        for j in range(block.shape[1] // 128):
            rows_ref[at : at + FIRST, :] = block[:, j * 128 : (j + 1) * 128]
            at += FIRST
    lane, span = iota((1, 128), 1), 64 // per_core
    line = jnp.zeros((1, 128), F32)
    for i in range(per_core):
        ends, decay = levels_first[0, i : i + 1, :], levels_first[1, i : i + 1, :]
        if i > 0:
            ends = pltpu.roll(ends, i * span, 1)
        line = jnp.where((lane >= i * span) & (lane < (i + 1) * span), ends, line)
        line = jnp.where((lane >= 64 + i * span) & (lane < 64 + (i + 1) * span), decay, line)
    for p, part in enumerate(split3(line)):
        rows_ref[at + p : at + p + 1, :] = part
    out_ref[0] = rows_ref[...].astype(BF16)


def join_kernel(first_ref, second_ref, out_ref):
    count = first_ref.shape[0]
    out_ref[0:count] = first_ref[...]
    out_ref[count:] = second_ref[...]


def gathered_kernel(
    per_core, length, offsets, lengths_ref, near_ref, far_ref, taps, key_edge,
    query_taps, query_edge,
    keys_ref, values_ref, levels_ref, conv_ref, by_chip, wide, value_rows, level_rows, narrow,
):
    half = near_ref.shape[0]
    chips = 2 * half
    me = lax.axis_index("seq") // 2
    width = key_edge.shape[2]
    key_width = width // per_core
    value_width = values_ref.shape[1]
    key_blocks, value_blocks = key_width // 128, value_width // 128
    for k, off in enumerate(offsets):
        message = near_ref[k] if k < half else far_ref[k - half]
        by_chip[lax.bitwise_xor(me, off)] = message.astype(F32)
    row = iota((16 * chips, 128), 0)
    position = length * lax.shift_right_logical(row, 4) + lax.bitwise_and(row, 15) - 8
    same = same_request(lengths_ref, position)
    value_rows[...] = jnp.zeros_like(value_rows)
    level_rows[...] = jnp.full_like(level_rows, 2 * very_negative)
    values_at = FIRST * per_core * key_blocks
    tails_at = values_at + FIRST * per_core * value_blocks
    levels_at = tails_at + 2 * FIRST * per_core * key_blocks
    span = 64 // per_core
    lines = [
        sum(by_chip[g, levels_at + p : levels_at + p + 1, :] for p in range(3))
        for g in range(chips)
    ]
    square = iota((FIRST, 128), 0) == iota((FIRST, 128), 1)
    for i in range(per_core):
        wide[...] = jnp.zeros_like(wide)
        since = jnp.zeros((1, 1), F32)
        for g in reversed(range(chips)):
            at = 16 * g + 8
            for j in range(key_blocks):
                columns = slice(j * 128, (j + 1) * 128)
                source = FIRST * (i * key_blocks + j)
                wide[8 + at : 8 + at + FIRST, columns] = by_chip[g, source : source + FIRST, :]
                if g > 0:
                    source += tails_at
                    wide[8 + at - FIRST : 8 + at, columns] = by_chip[
                        g - 1, source : source + FIRST, :
                    ]
            for j in range(value_blocks):
                source = values_at + FIRST * (i * value_blocks + j)
                value_rows[i * 16 * chips + at : i * 16 * chips + at + FIRST, j * 128 : (j + 1) * 128] = (
                    by_chip[g, source : source + FIRST, :]
                )
            ends = lines[g]
            if i > 0:
                ends = pltpu.roll(ends, 128 - i * span, 1)
            ends = jnp.where(g < me, ends + since, 2 * very_negative)
            decay = lines[g][:, 64 + i * span : 64 + i * span + 1]
            since = since + jnp.where(g < me, decay, 0.0)
            column = jnp.sum(jnp.where(square, ends, 0.0), axis=1, keepdims=True)
            level_rows[i * 16 * chips + at : i * 16 * chips + at + FIRST, :] = jnp.broadcast_to(
                column, (FIRST, 128)
            )
        keys_ref[i * 16 * chips : (i + 1) * 16 * chips, :] = conv_rows(
            same, 0, 16 * chips, taps, slice(i * key_width, (i + 1) * key_width), wide
        )
    values_ref[...] = value_rows[...].astype(BF16)
    levels_ref[...] = level_rows[...]
    same = same_request(lengths_ref, me * length + iota((16, 128), 0))
    previous = jnp.maximum(me - 1, 0)
    for which, (weights, edge) in enumerate(((query_taps, query_edge), (taps, key_edge))):
        for i in range(per_core):
            columns = slice(i * key_width, (i + 1) * key_width)
            for j in range(key_blocks):
                source = tails_at + FIRST * ((1 - which) * per_core + i) * key_blocks + FIRST * j
                narrow[8 - FIRST : 8, j * 128 : (j + 1) * 128] = by_chip[
                    previous, source : source + FIRST, :
                ]
            narrow[8:, :] = edge[0, :, columns].astype(F32)
            conv_ref[which, :, columns] = conv_rows(same, 0, 16, weights, columns, narrow)


def shifted_stab(infos, ranks, upto):
    out = []
    for i, (_, stab, _) in enumerate(infos):
        for j, (_, _, decay) in enumerate(infos):
            if i != j:
                inside = (ranks[j] > ranks[i]) & (ranks[j] < upto)
                stab = stab + jnp.where(inside, decay, 0.0)
        out.append(stab)
    return out


def total_kernel(*refs):
    *states, out = refs
    rows = out.shape[0] - INFO
    _, mine = core_place()
    ranks = [lax.bitwise_xor(mine, off) for off in range(4)]
    infos = [read_info(s) for s in states]
    stabs = shifted_stab(infos, ranks, 4)
    m = functools.reduce(jnp.maximum, stabs)
    weights = [jnp.exp(s - m) for s in stabs]
    out[0:rows, :] = sum(w * s[0:rows, :].astype(F32) for w, s in zip(weights, states)).astype(BF16)
    write_info(out, sum(w * i[0] for w, i in zip(weights, infos)), m, sum(i[2] for i in infos))


def is_later(bit):
    return lax.rem(lax.shift_right_logical(lax.axis_index("seq"), bit), 2) == 1


def round_kernel(bit, first, *refs):
    if first:
        total_ref, got_ref, prefix_out, total_out = refs
    else:
        prefix_ref, total_ref, got_ref, prefix_out, total_out = refs
    rows = total_ref.shape[0] - INFO
    later = is_later(bit)
    n_t, m_t, d_t = read_info(total_ref)
    n_g, m_g, d_g = read_info(got_ref)
    here, got = total_ref[0:rows, :].astype(F32), got_ref[0:rows, :].astype(F32)
    a_t = m_t + jnp.where(later, 0.0, d_g)
    a_g = m_g + jnp.where(later, d_t, 0.0)
    m = jnp.maximum(a_t, a_g)
    w_t, w_g = jnp.exp(a_t - m), jnp.exp(a_g - m)
    total_out[0:rows, :] = (w_t * here + w_g * got).astype(BF16)
    write_info(total_out, w_t * n_t + w_g * n_g, m, d_t + d_g)
    if first:
        n_p, m_p, d_p = jnp.zeros_like(n_g), jnp.full_like(m_g, very_negative), jnp.zeros_like(d_g)
        prefix = jnp.zeros_like(got)
    else:
        n_p, m_p, d_p = read_info(prefix_ref)
        prefix = prefix_ref[0:rows, :].astype(F32)
    a_g = jnp.where(later, m_g + d_p, 2 * very_negative)
    m = jnp.maximum(m_p, a_g)
    w_p = jnp.exp(m_p - m)
    w_g = jnp.where(later, jnp.exp(a_g - m), 0.0)
    prefix_out[0:rows, :] = (w_p * prefix + w_g * got).astype(BF16)
    write_info(prefix_out, w_p * n_p + w_g * n_g, m, d_p + jnp.where(later, d_g, 0.0))


def enter_kernel(bit, prefix_ref, *refs):
    states, outs = refs[:4], refs[4:]
    rows = outs[0].shape[0] - INFO
    _, mine = core_place()
    ranks = [lax.bitwise_xor(mine, off) for off in range(4)]
    infos = [read_info(s) for s in states]
    n_p, m_p, _ = read_info(prefix_ref)
    valid = True if bit is None else is_later(bit)
    weights = []
    for off, out in enumerate(outs):
        stabs = shifted_stab(infos, ranks, ranks[off])
        m_in = m_p
        for info, rank in zip(infos, ranks):
            m_in = m_in + jnp.where(rank < ranks[off], info[2], 0.0)
        m_in = jnp.where(valid, m_in, very_negative)
        stabs = [
            jnp.where(rank < ranks[off], s, 2 * very_negative) for s, rank in zip(stabs, ranks)
        ]
        m = functools.reduce(jnp.maximum, stabs, m_in)
        mine_in = [jnp.where(valid, jnp.exp(m_in - m), 0.0)] + [
            jnp.where(rank < ranks[off], jnp.exp(s - m), 0.0) for s, rank in zip(stabs, ranks)
        ]
        weights.append(mine_in)
        normals = [n_p] + [info[0] for info in infos]
        write_info(out, sum(w * n for w, n in zip(mine_in, normals)), m, jnp.zeros_like(m))
    step = math.gcd(rows, 64)
    for at in range(0, rows, step):
        parts = [r[at : at + step, :].astype(F32) for r in (prefix_ref, *states)]
        for off, out in enumerate(outs):
            out[at : at + step, :] = sum(
                w * part
                for k, (w, part) in enumerate(zip(weights[off], parts))
                if k != off + 1
            ).astype(BF16)


def query_kernel(
    per_core, lengths_ref, query_ref, query_other, taps_ref, own_values, value_other,
    conv_ref, taps, edge_ref, values, queries, wide, sems,
):
    core, _ = core_place()
    length, width = queries.shape
    key_width = width // per_core
    split = query_ref.shape[1] > width
    columns = pl.ds(pl.multiple_of(core * width, 128) if split else 0, width)
    copies = start_copies(
        sems,
        [(taps_ref.at[0, :, columns], taps)]
        + by_core(core, query_ref, query_other, columns, queries)
        + by_core(core, own_values, value_other, slice(None), values),
    )
    offset = lax.axis_index("seq") // 2 * length
    same = same_request(lengths_ref, offset + iota((length, 128), 0))
    for copy in copies:
        copy.wait()
    edge_ref[0] = queries[0:16, :]
    edge_ref[1] = queries[length - 16 :, :]
    for i in range(per_core):
        here = slice(i * key_width, (i + 1) * key_width)
        wide[0:8, :] = jnp.zeros((8, key_width), F32)
        wide[8:, :] = queries[:, here].astype(F32)
        for start in range(0, length, 128):
            conv_ref[start : start + 128, here] = conv_rows(
                same, start, start + 128, taps, here, wide
            )


def intra_kernel(
    per_core, lengths_ref, query_conv, key_ref, conv_first, values, gate_ref,
    query_ref, numerator_ref, stats_ref, keys,
):
    length, width = query_ref.shape
    key_width = width // per_core
    value_width = values.shape[1] // per_core
    key_scale = 1.0 / math.sqrt(key_width)
    offset = lax.axis_index("seq") // 2 * length
    query_ref[...] = query_conv[...]
    query_ref[0:16, :] = conv_first[0]
    keys[...] = key_ref[...]
    keys[0:16, :] = conv_first[1]
    gate, cumulative = gate_ref[0], gate_ref[1]
    by_token = cumulative.T
    segment = segment_of(lengths_ref, offset + iota((length, 1), 0))
    segment_row = segment_of(lengths_ref, offset + iota((1, length), 1))
    before = segment_of(lengths_ref, jnp.full((1, 1), offset - 1, jnp.int32))
    step = length // 2
    lane = iota((step, 128), 1)
    stats = [[jnp.zeros((step, 128), F32)] * 3 for _ in range(2)]
    for i in range(per_core):
        here = slice(i * key_width, (i + 1) * key_width)
        value_columns = slice(i * value_width, (i + 1) * value_width)
        for b in range(2):
            rows, stop = slice(b * step, (b + 1) * step), (b + 1) * step
            allowed = segment_row[:, 0:stop] == segment[rows]
            allowed &= iota((step, stop), 1) <= iota((step, stop), 0) + b * step
            total = by_token[rows, i : i + 1]
            log_weight = jnp.where(
                allowed,
                gate[i : i + 1, 0:stop] - cumulative[i : i + 1, 0:stop] + total,
                very_negative,
            )
            row_max = jnp.max(log_weight, axis=1, keepdims=True)
            scores = dot(query_ref[rows, here], keys[0:stop, here], ((1,), (1,))) * key_scale
            weights = scores * jnp.exp(log_weight - row_max)
            numerator_ref[rows, value_columns] = dot(
                weights.astype(BF16), values[0:stop, value_columns]
            )
            linked = jnp.where(segment[rows] == before, total, very_negative)
            found = (jnp.sum(weights, axis=1, keepdims=True), row_max, linked)
            stats[b] = [jnp.where(lane == i, new, old) for new, old in zip(found, stats[b])]
    for b in range(2):
        for k in range(3):
            stats_ref[k, b * step : (b + 1) * step, :] = stats[b][k]


def head_rows(
    per_core, start, memory, parts, stabs, query_ref, numerator_ref, stats_ref, out_ref
):
    step = out_ref.shape[0]
    key_width = query_ref.shape[1] // per_core
    value_width = memory.shape[1]
    key_scale = 1.0 / math.sqrt(key_width)
    span = pl.ds(pl.multiple_of(start, step), step)
    queries = [query_ref[span, i * key_width : (i + 1) * key_width] for i in range(per_core)]
    from_normal = sum(
        dot(q, parts[i * 128 : (i + 1) * 128, :], ((1,), (1,))) for i, q in enumerate(queries)
    )
    from_normal = (
        from_normal
        + pltpu.roll(from_normal, 128 - 8, 1)
        + pltpu.roll(from_normal, 128 - 16, 1)
    )
    row_max = stats_ref[1, span, :]
    carried = stabs[0:1, :] + stats_ref[2, span, :]
    m = jnp.maximum(row_max, carried)
    w_here = jnp.exp(row_max - m)
    w_in = jnp.exp(carried - m) * key_scale
    denominator = w_here * stats_ref[0, span, :] + w_in * from_normal
    scale = 1.0 / jnp.maximum(jnp.abs(denominator), 1.0)
    w_here, w_in = w_here * scale, w_in * scale
    for i in range(per_core):
        columns = slice(i * value_width, (i + 1) * value_width)
        from_memory = dot(queries[i], memory[i * key_width : (i + 1) * key_width, :])
        out_ref[:, columns] = (
            w_here[:, i : i + 1] * numerator_ref[span, columns] + w_in[:, i : i + 1] * from_memory
        ).astype(BF16)


def head_send_kernel(
    per_core, own_ref, got1, got2, got3, keys_ref, values_ref, levels_ref,
    query_ref, numerator_ref, stats_ref, send_ref, memory, parts, stabs, info,
):
    core, mine = core_place()
    key_width = query_ref.shape[1] // per_core
    value_width = memory.shape[1]
    rows = query_ref.shape[1] // 4
    for off, ref in enumerate((own_ref, got1, got2, got3)):
        piece = piece_of(mine, off)
        start = pl.multiple_of(piece * rows, rows)
        for j in range(value_width // 128):
            memory[pl.ds(start, rows), j * 128 : (j + 1) * 128] = ref[j * rows : (j + 1) * rows, :]
        info[piece] = ref[ref.shape[0] - INFO :, :]
    count = keys_ref.shape[0] // per_core
    row, lane = iota((128, key_width), 0), iota((1, 128), 1)
    levels = jnp.full((1, 128), very_negative, F32)
    for i in range(per_core):
        normal, stab, _ = read_info(info.at[i * key_width // rows], key_width)
        here = slice(i * key_width, (i + 1) * key_width)
        extra = slice(i * count, (i + 1) * count)
        weighted = keys_ref[extra, :].astype(F32) * jnp.exp(levels_ref[extra, 0:1] - stab)
        normal = normal + jnp.sum(weighted, axis=0, keepdims=True)
        memory[here, :] = (
            memory[here, :].astype(F32)
            + dot(weighted.astype(BF16), values_ref[extra, :], ((0,), (0,)))
        ).astype(BF16)
        levels = jnp.where(lane == i, stab, levels)
        block = jnp.zeros((128, key_width), F32)
        for k, part in enumerate(split3(normal)):
            block = jnp.where(row == 8 * k + i, part, block)
        parts[i * 128 : (i + 1) * 128, :] = block.astype(BF16)
    stabs[...] = jnp.broadcast_to(levels, stabs.shape)
    start = (1 - core) * send_ref.shape[0]
    head_rows(
        per_core, start, memory, parts, stabs, query_ref, numerator_ref, stats_ref, send_ref
    )


def head_keep_kernel(
    per_core, memory, parts, stabs, query_ref, numerator_ref, stats_ref, keep_ref
):
    core, _ = core_place()
    start = core * keep_ref.shape[0]
    head_rows(
        per_core, start, memory, parts, stabs, query_ref, numerator_ref, stats_ref, keep_ref
    )


def weight_part(weight_ref, half, rows, start, width):
    return weight_ref[
        pl.ds(pl.multiple_of(half * rows, 128), rows), pl.ds(pl.multiple_of(start, 128), width)
    ]


def keep_kernel(off, head_ref, weight_ref, part_ref):
    core, _ = core_place()
    rows, width = head_ref.shape[1], part_ref.shape[1]
    start = lax.bitwise_xor(lax.axis_index("head"), off) * width
    part_ref[...] = dot(head_ref[...], weight_part(weight_ref, core, rows, start, width))


def send_kernel(off, chunk, head_ref, weight_ref, kept_ref, part_ref):
    core, _ = core_place()
    rows, piece, width = head_ref.shape[1], part_ref.shape[1], kept_ref.shape[1]
    start = lax.bitwise_xor(lax.axis_index("head"), off) * width + chunk * piece
    part_ref[...] = (
        dot(head_ref[...], weight_part(weight_ref, 1 - core, rows, start, piece))
        + kept_ref[:, chunk * piece : (chunk + 1) * piece]
    ).astype(part_ref.dtype)


def own_kernel(keep_ref, got_ref, weight_ref, part_ref):
    core, _ = core_place()
    rows, width = keep_ref.shape[1], part_ref.shape[1]
    start = lax.axis_index("head") * width
    part_ref[...] = dot(
        keep_ref[...], weight_part(weight_ref, core, rows, start, width)
    ) + dot(got_ref[...], weight_part(weight_ref, 1 - core, rows, start, width))


def sum_kernel(chunk, count, own_ref, *refs):
    arrived, (out_ref, held, sems) = refs[:count], refs[-3:]
    width = held.shape[1]
    columns = pl.ds(chunk * width, width)
    parts = sems.shape[0]
    step = own_ref.shape[0] // parts
    copies = []
    for part in range(parts):
        rows = slice(part * step, (part + 1) * step)
        total = own_ref[rows, chunk * width : (chunk + 1) * width]
        for ref in arrived:
            total = total + ref[rows, :].astype(F32)
        held[rows, :] = total.astype(held.dtype)
        span = pl.ds(part * step, step)
        copies.append(
            pltpu.make_async_copy(held.at[span, :], out_ref.at[span, columns], sems.at[part])
        )
        copies[-1].start()
    for copy in copies:
        copy.wait()


def call(kernel, out_shape, spaces, scratch, name, flops=0, nbytes=0, limit=24, out=pltpu.VMEM,
         aliases=None):
    place = {"v": pltpu.VMEM, "s": pltpu.SMEM, "a": pl.ANY, "h": pl.ANY}
    outs = jax.tree.map(lambda _: pl.BlockSpec(memory_space=out), out_shape)
    inner = pl.pallas_call(
        kernel,
        out_shape=out_shape,
        in_specs=[pl.BlockSpec(memory_space=place[s]) for s in spaces],
        out_specs=outs,
        scratch_shapes=scratch,
        compiler_params=pltpu.CompilerParams(vmem_limit_bytes=limit << 20),
        cost_estimate=pl.CostEstimate(flops=flops, bytes_accessed=nbytes, transcendentals=0),
        name=name,
        input_output_aliases=aliases or {},
    )

    def run(*args):
        return inner(
            *(
                pltpu.with_memory_space_constraint(x, pltpu.HBM) if s in "hs" else x
                for s, x in zip(spaces, args, strict=True)
            )
        )

    return run


def on_device(
    query_input, key_input, value_input, kernel_taps, input_gate, forget_gate, request_lengths,
    output_weight,
):
    seq_count, head_count = lax.axis_size("seq"), lax.axis_size("head")
    length, key_cols = query_input.shape
    heads = input_gate.shape[0]
    value_cols = value_input.shape[1]
    out_cols = output_weight.shape[1] // head_count
    chip_length = 2 * length
    key_width = key_cols // heads
    per_core = max(1, heads // 2)
    part_keys, part_values = per_core * key_width, value_cols // 2
    value_width = part_values // per_core
    lags = kernel_taps.shape[1]
    rows = part_keys // 4

    def shape(dims, dtype=F32):
        return jax.ShapeDtypeStruct(dims, dtype)

    def swap(x, off):
        return lax.ppermute(x, "seq", [(i, i ^ off) for i in range(seq_count)])

    gates, key_send, value_send = call(
        gates_kernel,
        (
            shape((2, heads, length)),
            shape((length, part_keys), BF16),
            shape((length, part_values), BF16),
        ),
        "hhhh", [pltpu.SemaphoreType.DMA((4,))], "gates", flops=4 << 30,
    )(input_gate, forget_gate, key_input, value_input)
    gates_other, key_other, value_other = swap(gates, 1), swap(key_send, 1), swap(value_send, 1)
    key_after, value_after, gates = lax.optimization_barrier((key_input, value_input, gates))
    own_keys, own_values, taps = call(
        own_kernel_parts,
        (
            shape((length, part_keys), BF16),
            shape((length, part_values), BF16),
            shape((lags, part_keys)),
        ),
        "hhh", [pltpu.SemaphoreType.DMA((3,))], "own_part", flops=4 << 30,
    )(key_after, value_after, kernel_taps)
    query_after, gates = lax.optimization_barrier((query_input, gates))
    query_other = swap(query_after, 1)

    one = shape((rows * value_width // 128 + INFO, 128), BF16)
    key_conv, gate_sums, key_edge, levels, *pieces = call(
        functools.partial(chip_kernel, per_core),
        (
            shape((chip_length, part_keys), BF16),
            shape((2, 8, chip_length)),
            shape((2, 16, part_keys), BF16),
            shape((2, 8, 128)),
        )
        + (one,) * 4,
        "s" + "v" * 7,
        [
            pltpu.VMEM((2, max(8, heads), chip_length), F32),
            pltpu.VMEM((2, 8, chip_length), F32),
            pltpu.VMEM((per_core, chip_length + 8, key_width), F32),
            pltpu.VMEM((chip_length, part_keys), BF16),
            pltpu.VMEM((part_keys, value_width), BF16),
            pltpu.VMEM((8, key_width), F32),
            pltpu.VMEM((2, 8, 128), F32),
        ],
        "chip_state",
        flops=1 << 30,
    )(
        request_lengths, own_keys, own_values, key_other, value_other, gates, gates_other, taps
    )
    states = [pieces[0]] + [swap(pieces[off], 2 * off) for off in (1, 2, 3)]

    count = 16 * seq_count // 2
    lines = FIRST * per_core * (3 * key_width + value_width) // 128 + 3
    lines = -(-lines // 16) * 16
    message = call(
        functools.partial(message_kernel, per_core), shape((1, lines, 128), BF16), "havvvv",
        [
            pltpu.VMEM((lines, 128), F32),
            pltpu.VMEM((16, part_keys), BF16),
            pltpu.SemaphoreType.DMA((1,)),
        ],
        "message",
    )(query_input, query_other, key_edge, own_values, value_other, levels)
    bits = seq_count.bit_length() - 1
    steps = [4, 2, 8] if bits == 4 else [1 << b for b in range(1, bits)]
    near, far, offsets = message, swap(message, steps[0]), [0, steps[0] // 2]
    query_conv, query_taps, query_edge, values = call(
        functools.partial(query_kernel, per_core),
        (
            shape((chip_length, part_keys), BF16),
            shape((lags, part_keys)),
            shape((2, 16, part_keys), BF16),
            shape((chip_length, part_values), BF16),
        ),
        "shahvv",
        [
            pltpu.VMEM((chip_length, part_keys), BF16),
            pltpu.VMEM((chip_length + 8, key_width), F32),
            pltpu.SemaphoreType.DMA((5,)),
        ],
        "query_conv",
        flops=1 << 30,
    )(request_lengths, query_input, query_other, kernel_taps, own_values, value_other)
    states, query_conv, far = lax.optimization_barrier((states, query_conv, far))
    total = call(total_kernel, one, "vvvv", [], "group_total")(*states)
    flag = 3
    prefix = swap(total, 12 if bits == 4 else 8)
    near, far, total = lax.optimization_barrier((near, far, total))
    for step in steps[1:]:
        near = call(
            join_kernel, shape((2 * near.shape[0], lines, 128), BF16), "vv", [], "join"
        )(near, far)
        far = swap(near, step)
        offsets = offsets + [off ^ (step // 2) for off in offsets]
    if bits > 4:
        flag = None
        prefix, total = call(
            functools.partial(round_kernel, 3, True), (one, one), "vv", [], "round_state"
        )(total, prefix)
        for bit in range(4, bits):
            prefix, total = call(
                functools.partial(round_kernel, bit, False), (one, one), "vvv", [], "round_state"
            )(prefix, total, swap(total, 1 << bit))
    enter = call(functools.partial(enter_kernel, flag), (one,) * 4, "vvvvv", [], "enter_state")(
        prefix, *states
    )
    gate_sums, near, *enter = lax.optimization_barrier((gate_sums, near, *enter))
    enter = [enter[0]] + [swap(enter[off], 2 * off) for off in (1, 2, 3)]
    *extras, conv_first = call(
        functools.partial(gathered_kernel, per_core, chip_length, tuple(offsets)),
        (
            shape((per_core * count, key_width), BF16),
            shape((per_core * count, value_width), BF16),
            shape((per_core * count, 128)),
            shape((2, 16, part_keys), BF16),
        ),
        "svvvvvv",
        [
            pltpu.VMEM((seq_count // 2, lines, 128), F32),
            pltpu.VMEM((count + 8, key_width), F32),
            pltpu.VMEM((per_core * count, value_width), F32),
            pltpu.VMEM((per_core * count, 128), F32),
            pltpu.VMEM((24, key_width), F32),
        ],
        "gathered_first",
    )(request_lengths, near, far, taps, key_edge, query_taps, query_edge)
    inside = call(
        functools.partial(intra_kernel, per_core),
        (
            shape((chip_length, part_keys), BF16),
            shape((chip_length, part_values)),
            shape((3, chip_length, 128)),
        ),
        "svvvvv",
        [pltpu.VMEM((chip_length, part_keys), BF16)],
        "intra",
        flops=4 << 30,
    )(request_lengths, query_conv, key_conv, conv_first, values, gate_sums)
    half_out = shape((length, part_values), BF16)
    send, *entered = call(
        functools.partial(head_send_kernel, per_core),
        (
            half_out,
            shape((part_keys, value_width), BF16),
            shape((128 * per_core, key_width), BF16),
            shape((8, 128)),
        ),
        "v" * 10, [pltpu.VMEM((4, INFO, 128), BF16)], "head_send",
    )(*enter, *extras, *inside)
    keep = call(
        functools.partial(head_keep_kernel, per_core), half_out, "v" * 6, [], "head_keep",
        flops=1 << 30,
    )(*entered, *inside)
    got = swap(send, 1)

    chunks = 2 if head_count == 2 and out_cols % 256 == 0 else 1
    piece = out_cols // chunks
    arrived = []
    mixed = call(
        own_kernel, shape((length, out_cols)), "vvv", [], "project_own", flops=4 << 30
    )(keep, got, output_weight)
    for off in range(1, head_count):
        kept = call(
            functools.partial(keep_kernel, off), shape((length, out_cols)), "vv", [],
            "project_kept", flops=2 << 30,
        )(keep, output_weight)
        columns, after = [], got
        for chunk in range(chunks):
            part = call(
                functools.partial(send_kernel, off, chunk), shape((length, piece), BF16), "vvv",
                [], "project_other",
            )(after, output_weight, kept)
            columns.append(
                lax.ppermute(part, "head", [(i, i ^ off) for i in range(head_count)])
            )
            after, mixed = lax.optimization_barrier((got, mixed))
        arrived.append(columns)
    out = []
    for chunk in range(chunks):
        out = [
            call(
                functools.partial(sum_kernel, chunk, len(arrived)),
                shape((length, out_cols), BF16),
                "v" * (1 + len(arrived)) + "a" * len(out),
                [pltpu.VMEM((length, piece), BF16), pltpu.SemaphoreType.DMA((2,))],
                "mixed_out", out=pl.ANY, aliases={1 + len(arrived): 0} if out else None,
            )(mixed, *(columns[chunk] for columns in arrived), *out)
        ]
    return out[0]


def solution(mesh):
    placed = (
        P("seq", "head"),
        P("seq", "head"),
        P("seq", "head"),
        P(None, None, "head"),
        P("head", "seq"),
        P("head", "seq"),
        P(),
        P("head", None),
    )
    return jax.shard_map(
        on_device, mesh=mesh, in_specs=placed, out_specs=P("seq", "head"), check_vma=False
    )
```
